32 devices in a mesh: dp: 4 (over y, x), fsdp: 8 (over z, core).
Axes of the slice: x: 2, y: 2, z: 4, core: 2. Of those that a mesh axis runs over, the one named last changes fastest.
Arguments:
- block_input: bfloat16 [2, 128, 128, 768], P(None, ('dp', 'fsdp')), may hold values from -6 to 6
- out_grad: bfloat16 [2, 128, 128, 768], P(None, ('dp', 'fsdp')), may hold values from -6 to 6
- timestep: int32 [2, 128], P(None, ('dp', 'fsdp')), may hold values from 0 to 1999
- dataset: int32 [2, 128], P(None, ('dp', 'fsdp')), may hold values from 0 to 1, as said below
- lengths: int32 [2, 128], P(None, ('dp', 'fsdp')), may hold values from 16 to 128, as said below
- norm1_gain: bfloat16 [768], P(('dp', 'fsdp')), may hold values from 0.099609375 to 1.8984375
- qkv_weight: bfloat16 [768, 2304], P(('dp', 'fsdp')), may hold values from -0.21875 to 0.21875
- out_weight: bfloat16 [768, 768], P(('dp', 'fsdp')), may hold values from -0.875 to 0.875
- norm2_gain: bfloat16 [768], P(('dp', 'fsdp')), may hold values from 0.099609375 to 1.8984375
- up_weight: bfloat16 [768, 3072], P(('dp', 'fsdp')), may hold values from -0.21875 to 0.21875
- down_weight: bfloat16 [3072, 768], P(('dp', 'fsdp')), may hold values from -0.109375 to 0.109375
- time_in: bfloat16 [512, 128], P(('dp', 'fsdp')), may hold values from -0.5 to 0.5
- time_out: bfloat16 [512, 768], P(('dp', 'fsdp')), may hold values from -0.25 to 0.25
- data_embed: bfloat16 [768, 2], P(('dp', 'fsdp')), may hold values from -3 to 3
Outputs:
- block_output: bfloat16 [2, 128, 128, 768], P(None, ('dp', 'fsdp'))
- input_grad: bfloat16 [2, 128, 128, 768], P(None, ('dp', 'fsdp'))
- norm1_gain_grad: float32 [768], P(('dp', 'fsdp'))
- qkv_weight_grad: float32 [768, 2304], P(('dp', 'fsdp'))
- out_weight_grad: float32 [768, 768], P(('dp', 'fsdp'))
- norm2_gain_grad: float32 [768], P(('dp', 'fsdp'))
- up_weight_grad: float32 [768, 3072], P(('dp', 'fsdp'))
- down_weight_grad: float32 [3072, 768], P(('dp', 'fsdp'))
- time_in_grad: float32 [512, 128], P(('dp', 'fsdp'))
- time_out_grad: float32 [512, 768], P(('dp', 'fsdp'))
- data_embed_grad: float32 [768, 2], P(('dp', 'fsdp'))
The draws below stay inside these ranges and needn't reach their ends.
Inputs may be any that keep to these rules, and one draw needn't show every extreme that they name: In every micro-batch the first of each device's 4 sequences is of dataset 1. `lengths`: a sequence of dataset 0 has at most 64 tokens; in every micro-batch the first of each device's 4 sequences has 128.
All inputs are finite; a program needn't handle non-finite values.
Results may differ from the reference program's by a relative error of at most 0.013.
Values may be sent and summed in bfloat16 or wider, within the bound.
No kernel may reach another device: no remote copies, remote signals or barrier semaphores. Data moves between devices by JAX's collectives and lax.ppermute only.
A program may use at most 192 MiB of HBM per device.

```python
import math
import jax
import jax.numpy as jnp
from jax import lax

D = 768
HEAD_DIM = 64
FF = 3072
TE_IN = 128
TE_HID = 512
DATASETS = 2
SEQ_LEN = 128
SEQ_DEV = 4
MICRO = 2
SEQS = 128


def pick_sets(key):
    set_key, len_key = jax.random.split(key)
    draw_shape = (MICRO, SEQS)
    dataset_ids = jax.random.randint(set_key, draw_shape, 0, DATASETS)
    leading = (jnp.arange(SEQS) % SEQ_DEV == 0)[None, :]
    dataset_ids = jnp.where(leading, DATASETS - 1, dataset_ids)
    ceiling = jnp.where(dataset_ids == DATASETS - 1, SEQ_LEN, SEQ_LEN // 2)
    shortest = SEQ_LEN // 8
    raw_draw = jax.random.randint(len_key, draw_shape, 0, 1 << 20)
    seq_lengths = shortest + raw_draw % (ceiling - shortest + 1)
    seq_lengths = jnp.where(leading, SEQ_LEN, seq_lengths)
    return (dataset_ids.astype(jnp.int32), seq_lengths.astype(jnp.int32))


def draw_dataset(key, part):
    shared = pick_sets(key)
    return shared[0]


def draw_lengths(key, part):
    shared = pick_sets(key)
    return shared[1]


def with_ends(values, key, least, top_value):
    longest = values.shape.index(max(values.shape))
    spots = []
    for shift in (0, 1):
        where = [jax.random.randint(jax.random.fold_in(key, axis), (), 0, length) for axis, length in enumerate(values.shape)]
        where[longest] = (where[longest] + shift) % values.shape[longest]
        spots.append(tuple(where))
    return values.at[spots[0]].set(least).at[spots[1]].set(top_value)


def levels(key, shape, cuts, low, top_value):
    level, own = 1.0, jax.random.fold_in(key, 6)
    for position, blocks in cuts:
        steps = jnp.exp(jax.random.uniform(jax.random.fold_in(own, position), (blocks,), jnp.float32, low / len(cuts), top_value / len(cuts)))
        level = level * jnp.repeat(steps, shape[position] // blocks).reshape([-1 if axis == position else 1 for axis in range(len(shape))])
    return level


def noise(key, extent, width, limit, cuts=(), kind=jnp.bfloat16):
    level = levels(key, extent, cuts, -0.22, 0.18) if cuts else 1.0
    values = jax.random.normal(key, extent, jnp.float32) * width * level
    return jnp.minimum(jnp.maximum(values, -limit), limit).astype(kind)


def setup_inputs(seed: int = 0) -> dict:
    seeds = jax.random.split(jax.random.key(seed), 15)
    return {
        "block_input": noise(seeds[0], (MICRO, SEQS, SEQ_LEN, D), 1.0, 6.0, ((1, 32),)),
        "out_grad": noise(seeds[1], (MICRO, SEQS, SEQ_LEN, D), 1.0, 6.0, ((1, 32),)),
        "timestep": with_ends(jax.random.randint(seeds[2], (MICRO, SEQS), 0, 2000), jax.random.fold_in(seeds[2], 1), 0, 1999).astype(jnp.int32),
        "dataset": draw_dataset(jax.random.fold_in(seeds[14], 71), 0),
        "lengths": draw_lengths(jax.random.fold_in(seeds[14], 71), 0),
        "norm1_gain": jnp.clip(1.0 + 0.18 * jax.random.normal(seeds[5], (D,), jnp.float32), 0.099609375, 1.8984375).astype(jnp.bfloat16),
        "qkv_weight": noise(seeds[6], (D, 3 * D), D ** -0.5, 0.21875, ((0, 32),)),
        "out_weight": noise(seeds[7], (D, D), (D // 16) ** -0.5, 0.875, ((0, 32),)),
        "norm2_gain": jnp.clip(1.0 + 0.18 * jax.random.normal(seeds[8], (D,), jnp.float32), 0.099609375, 1.8984375).astype(jnp.bfloat16),
        "up_weight": noise(seeds[9], (D, FF), D ** -0.5, 0.21875, ((0, 32),)),
        "down_weight": noise(seeds[10], (FF, D), FF ** -0.5, 0.109375, ((0, 32),)),
        "time_in": noise(seeds[11], (TE_HID, TE_IN), TE_IN ** -0.5, 0.5, ((0, 32),)),
        "time_out": noise(seeds[12], (TE_HID, D), TE_HID ** -0.5, 0.25, ((0, 32),)),
        "data_embed": noise(seeds[13], (D, DATASETS), 0.5, 3.0, ((0, 32),)),
    }


@jax.custom_vjp
def low(v):
    return lax.optimization_barrier(v.astype(jnp.bfloat16)).astype(jnp.float32)

@jax.custom_vjp
def low_back(v):
    return v

def low_keep(v):
    return (low(v), None)

def low_pass(kept, grad):
    return (grad,)

def back_keep(v):
    return (v, None)

def back_low(kept, grad):
    return (low(grad),)
low.defvjp(low_keep, low_pass)
low_back.defvjp(back_keep, back_low)

def matmul(left, right):
    return jnp.dot(left, right, precision=lax.Precision.HIGHEST)

def layer_norm(tok_rows, gain):
    center = tok_rows - lax.optimization_barrier(jnp.mean(tok_rows, axis=-1, keepdims=True))
    spread = lax.optimization_barrier(jnp.mean(center * center, axis=-1, keepdims=True))
    return center * lax.rsqrt(spread + 1e-05) * gain

def sinusoid(timestep):
    half_width = TE_IN // 2
    frequency = jnp.exp(-math.log(10000.0) * jnp.arange(half_width, dtype=jnp.float32) / half_width)
    angles = timestep.astype(jnp.float32)[:, None] * frequency[None, :]
    return jnp.concatenate([jnp.cos(angles), jnp.sin(angles)], axis=-1)

def block(inputs, params, timestep, dataset, lengths):
    gain_first, w_qkv, w_out, gain_second, w_up, w_down, time_in, time_out, data_embed = params
    groups, seq_len, model_width = inputs.shape
    heads_count = model_width // HEAD_DIM
    highest = lax.Precision.HIGHEST
    features = low(sinusoid(timestep))
    time_hidden = low(jax.nn.silu(matmul(features, time_in.T)))
    time_embed = matmul(time_hidden, time_out) + jnp.take(data_embed, dataset, axis=1).T
    resid_in = inputs + time_embed[:, None, :]
    normed = low(layer_norm(resid_in, gain_first))
    qkv_all = low(low_back(jnp.einsum('gld,de->gle', normed, w_qkv, precision=highest)))
    qkv_all = qkv_all.reshape(groups, seq_len, 3, heads_count, HEAD_DIM)
    query_rows = qkv_all[:, :, 0]
    key_rows = qkv_all[:, :, 1]
    value_rows = qkv_all[:, :, 2]
    raw_scores = jnp.einsum('glhd,gmhd->ghlm', query_rows, key_rows, precision=highest) * HEAD_DIM ** (-0.5)
    key_mask = jnp.arange(seq_len)[None, :] < lengths[:, None]
    scores = low_back(jnp.where(key_mask[:, None, None, :], raw_scores, -1000000000.0))
    probs_low = low(jax.nn.softmax(scores, axis=-1))
    attended = low(low_back(jnp.einsum('ghlm,gmhd->glhd', probs_low, value_rows, precision=highest)))
    attended = attended.reshape(groups, seq_len, model_width)
    branch_attn = low_back(jnp.einsum('gld,de->gle', attended, w_out, precision=highest))
    resid_mid = resid_in + branch_attn
    normed_two = low(layer_norm(resid_mid, gain_second))
    up_proj = low_back(jnp.einsum('gld,df->glf', normed_two, w_up, precision=highest))
    activated = low(jax.nn.gelu(up_proj, approximate=False))
    branch_mlp = low_back(jnp.einsum('glf,fd->gld', activated, w_down, precision=highest))
    return resid_mid + branch_mlp

def reference(block_input, out_grad, timestep, dataset, lengths, norm1_gain, qkv_weight, out_weight, norm2_gain, up_weight, down_weight, time_in, time_out, data_embed):
    params = tuple((tensor.astype(jnp.float32) for tensor in (norm1_gain, qkv_weight, out_weight, norm2_gain, up_weight, down_weight, time_in, time_out, data_embed)))
    micro_count, seq_all, seq_len, model_width = block_input.shape
    total_seqs = micro_count * seq_all
    group_size = math.gcd(total_seqs, max(1, 4096 // seq_len))
    steps_count = total_seqs // group_size

    def regroup(array):
        return array.reshape((steps_count, group_size) + array.shape[2:])

    def scan_step(running, pieces):
        inputs_group, cot_group, time_group, set_group, len_group = pieces

        def forward_fn(inputs_x, params_x):
            return block(inputs_x, params_x, time_group, set_group, len_group)
        results, back_fn = jax.vjp(forward_fn, inputs_group, params)
        grad_inputs, grad_params = back_fn(cot_group)
        running = jax.tree.map(lambda before, update: before + update, running, grad_params)
        return (running, (results.astype(jnp.bfloat16), grad_inputs.astype(jnp.bfloat16)))
    zeros_start = tuple((jnp.zeros_like(tensor) for tensor in params))
    totals, (results, grad_inputs) = lax.scan(scan_step, zeros_start, (regroup(block_input.astype(jnp.float32)), regroup(out_grad.astype(jnp.float32)), regroup(timestep), regroup(dataset), regroup(lengths)))
    results = results.reshape(block_input.shape)
    grad_inputs = grad_inputs.reshape(block_input.shape)
    return (results, grad_inputs, totals[0], totals[1], totals[2], totals[3], totals[4], totals[5], totals[6], totals[7], totals[8])
```

```python
from functools import partial
import math

import jax
import jax.numpy as jnp
from jax import lax
from jax.experimental import pallas as pl
from jax.experimental.pallas import tpu as pltpu
from jax.sharding import PartitionSpec as P

HEAD_DIM = 64
AXES = ("dp", "fsdp")
LANES = 384
CHIPS = 16
WIDTH = 768
FF = 3072
VMEM_MIB = 58
F32 = jnp.float32
BF16 = jnp.bfloat16
NEG = -1000000000.0
PHI_RATE = 0.4 / math.sqrt(2.0)
PHI_POLY = (
    0.2256758619023266,
    0.22566959976942397,
    0.20784266147672614,
    0.16854232328082183,
    0.14142988763898146,
    -0.005603842501456246,
    0.16908061566688656,
    -0.18289823607849773,
    0.05026125371366006,
)


def sinusoid(timestep, half_width):
    frequency = jnp.exp(-math.log(10000.0) * jnp.arange(half_width, dtype=F32) / half_width)
    angles = timestep.astype(F32)[:, None] * frequency[None, :]
    return jnp.concatenate([jnp.cos(angles), jnp.sin(angles)], axis=-1)


def dot(left, right):
    return jnp.dot(left, right, preferred_element_type=F32)


def dot_last(left, right):
    return lax.dot_general(left, right, (((1,), (1,)), ((), ())), preferred_element_type=F32)


def dot_first(left, right):
    return lax.dot_general(left, right, (((0,), (0,)), ((), ())), preferred_element_type=F32)


def position_bits(core, masks):
    return [sum(masks[core][b] for b in range(4) if (p >> b) & 1) for p in range(CHIPS)]


CHIP_MASKS = ((2, 1, 8, 4), (2, 1, 4, 8))
ORDER = [position_bits(core, CHIP_MASKS) for core in (0, 1)]
INVERSE = [[ORDER[core].index(k) for k in range(CHIPS)] for core in (0, 1)]


def core_swap(x):
    return lax.ppermute(x, AXES, [(i, i ^ 1) for i in range(2 * CHIPS)])


def chip_swap(x, step):
    return lax.ppermute(
        x, AXES, [(i, i ^ (CHIP_MASKS[i & 1][step] * 2)) for i in range(2 * CHIPS)]
    )


def gather_pieces(piece):
    held = piece
    for step in range(3):
        held = jnp.concatenate([held, chip_swap(held, step)], axis=0)
    far = chip_swap(held, 3)
    return held, far, core_swap(held), core_swap(far)


def add_parts(parts, start, stop):
    total = parts[0][start:stop].astype(F32)
    for part in parts[1:]:
        total = total + part[start:stop].astype(F32)
    return total


def scatter_pieces(mine, theirs):
    parts = [mine, core_swap(theirs)]
    for step, size in ((3, 8), (2, 4), (1, 2), (0, 1)):
        parts.append(chip_swap(add_parts(parts, size, 2 * size).astype(BF16), step))
    return add_parts(parts, 0, 1)[0]


def vmem(count):
    return [pl.BlockSpec(memory_space=pltpu.VMEM)] * count


def smem(count):
    return [pl.BlockSpec(memory_space=pltpu.SMEM)] * count


def anywhere(count):
    return [pl.BlockSpec(memory_space=pl.ANY)] * count


def params():
    return pltpu.CompilerParams(vmem_limit_bytes=VMEM_MIB * 1024 * 1024)


def cost(flops, nbytes, transcendentals=0):
    return pl.CostEstimate(flops=flops, bytes_accessed=nbytes, transcendentals=transcendentals)


def ln_stats(v):
    center = v - jnp.mean(v, axis=-1, keepdims=True)
    scale = lax.rsqrt(jnp.mean(center * center, axis=-1, keepdims=True) + 1e-05)
    return center * scale, scale


def ln_back(y, gain, xhat, scale):
    yg = y * gain
    return scale * (
        yg - jnp.mean(yg, axis=-1, keepdims=True) - xhat * jnp.mean(yg * xhat, axis=-1, keepdims=True)
    )


def first_core(tab):
    return tab[64]


def each_piece(tab, parts, fn):
    core = first_core(tab)
    for side in (0, 1):
        half = core if side == 0 else 1 - core
        for group in (0, 1):
            part = parts[side * 2 + group]

            def body(q, _, part=part, side=side, group=group, half=half):
                chip = tab[side * CHIPS + group * 8 + q]
                fn(part.at[q], chip, half)
                return 0

            lax.fori_loop(0, 8, body, 0)


def rows_of(chip, size):
    return pl.ds(pl.multiple_of(chip * size, size), size)


def lanes_of(half, size, base=0):
    return pl.ds(pl.multiple_of(half * size + base, 128), LANES)


def attention_forward_kernel(
    tab, lens, g_a, g_b, g_c, g_d, x_ref, feat_ref, set_ref,
    normed_ref, qkv_ref, probs_ref, att_ref, mid_ref, two_ref, te_ref, vec_ref,
    w_qkv, w_out, w_time, extra, sem_qkv, sem_out, sem_time, sem_extra,
):
    def fetch(src, chip, half):
        for sec in range(3):
            pltpu.make_async_copy(
                src.at[pl.ds(48 * sec, 48), :],
                w_qkv.at[rows_of(chip, 48), lanes_of(half, 3 * LANES, sec * LANES)],
                sem_qkv,
            ).start()
        pltpu.make_async_copy(
            src.at[pl.ds(144, 48), :], w_out.at[rows_of(chip, 48), lanes_of(half, LANES)], sem_out
        ).start()
        for owner in (0, 1):
            pltpu.make_async_copy(
                src.at[pl.ds(192 + 16 * owner, 16), :],
                w_time.at[owner, rows_of(chip, 16), lanes_of(half, LANES)],
                sem_time,
            ).start()
        pltpu.make_async_copy(
            src.at[pl.ds(224, 16), :], extra.at[half, rows_of(chip, 16), :], sem_extra
        ).start()

    each_piece(tab, (g_a, g_b, g_c, g_d), fetch)
    pltpu.make_async_copy(extra, extra, sem_extra).wait()
    pltpu.make_async_copy(w_time, w_time, sem_time).wait()

    lane = lax.broadcasted_iota(jnp.int32, (128, WIDTH), 1)
    spread = (lax.broadcasted_iota(jnp.int32, (128, WIDTH), 0) == lane % 24).astype(BF16)
    vectors = jnp.zeros((16, WIDTH), F32)
    embed = jnp.zeros((8, WIDTH), F32)
    for owner in (0, 1):
        wide = dot(extra[owner, :, 128:256], spread)
        chip = lax.broadcasted_iota(jnp.int32, (256, WIDTH), 0) // 16
        place = lax.broadcasted_iota(jnp.int32, (256, WIDTH), 1) // 24
        wide = jnp.where(place == chip * 2 + owner, wide, 0.0)
        vectors = vectors + jnp.sum(wide.reshape(CHIPS, 16, WIDTH), axis=0)
        pre = dot_last(feat_ref[...], extra[owner, :, 0:128])
        hidden = (pre / (1.0 + jnp.exp(-pre))).astype(BF16)
        embed = embed + dot(hidden, w_time[owner])
    vec_ref[...] = vectors
    chosen = set_ref[...]
    embed = embed + jnp.where(chosen > 0.5, vectors[3:4, :], vectors[2:3, :])
    te_ref[...] = embed
    gain_one = vectors[0:1, :]
    gain_two = vectors[1:2, :]

    def norm_body(s, _):
        rows = pl.ds(pl.multiple_of(s * 128, 128), 128)
        xhat, _unused = ln_stats(x_ref[rows, :].astype(F32) + te_ref[pl.ds(s, 1), :])
        normed_ref[rows, :] = (xhat * gain_one).astype(BF16)
        return 0

    lax.fori_loop(0, 8, norm_body, 0)
    pltpu.make_async_copy(w_qkv, w_qkv, sem_qkv).wait()

    def qkv_body(i, _):
        rows = pl.ds(pl.multiple_of(i * 256, 256), 256)
        qkv_ref[rows, :] = dot(normed_ref[rows, :], w_qkv[...]).astype(BF16)
        return 0

    lax.fori_loop(0, 4, qkv_body, 0)

    def attend_body(s, _):
        rows = pl.ds(pl.multiple_of(s * 128, 128), 128)
        low_half = lax.broadcasted_iota(jnp.int32, (128, 128), 1) < HEAD_DIM
        keep = lax.broadcasted_iota(jnp.int32, (256, 128), 1) < lens[s]
        for pair in range(6):
            base = (pair // 3) * 3 * LANES + (pair % 3) * 128
            query = qkv_ref[rows, base : base + 128]
            key = qkv_ref[rows, base + LANES : base + LANES + 128]
            value = qkv_ref[rows, base + 2 * LANES : base + 2 * LANES + 128]
            none = jnp.zeros_like(query)
            stacked = jnp.concatenate(
                [jnp.where(low_half, query, none), jnp.where(low_half, none, query)], axis=0
            )
            scores = jnp.where(keep, dot_last(stacked, key) * HEAD_DIM ** (-0.5), NEG)
            shifted = jnp.exp(scores - jnp.max(scores, axis=-1, keepdims=True))
            probs = (shifted / jnp.sum(shifted, axis=-1, keepdims=True)).astype(BF16)
            probs_ref[pl.ds(pl.multiple_of((s * 6 + pair) * 256, 256), 256), :] = probs
            values = jnp.concatenate(
                [jnp.where(low_half, value, none), jnp.where(low_half, none, value)], axis=0
            )
            both = jnp.concatenate([probs[:128], probs[128:]], axis=1)
            att_ref[rows, pair * 128 : pair * 128 + 128] = dot(both, values).astype(BF16)
        return 0

    lax.fori_loop(0, 8, attend_body, 0)
    pltpu.make_async_copy(w_out, w_out, sem_out).wait()

    def out_body(s, _):
        rows = pl.ds(pl.multiple_of(s * 128, 128), 128)
        mid = (
            x_ref[rows, :].astype(F32)
            + te_ref[pl.ds(s, 1), :]
            + dot(att_ref[rows, :], w_out[...])
        )
        mid_ref[rows, :] = mid
        xhat, _unused = ln_stats(mid)
        two_ref[rows, :] = (xhat * gain_two).astype(BF16)
        return 0

    lax.fori_loop(0, 8, out_body, 0)


def attention_forward(tab, lens, pieces, rows, features, sets):
    shape = jax.ShapeDtypeStruct
    return pl.pallas_call(
        attention_forward_kernel,
        out_shape=(
            shape((1024, WIDTH), BF16),
            shape((1024, 3 * WIDTH), BF16),
            shape((48 * 256, 128), BF16),
            shape((1024, WIDTH), BF16),
            shape((1024, WIDTH), F32),
            shape((1024, WIDTH), BF16),
            shape((8, WIDTH), F32),
            shape((16, WIDTH), F32),
        ),
        in_specs=smem(2) + anywhere(4) + vmem(3),
        out_specs=tuple(vmem(8)),
        scratch_shapes=[
            pltpu.VMEM((WIDTH, 3 * WIDTH), BF16),
            pltpu.VMEM((WIDTH, WIDTH), BF16),
            pltpu.VMEM((2, 256, WIDTH), BF16),
            pltpu.VMEM((2, 256, LANES), BF16),
        ]
        + [pltpu.SemaphoreType.DMA] * 4,
        compiler_params=params(),
        cost_estimate=cost(8_000_000_000, 24_000_000, 2_000_000),
        name="attention_forward",
    )(tab, lens, *pieces, rows, features, sets)


def gelu_parts(u):
    size = jnp.abs(u)
    t = 1.0 / (1.0 + PHI_RATE * size)
    poly = jnp.full_like(t, PHI_POLY[-1])
    for coefficient in PHI_POLY[-2::-1]:
        poly = poly * t + coefficient
    bell = jnp.exp(u * u * -0.5)
    tail = bell * (t * poly * 0.5)
    return jnp.where(u > 0, 1.0 - tail, tail), bell * (1.0 / math.sqrt(2.0 * math.pi))


def mlp_kernel(
    tab, g_a, g_b, g_c, g_d, two_ref, out_grad_ref, mid_ref, vec_ref,
    mine_ref, theirs_ref, result_ref, grad_mid_ref, branch_ref, gain_ref,
    w_up, w_down, act, grad_up, back, part, sem_up, sem_down,
):
    core = first_core(tab)

    def fetch(src, chip, half):
        pltpu.make_async_copy(
            src.at[pl.ds(0, 192), :], w_down.at[rows_of(chip, 192), lanes_of(half, LANES)], sem_down
        ).start()
        for block in range(4):
            pltpu.make_async_copy(
                src.at[pl.ds(192 + 48 * block, 48), :],
                w_up.at[rows_of(chip, 48), lanes_of(half, 4 * LANES, block * LANES)],
                sem_up,
            ).start()

    each_piece(tab, (g_a, g_b, g_c, g_d), fetch)
    pltpu.make_async_copy(w_up, w_up, sem_up).wait()
    pltpu.make_async_copy(w_down, w_down, sem_down).wait()

    def chunk_body(j, _):
        cols = pl.ds(pl.multiple_of(j * WIDTH, WIDTH), WIDTH)

        def row_body(i, _):
            rows = pl.ds(pl.multiple_of(i * 256, 256), 256)
            up = dot(two_ref[rows, :], w_up[:, cols])
            grad_act = dot_last(out_grad_ref[rows, :], w_down[cols, :])
            cdf, density = gelu_parts(up)
            activated = (up * cdf).astype(BF16)
            act[rows, :] = activated
            grad = (grad_act * (cdf + up * density)).astype(BF16)
            grad_up[rows, :] = grad
            down = dot(activated, w_down[cols, :])
            normed_back = dot_last(grad, w_up[:, cols])

            @pl.when(j == 0)
            def _():
                grad_mid_ref[rows, :] = mid_ref[rows, :] + down
                back[rows, :] = normed_back

            @pl.when(j > 0)
            def _():
                grad_mid_ref[rows, :] = grad_mid_ref[rows, :] + down
                back[rows, :] = back[rows, :] + normed_back

            return 0

        lax.fori_loop(0, 4, row_body, 0)
        part[...] = dot_first(act[...], out_grad_ref[...]).astype(BF16)
        for side, target in ((0, mine_ref), (1, theirs_ref)):
            half = core if side == 0 else 1 - core
            for k in range(4):
                place = tab[32 + side * CHIPS + j * 4 + k]
                target[place, 0:192, :] = part[192 * k : 192 * k + 192, lanes_of(half, LANES)]
        part[...] = dot_first(two_ref[...], grad_up[...]).astype(BF16)
        for side, target in ((0, mine_ref), (1, theirs_ref)):
            half = core if side == 0 else 1 - core

            @pl.when(j // 2 == half)
            def _(side=side, target=target):
                def store_body(chip, _):
                    place = tab[32 + side * CHIPS + chip]
                    for b in range(2):
                        row = pl.multiple_of(192 + 48 * (2 * (j % 2) + b), 48)
                        target[place, pl.ds(row, 48), :] = part[
                            rows_of(chip, 48), b * LANES : (b + 1) * LANES
                        ]
                    return 0

                lax.fori_loop(0, CHIPS, store_body, 0)

        return 0

    lax.fori_loop(0, 4, chunk_body, 0)
    gain_two = vec_ref[1:2, :]

    def norm_body(s, total):
        rows = pl.ds(pl.multiple_of(s * 128, 128), 128)
        result_ref[rows, :] = grad_mid_ref[rows, :].astype(BF16)
        xhat, scale = ln_stats(mid_ref[rows, :])
        y = back[rows, :]
        grad = out_grad_ref[rows, :].astype(F32) + ln_back(y, gain_two, xhat, scale)
        grad_mid_ref[rows, :] = grad
        branch_ref[rows, :] = grad.astype(BF16)
        return total + jnp.sum(y * xhat, axis=0, keepdims=True)

    gain_ref[...] = lax.fori_loop(0, 8, norm_body, jnp.zeros((1, WIDTH), F32))


def mlp(tab, pieces, two, out_grad, mid, vectors):
    shape = jax.ShapeDtypeStruct
    return pl.pallas_call(
        mlp_kernel,
        out_shape=(
            shape((CHIPS, 384, LANES), BF16),
            shape((CHIPS, 384, LANES), BF16),
            shape((1024, WIDTH), BF16),
            shape((1024, WIDTH), F32),
            shape((1024, WIDTH), BF16),
            shape((1, WIDTH), F32),
        ),
        in_specs=smem(1) + anywhere(4) + vmem(4),
        out_specs=tuple(vmem(6)),
        scratch_shapes=[
            pltpu.VMEM((WIDTH, FF), BF16),
            pltpu.VMEM((FF, WIDTH), BF16),
            pltpu.VMEM((1024, WIDTH), BF16),
            pltpu.VMEM((1024, WIDTH), BF16),
            pltpu.VMEM((1024, WIDTH), F32),
            pltpu.VMEM((WIDTH, WIDTH), BF16),
            pltpu.SemaphoreType.DMA,
            pltpu.SemaphoreType.DMA,
        ],
        compiler_params=params(),
        cost_estimate=cost(30_000_000_000, 40_000_000, 3_000_000),
        name="mlp",
    )(tab, *pieces, two, out_grad, mid, vectors)


def attention_backward_kernel(
    tab, g_a, g_b, g_c, g_d, branch_ref, att_ref, qkv_ref, probs_ref, normed_ref,
    mine_ref, theirs_ref, grad_qkv_ref,
    w_out, grad_att, part, sem,
):
    core = first_core(tab)

    def fetch(src, chip, half):
        pltpu.make_async_copy(
            src.at[pl.ds(144, 48), :], w_out.at[rows_of(chip, 48), lanes_of(half, LANES)], sem
        ).start()

    each_piece(tab, (g_a, g_b, g_c, g_d), fetch)
    pltpu.make_async_copy(w_out, w_out, sem).wait()

    def grad_att_body(i, _):
        rows = pl.ds(pl.multiple_of(i * 256, 256), 256)
        grad_att[rows, :] = dot_last(branch_ref[rows, :], w_out[...]).astype(BF16)
        return 0

    lax.fori_loop(0, 4, grad_att_body, 0)

    def store(side, target, block, columns):
        def store_body(chip, _):
            place = tab[32 + side * CHIPS + chip]
            target[place, 48 * block : 48 * block + 48, :] = part[rows_of(chip, 48), columns]
            return 0

        lax.fori_loop(0, CHIPS, store_body, 0)

    part[...] = dot_first(att_ref[...], branch_ref[...]).astype(BF16)
    store(0, mine_ref, 3, lanes_of(core, LANES))
    store(1, theirs_ref, 3, lanes_of(1 - core, LANES))

    def attend_body(s, _):
        rows = pl.ds(pl.multiple_of(s * 128, 128), 128)
        low_half = lax.broadcasted_iota(jnp.int32, (128, 128), 1) < HEAD_DIM

        def heads(x):
            none = jnp.zeros_like(x)
            return jnp.concatenate(
                [jnp.where(low_half, x, none), jnp.where(low_half, none, x)], axis=0
            )

        for pair in range(6):
            base = (pair // 3) * 3 * LANES + (pair % 3) * 128
            query = heads(qkv_ref[rows, base : base + 128])
            key = heads(qkv_ref[rows, base + LANES : base + LANES + 128])
            value = qkv_ref[rows, base + 2 * LANES : base + 2 * LANES + 128]
            up = heads(grad_att[rows, pair * 128 : pair * 128 + 128])
            probs_low = probs_ref[pl.ds(pl.multiple_of((s * 6 + pair) * 256, 256), 256), :]
            probs = probs_low.astype(F32)
            grad_probs = dot_last(up, value)
            inner = jnp.sum(probs * grad_probs, axis=-1, keepdims=True)
            grad_scores = (probs * (grad_probs - inner)).astype(BF16)
            both = jnp.concatenate([grad_scores[:128], grad_scores[128:]], axis=1)
            grad_query = dot(both, key) * HEAD_DIM ** (-0.5)
            grad_key = dot_first(grad_scores, query) * HEAD_DIM ** (-0.5)
            grad_value = dot_first(probs_low, up)
            grad_qkv_ref[rows, base : base + 128] = grad_query.astype(BF16)
            grad_qkv_ref[rows, base + LANES : base + LANES + 128] = grad_key.astype(BF16)
            grad_qkv_ref[rows, base + 2 * LANES : base + 2 * LANES + 128] = grad_value.astype(BF16)
        return 0

    lax.fori_loop(0, 8, attend_body, 0)

    for half in (0, 1):
        for sec in range(3):
            col = half * 3 * LANES + sec * LANES
            part[:, 0:LANES] = dot_first(
                normed_ref[...], grad_qkv_ref[:, col : col + LANES]
            ).astype(BF16)

            @pl.when(core == half)
            def _(sec=sec):
                store(0, mine_ref, sec, slice(0, LANES))

            @pl.when(core != half)
            def _(sec=sec):
                store(1, theirs_ref, sec, slice(0, LANES))


def attention_backward(tab, pieces, branch, att, qkv, probs, normed):
    shape = jax.ShapeDtypeStruct
    return pl.pallas_call(
        attention_backward_kernel,
        out_shape=(
            shape((CHIPS, 192, LANES), BF16),
            shape((CHIPS, 192, LANES), BF16),
            shape((1024, 3 * WIDTH), BF16),
        ),
        in_specs=smem(1) + anywhere(4) + vmem(5),
        out_specs=tuple(vmem(3)),
        scratch_shapes=[
            pltpu.VMEM((WIDTH, WIDTH), BF16),
            pltpu.VMEM((1024, WIDTH), BF16),
            pltpu.VMEM((WIDTH, WIDTH), BF16),
            pltpu.SemaphoreType.DMA,
        ],
        compiler_params=params(),
        cost_estimate=cost(10_000_000_000, 20_000_000),
        name="attention_backward",
    )(tab, *pieces, branch, att, qkv, probs, normed)


def input_backward_kernel(
    tab, g_a, g_b, g_c, g_d, grad_qkv_ref, x_ref, te_ref, vec_ref, grad_mid_ref, gain_two_ref,
    input_ref, small_ref,
    w_qkv, sem,
):
    def fetch(src, chip, half):
        for sec in range(3):
            pltpu.make_async_copy(
                src.at[pl.ds(48 * sec, 48), :],
                w_qkv.at[rows_of(chip, 48), lanes_of(half, 3 * LANES, sec * LANES)],
                sem,
            ).start()

    each_piece(tab, (g_a, g_b, g_c, g_d), fetch)
    pltpu.make_async_copy(w_qkv, w_qkv, sem).wait()
    gain = vec_ref[0:1, :]

    def body(s, total):
        rows = pl.ds(pl.multiple_of(s * 128, 128), 128)
        y = dot_last(grad_qkv_ref[rows, :], w_qkv[...])
        xhat, scale = ln_stats(x_ref[rows, :].astype(F32) + te_ref[pl.ds(s, 1), :])
        grad = grad_mid_ref[rows, :] + ln_back(y, gain, xhat, scale)
        input_ref[rows, :] = grad.astype(BF16)
        small_ref[pl.ds(s, 1), :] = jnp.sum(grad, axis=0, keepdims=True)
        return total + jnp.sum(y * xhat, axis=0, keepdims=True)

    small_ref[8:9, :] = lax.fori_loop(0, 8, body, jnp.zeros((1, WIDTH), F32))
    small_ref[9:10, :] = gain_two_ref[...]
    small_ref[10:16, :] = jnp.zeros((6, WIDTH), F32)


def input_backward(tab, pieces, grad_qkv, rows, embed, vectors, grad_mid, gain_two):
    shape = jax.ShapeDtypeStruct
    return pl.pallas_call(
        input_backward_kernel,
        out_shape=(shape((1024, WIDTH), BF16), shape((16, WIDTH), F32)),
        in_specs=smem(1) + anywhere(4) + vmem(6),
        out_specs=tuple(vmem(2)),
        scratch_shapes=[pltpu.VMEM((WIDTH, 3 * WIDTH), BF16), pltpu.SemaphoreType.DMA],
        compiler_params=params(),
        cost_estimate=cost(4_000_000_000, 18_000_000),
        name="input_backward",
    )(tab, *pieces, grad_qkv, rows, embed, vectors, grad_mid, gain_two)


def pick(stacked, index):
    return lax.dynamic_index_in_dim(stacked, index, 0, keepdims=False)


def in_core_order(core, own, other, axis):
    return jnp.where(
        core == 0,
        jnp.concatenate([own, other], axis=axis),
        jnp.concatenate([other, own], axis=axis),
    )


def pack_extra(time_in, vectors, ints):
    rows = time_in.shape[0]
    filler = jnp.zeros((rows, 128), BF16)
    vec = lax.dynamic_update_slice(filler, vectors, (0, 0))
    num = lax.dynamic_update_slice(filler, ints[None, :], (0, 0))
    return jnp.concatenate([time_in, vec, num], axis=1)


def split_time(timestep, dataset):
    steps = timestep.reshape(-1)
    return jnp.concatenate([steps // 64, steps % 64, dataset.reshape(-1)]).astype(BF16)


def gather_all(x):
    return lax.all_gather(x, AXES, axis=0, tiled=True)


def shards(
    block_input,
    out_grad,
    timestep,
    dataset,
    lengths,
    norm1_gain,
    qkv_weight,
    out_weight,
    norm2_gain,
    up_weight,
    down_weight,
    time_in,
    time_out,
    data_embed,
    devices,
):
    flat = lax.axis_index(AXES)
    exchange = devices == 2 * CHIPS
    vectors = jnp.concatenate([norm1_gain[None], norm2_gain[None], data_embed.T], axis=0)
    numbers = split_time(timestep, dataset)
    count = numbers.shape[0] // 3
    if exchange:
        core = flat & 1
        chip = flat >> 1
        order = jnp.array(ORDER, jnp.int32)
        inverse = jnp.array(INVERSE, jnp.int32)
        where = jnp.bitwise_xor(chip, jnp.arange(CHIPS, dtype=jnp.int32))
        first = core == 0
        tab = jnp.concatenate(
            [
                jnp.bitwise_xor(chip, jnp.where(first, order[0], order[1])),
                jnp.bitwise_xor(chip, jnp.where(first, order[1], order[0])),
                jnp.where(first, inverse[0][where], inverse[1][where]),
                jnp.where(first, inverse[1][where], inverse[0][where]),
                jnp.full((8,), core, jnp.int32),
            ]
        )
        wide = jnp.concatenate(
            [qkv_weight.reshape(24, 3, 2, LANES), out_weight.reshape(24, 1, 2, LANES)], axis=1
        ).transpose(2, 1, 0, 3)
        time_halves = time_out.reshape(16, 2, LANES).transpose(1, 0, 2)
        both = jnp.concatenate([wide.reshape(2, 96, LANES), time_halves], axis=1)
        own = pick(both, core)
        other = core_swap(pick(both, 1 - core))
        blocks = in_core_order(
            core, own[:96].reshape(4, 24, LANES), other[:96].reshape(4, 24, LANES), 1
        )
        attention_piece = jnp.concatenate(
            [
                blocks.reshape(192, LANES),
                in_core_order(core, own[96:], other[96:], 0),
                pack_extra(time_in, vectors, numbers),
            ],
            axis=0,
        )[None]
        up_halves = up_weight.reshape(24, 2, 4, LANES).transpose(1, 2, 0, 3)
        down_halves = down_weight.reshape(96, 2, LANES).transpose(1, 0, 2)
        both = jnp.concatenate([down_halves, up_halves.reshape(2, 96, LANES)], axis=1)
        own = pick(both, core)
        other = core_swap(pick(both, 1 - core))
        blocks = in_core_order(
            core, own[96:].reshape(4, 24, LANES), other[96:].reshape(4, 24, LANES), 1
        )
        mlp_piece = jnp.concatenate(
            [in_core_order(core, own[:96], other[:96], 0), blocks.reshape(192, LANES)], axis=0
        )[None]
        attention_pieces = gather_pieces(attention_piece)
        mlp_pieces = gather_pieces(mlp_piece)
        seen = jnp.concatenate([g[:, 224, 256 : 256 + 3 * count] for g in attention_pieces], axis=0)
    else:
        tab = jnp.concatenate(
            [jnp.tile(jnp.arange(CHIPS, dtype=jnp.int32), 4), jnp.zeros((8,), jnp.int32)]
        )
        full_qkv = gather_all(qkv_weight).reshape(CHIPS, 48, 3, 2, LANES)
        full_out = gather_all(out_weight).reshape(CHIPS, 48, 1, 2, LANES)
        full_up = gather_all(up_weight).reshape(CHIPS, 48, 2, 4, LANES)
        full_down = gather_all(down_weight).reshape(CHIPS, 192, 2, LANES)
        full_tin = gather_all(time_in).reshape(CHIPS, 2, 16, 128)
        full_tout = gather_all(time_out).reshape(CHIPS, 32, 2, LANES)
        full_vec = lax.all_gather(vectors, AXES, axis=1, tiled=True).reshape(4, CHIPS, 2, 24)
        seen = gather_all(numbers[None])
        extra = jnp.zeros((CHIPS, 2, 16, LANES), BF16)
        extra = extra.at[:, :, :, :128].set(full_tin)
        extra = extra.at[:, :, 0:4, 128:152].set(full_vec.transpose(1, 2, 0, 3))
        attention_pieces = []
        mlp_pieces = []
        for half in (0, 1):
            wide = jnp.concatenate([full_qkv[:, :, :, half], full_out[:, :, :, half]], axis=2)
            whole = jnp.concatenate(
                [
                    wide.transpose(0, 2, 1, 3).reshape(CHIPS, 192, LANES),
                    full_tout[:, :, half],
                    extra[:, half],
                ],
                axis=1,
            )
            attention_pieces += [whole[:8], whole[8:]]
            whole = jnp.concatenate(
                [
                    full_down[:, :, half],
                    full_up[:, :, half].transpose(0, 2, 1, 3).reshape(CHIPS, 192, LANES),
                ],
                axis=1,
            )
            mlp_pieces += [whole[:8], whole[8:]]

    micros, seqs, seq_len, width = block_input.shape
    tokens = micros * seqs * seq_len
    x_rows = block_input.reshape(tokens, width)
    grad_rows = out_grad.reshape(tokens, width)
    features = sinusoid(timestep.reshape(-1), time_in.shape[1] // 2).astype(BF16)
    sets = dataset.reshape(-1, 1).astype(F32)
    normed, qkv, probs, att, mid, two, embed, vecs = attention_forward(
        tab, lengths.reshape(-1), attention_pieces, x_rows, features, sets
    )
    mlp_mine, mlp_theirs, result, grad_mid, branch, gain_two = mlp(
        tab, mlp_pieces, two, grad_rows, mid, vecs
    )
    att_mine, att_theirs, grad_qkv = attention_backward(
        tab, attention_pieces, branch, att, qkv, probs, normed
    )
    grad_input, small = input_backward(
        tab, attention_pieces, grad_qkv, x_rows, embed, vecs, grad_mid, gain_two
    )

    small = small.astype(BF16)[None]
    if exchange:
        every = jnp.concatenate(gather_pieces(small), axis=0)
    else:
        every = gather_all(small)
    every = every.reshape(devices * 16, width)
    steps = seen[:, :count] * 64 + seen[:, count : 2 * count].astype(F32)
    wave = sinusoid(steps.reshape(-1), time_in.shape[1] // 2).astype(BF16)
    wave = jnp.pad(wave.reshape(devices, count, -1), ((0, 0), (0, 16 - count), (0, 0)))
    wave = wave.reshape(devices * 16, -1)
    which = jnp.pad(seen[:, 2 * count :], ((0, 0), (0, 16 - count))).reshape(-1)
    place = jnp.tile(jnp.arange(16), devices)
    hot = jnp.stack(
        [(place < count) & (which == 0), (place < count) & (which == 1), place == 8, place == 9]
    ).astype(BF16)
    pre = dot_last(wave, time_in)
    gate = 1.0 / (1.0 + jnp.exp(-pre))
    hidden = (pre * gate).astype(BF16)
    grad_tout = dot_first(hidden, every)
    grad_pre = dot_last(every, time_out) * (gate * (1.0 + pre * (1.0 - gate)))
    grad_tin = dot_first(grad_pre.astype(BF16), wave)
    sums = dot(hot, every)
    own_cols = norm1_gain.shape[0]
    sums = lax.dynamic_slice_in_dim(sums, flat * own_cols, own_cols, 1)

    if exchange:
        piece = scatter_pieces(mlp_mine, mlp_theirs)
        down = piece[:192].reshape(2, 96, LANES)
        up = piece[192:].reshape(4, 2, 24, LANES).transpose(1, 0, 2, 3).reshape(2, 96, LANES)
        both = jnp.concatenate([down, up], axis=1)
        own = pick(both, core)
        other = core_swap(pick(both, 1 - core))
        grad_down = in_core_order(core, own[:96], other[:96], 1)
        grad_up = in_core_order(
            core, own[96:].reshape(4, 24, LANES), other[96:].reshape(4, 24, LANES), 0
        )
        grad_up = grad_up.transpose(1, 0, 2).reshape(24, FF)
        piece = scatter_pieces(att_mine, att_theirs)
        both = piece.reshape(4, 2, 24, LANES).transpose(1, 0, 2, 3)
        own = pick(both, core)
        other = core_swap(pick(both, 1 - core))
        joined = in_core_order(core, own[:, None], other[:, None], 1)
        joined = joined.transpose(2, 0, 1, 3).reshape(24, 4 * WIDTH)
        grad_qkv_weight = joined[:, : 3 * WIDTH]
        grad_out_weight = joined[:, 3 * WIDTH :]
    else:
        scatter = partial(lax.psum_scatter, axis_name=AXES, scatter_dimension=0, tiled=True)
        both = jnp.stack([mlp_mine, mlp_theirs]).astype(F32)
        grad_down = scatter(both[:, :, :192].transpose(1, 2, 0, 3).reshape(FF, WIDTH))
        grad_up = scatter(
            both[:, :, 192:].reshape(2, CHIPS, 4, 48, LANES).transpose(1, 3, 0, 2, 4).reshape(WIDTH, FF)
        )
        both = jnp.stack([att_mine, att_theirs]).astype(F32).reshape(2, CHIPS, 4, 48, LANES)
        both = scatter(both.transpose(1, 3, 2, 0, 4).reshape(WIDTH, 4 * WIDTH))
        grad_qkv_weight = both[:, : 3 * WIDTH]
        grad_out_weight = both[:, 3 * WIDTH :]

    return (
        result.reshape(block_input.shape),
        grad_input.reshape(block_input.shape),
        sums[2],
        grad_qkv_weight,
        grad_out_weight,
        sums[3],
        grad_up,
        grad_down,
        grad_tin,
        grad_tout,
        sums[:2].T,
    )


def solution(mesh):
    devices = mesh.shape["dp"] * mesh.shape["fsdp"]
    seq_spec = P(None, AXES, None, None)
    int_spec = P(None, AXES)
    row_spec = P(AXES, None)
    in_specs = (seq_spec, seq_spec, int_spec, int_spec, int_spec, P(AXES), row_spec, row_spec, P(AXES))
    in_specs = in_specs + (row_spec,) * 5
    out_specs = (seq_spec, seq_spec, P(AXES), row_spec, row_spec, P(AXES)) + (row_spec,) * 5
    return jax.shard_map(
        partial(shards, devices=devices),
        mesh=mesh,
        in_specs=in_specs,
        out_specs=out_specs,
        check_vma=False,
    )
```

```python
from functools import partial
import math

import jax
import jax.numpy as jnp
from jax import lax
from jax.experimental import pallas as pl
from jax.experimental.pallas import tpu as pltpu
from jax.sharding import PartitionSpec as P

HEAD_DIM = 64
AXES = ("dp", "fsdp")
LANES = 384
CHIPS = 16
WIDTH = 768
FF = 3072
VMEM_MIB = 58
F32 = jnp.float32
BF16 = jnp.bfloat16
NEG = -1000000000.0


def sinusoid(timestep, half_width):
    frequency = jnp.exp(-math.log(10000.0) * jnp.arange(half_width, dtype=F32) / half_width)
    angles = timestep.astype(F32)[:, None] * frequency[None, :]
    return jnp.concatenate([jnp.cos(angles), jnp.sin(angles)], axis=-1)


def dot(left, right):
    return jnp.dot(left, right, preferred_element_type=F32)


def dot_last(left, right):
    return lax.dot_general(left, right, (((1,), (1,)), ((), ())), preferred_element_type=F32)


def dot_first(left, right):
    return lax.dot_general(left, right, (((0,), (0,)), ((), ())), preferred_element_type=F32)


def position_bits(core, masks):
    return [sum(masks[core][b] for b in range(4) if (p >> b) & 1) for p in range(CHIPS)]


CHIP_MASKS = ((2, 1, 8, 4), (2, 1, 4, 8))
ORDER = [position_bits(core, CHIP_MASKS) for core in (0, 1)]
INVERSE = [[ORDER[core].index(k) for k in range(CHIPS)] for core in (0, 1)]


def core_swap(x):
    return lax.ppermute(x, AXES, [(i, i ^ 1) for i in range(2 * CHIPS)])


def chip_swap(x, position):
    return lax.ppermute(
        x, AXES, [(i, i ^ (ORDER[i & 1][position] * 2)) for i in range(2 * CHIPS)]
    )


def after(x, *others):
    return lax.optimization_barrier((x,) + others)[0]


def gather_line(piece):
    return jnp.concatenate([piece] + [chip_swap(piece, p) for p in (1, 2, 3)], axis=0)


def gather_plane(held):
    return jnp.concatenate([held, chip_swap(held, 4)], axis=0)


def gather_pieces(piece):
    held = gather_plane(gather_line(piece))
    far = chip_swap(held, 8)
    return held, far, core_swap(held), core_swap(far)


class Scatter:
    def __init__(self, theirs):
        self.parts = [core_swap(theirs)]
        self.steps = [(8,), (4,), (1, 2, 3)]

    def sum(self, start, stop):
        total = self.parts[0][start:stop].astype(F32)
        for part in self.parts[1:]:
            total = total + part[start:stop].astype(F32)
        return total

    def send(self):
        self.positions = self.steps.pop(0)
        size = 1 if len(self.positions) == 3 else self.positions[0]
        self.sent = tuple(self.sum(p, p + size).astype(BF16) for p in self.positions)
        return self.sent

    def receive(self, *others):
        brought = [chip_swap(x, p) for x, p in zip(self.sent, self.positions)]
        self.parts += [after(x, *others) for x in brought] if others else brought

    def step(self, *others):
        self.receive(*others)
        return self.send()

    def total(self, *others):
        self.receive(*others)
        return self.sum(0, 1)[0]


VMEM_SPEC = pl.BlockSpec(memory_space=pltpu.VMEM)
SMEM_SPEC = pl.BlockSpec(memory_space=pltpu.SMEM)
ANY_SPEC = pl.BlockSpec(memory_space=pl.ANY)


def tiles(rows, cols):
    return pl.BlockSpec((rows, cols), lambda i: (i, 0))


def columns(rows, cols):
    return pl.BlockSpec((rows, cols), lambda i: (0, i))


def fixed(*shape):
    return pl.BlockSpec(shape, lambda i: (0,) * len(shape))


def shaped(shape, dtype=BF16):
    return jax.ShapeDtypeStruct(shape, dtype)


def params():
    return pltpu.CompilerParams(vmem_limit_bytes=VMEM_MIB * 1024 * 1024)


def cost(flops, nbytes, transcendentals=0):
    return pl.CostEstimate(flops=flops, bytes_accessed=nbytes, transcendentals=transcendentals)


def ln_stats(v):
    center = v - jnp.mean(v, axis=-1, keepdims=True)
    scale = lax.rsqrt(jnp.mean(center * center, axis=-1, keepdims=True) + 1e-05)
    return center * scale, scale


def ln_back(y, gain, xhat, scale):
    yg = y * gain
    return scale * (
        yg - jnp.mean(yg, axis=-1, keepdims=True) - xhat * jnp.mean(yg * xhat, axis=-1, keepdims=True)
    )


def first_core(tab):
    return tab[64]


def each_piece(tab, parts, fn):
    core = first_core(tab)
    for side in (0, 1):
        half = core if side == 0 else 1 - core
        for group in (0, 1):
            part = parts[side * 2 + group]

            def body(q, _, part=part, side=side, group=group, half=half):
                chip = tab[side * CHIPS + group * 8 + q]
                fn(part.at[q], chip, half)
                return 0

            lax.fori_loop(0, 8, body, 0)


def rows_of(chip, size):
    return pl.ds(pl.multiple_of(chip * size, size), size)


def lanes_of(half, size, base=0):
    return pl.ds(pl.multiple_of(half * size + base, 128), LANES)


def fetch_pieces(tab, parts, rows, dst, sem):
    each_piece(
        tab,
        parts,
        lambda src, chip, half: pltpu.make_async_copy(
            src.at[pl.ds(0, rows), :], dst.at[chip, half], sem
        ).start(),
    )


def block(pieces, half, first, rows=48):
    return pieces[:, half, first : first + rows, :].reshape(CHIPS * rows, LANES)


def both_halves(pieces, first, rows=48):
    return jnp.concatenate([block(pieces, h, first, rows) for h in (0, 1)], axis=1)


def down_rows(pieces, j):
    return jnp.concatenate(
        [pieces[4 * j : 4 * j + 4, h].reshape(WIDTH, LANES) for h in (0, 1)], axis=1
    )


def qkv_columns(pieces, half):
    return jnp.concatenate([block(pieces, half, 48 * sec) for sec in range(3)], axis=1)


def finish(ref, sem):
    pltpu.make_async_copy(ref, ref, sem).wait()


def add_embed(x, embed, i):
    seqs = x.shape[0] // 128
    parts = [
        x[128 * k : 128 * k + 128].astype(F32) + embed[pl.ds(i * seqs + k, 1), :]
        for k in range(seqs)
    ]
    return jnp.concatenate(parts, axis=0)


def qkv_kernel(
    tab, g_a, g_b, g_c, g_d, x_ref, feat_ref, set_ref,
    normed_ref, qkv_ref, te_ref, vec_ref,
    w, sem,
):
    i = pl.program_id(0)

    @pl.when(i == 0)
    def _():
        fetch_pieces(tab, (g_a, g_b, g_c, g_d), 192, w, sem)
        finish(w, sem)
        lane = lax.broadcasted_iota(jnp.int32, (128, WIDTH), 1)
        spread = (lax.broadcasted_iota(jnp.int32, (128, WIDTH), 0) == lane % 24).astype(BF16)
        vectors = jnp.zeros((16, WIDTH), F32)
        embed = jnp.zeros((8, WIDTH), F32)
        for owner in (0, 1):
            extra = block(w, owner, 176, 16)
            wide = dot(extra[:, 128:256], spread)
            chip = lax.broadcasted_iota(jnp.int32, (256, WIDTH), 0) // 16
            place = lax.broadcasted_iota(jnp.int32, (256, WIDTH), 1) // 24
            wide = jnp.where(place == chip * 2 + owner, wide, 0.0)
            vectors = vectors + jnp.sum(wide.reshape(CHIPS, 16, WIDTH), axis=0)
            pre = dot_last(feat_ref[...], extra[:, 0:128])
            hidden = (pre / (1.0 + jnp.exp(-pre))).astype(BF16)
            embed = embed + dot(hidden, both_halves(w, 144 + 16 * owner, 16))
        vec_ref[...] = vectors
        te_ref[...] = embed + jnp.where(set_ref[...] > 0.5, vectors[3:4, :], vectors[2:3, :])

    xhat, _unused = ln_stats(add_embed(x_ref[...], te_ref, i))
    normed_ref[...] = (xhat * vec_ref[0:1, :]).astype(BF16)
    for half in (0, 1):
        cols = slice(half * 3 * LANES, (half + 1) * 3 * LANES)
        qkv_ref[:, cols] = dot(normed_ref[...], qkv_columns(w, half)).astype(BF16)


def qkv_forward(tab, pieces, rows, features, sets):
    return pl.pallas_call(
        qkv_kernel,
        grid=(4,),
        out_shape=(
            shaped((1024, WIDTH)),
            shaped((1024, 3 * WIDTH)),
            shaped((8, WIDTH), F32),
            shaped((16, WIDTH), F32),
        ),
        in_specs=[SMEM_SPEC] + [ANY_SPEC] * 4 + [tiles(256, WIDTH), fixed(8, 128), fixed(8, 1)],
        out_specs=(tiles(256, WIDTH), tiles(256, 3 * WIDTH), fixed(8, WIDTH), fixed(16, WIDTH)),
        scratch_shapes=[pltpu.VMEM((CHIPS, 2, 192, LANES), BF16), pltpu.SemaphoreType.DMA],
        compiler_params=params(),
        cost_estimate=cost(4_000_000_000, 12_000_000),
        name="qkv_forward",
    )(tab, *pieces, rows, features, sets)


def two_heads(x, low_half):
    none = jnp.zeros_like(x)
    return jnp.concatenate([jnp.where(low_half, x, none), jnp.where(low_half, none, x)], axis=0)


def side_by_side(x):
    return jnp.concatenate([x[:128], x[128:]], axis=1)


def pair_base(pair):
    return (pair // 3) * 3 * LANES + (pair % 3) * 128


def attention_kernel(lens, qkv_ref, probs_ref, att_ref):
    low_half = lax.broadcasted_iota(jnp.int32, (128, 128), 1) < HEAD_DIM
    lane = lax.broadcasted_iota(jnp.int32, (256, 128), 1)
    for k in range(2):
        keep = lane < lens[pl.program_id(0) * 2 + k]
        rows = slice(128 * k, 128 * k + 128)
        scores = []
        for pair in range(6):
            base = pair_base(pair)
            query = two_heads(qkv_ref[rows, base : base + 128], low_half)
            key = qkv_ref[rows, base + LANES : base + LANES + 128]
            scores.append(jnp.where(keep, dot_last(query, key) * HEAD_DIM ** (-0.5), NEG))
        probs = []
        for pair in range(6):
            shifted = jnp.exp(scores[pair] - jnp.max(scores[pair], axis=-1, keepdims=True))
            total = jnp.sum(shifted, axis=-1, keepdims=True)
            probs.append((shifted * (1.0 / total)).astype(BF16))
            first = 256 * (6 * k + pair)
            probs_ref[first : first + 256, :] = probs[pair]
        for pair in range(6):
            base = pair_base(pair) + 2 * LANES
            value = two_heads(qkv_ref[rows, base : base + 128], low_half)
            att_ref[rows, pair * 128 : pair * 128 + 128] = dot(
                side_by_side(probs[pair]), value
            ).astype(BF16)


def attention(lens, qkv):
    return pl.pallas_call(
        attention_kernel,
        grid=(4,),
        out_shape=(shaped((48 * 256, 128)), shaped((1024, WIDTH))),
        in_specs=[SMEM_SPEC, tiles(256, 3 * WIDTH)],
        out_specs=(tiles(12 * 256, 128), tiles(256, WIDTH)),
        compiler_params=params(),
        cost_estimate=cost(4_000_000_000, 9_000_000, 1_600_000),
        name="attention",
    )(lens, qkv)


def gelu_parts(u):
    cdf = 0.5 + 0.5 * lax.erf(u * math.sqrt(0.5))
    return cdf, jnp.exp(u * u * -0.5) * (1.0 / math.sqrt(2.0 * math.pi))


def up_kernel(
    g_ref, att_ref, x_ref, te_ref, vec_ref,
    mid_ref, two_ref, act_ref, slope_ref,
    w, sem,
):
    i = pl.program_id(0)

    @pl.when(i == 0)
    def _():
        pltpu.make_async_copy(g_ref, w, sem).start()
        finish(w, sem)

    mid = add_embed(x_ref[...], te_ref, i) + dot(att_ref[...], w[:, FF:])
    mid_ref[...] = mid
    xhat, _unused = ln_stats(mid)
    two_ref[...] = (xhat * vec_ref[1:2, :]).astype(BF16)
    for j in range(4):
        cols = slice(j * WIDTH, (j + 1) * WIDTH)
        up = dot(two_ref[...], w[:, cols])
        cdf, density = gelu_parts(up)
        act_ref[:, cols] = (up * cdf).astype(BF16)
        slope_ref[:, cols] = (cdf + up * density).astype(BF16)


def up_forward(gathered, att, rows, embed, vectors):
    return pl.pallas_call(
        up_kernel,
        grid=(4,),
        out_shape=(
            shaped((1024, WIDTH), F32),
            shaped((1024, WIDTH)),
            shaped((1024, FF)),
            shaped((1024, FF)),
        ),
        in_specs=[ANY_SPEC, tiles(256, WIDTH), tiles(256, WIDTH), fixed(8, WIDTH), fixed(16, WIDTH)],
        out_specs=(tiles(256, WIDTH), tiles(256, WIDTH), tiles(256, FF), tiles(256, FF)),
        scratch_shapes=[pltpu.VMEM((WIDTH, FF + WIDTH), BF16), pltpu.SemaphoreType.DMA],
        compiler_params=params(),
        cost_estimate=cost(8_000_000_000, 26_000_000, 6_000_000),
        name="up_forward",
    )(gathered, att, rows, embed, vectors)


def half_of(tab, side):
    return first_core(tab) if side == 0 else 1 - first_core(tab)


def down_grad_kernel(act_ref, out_grad_ref, out_ref):
    out_ref[...] = dot_first(act_ref[...], out_grad_ref[...]).astype(BF16)


def down_grad(act, out_grad):
    return pl.pallas_call(
        down_grad_kernel,
        grid=(4,),
        out_shape=shaped((FF, WIDTH)),
        in_specs=[columns(1024, WIDTH), fixed(1024, WIDTH)],
        out_specs=tiles(WIDTH, WIDTH),
        compiler_params=params(),
        cost_estimate=cost(5_000_000_000, 13_000_000),
        name="down_grad",
    )(act, out_grad)


def store_blocks(tab, side, target, first, part, lanes):
    for chip in range(CHIPS):
        place = tab[32 + side * CHIPS + chip]
        target[place, pl.ds(first, 48), :] = part[48 * chip : 48 * chip + 48, lanes]


def up_grad_kernel(tab, two_ref, grad_up_ref, out_ref, part):
    j = pl.program_id(0)
    part[...] = dot_first(two_ref[...], grad_up_ref[...]).astype(BF16)
    for b in range(2):
        first = pl.multiple_of((2 * j + b) * 48, 48)
        store_blocks(tab, 0, out_ref, first, part, slice(b * LANES, (b + 1) * LANES))


def up_grad(tab, two, grad_up):
    return pl.pallas_call(
        up_grad_kernel,
        grid_spec=pltpu.PrefetchScalarGridSpec(
            num_scalar_prefetch=1,
            grid=(2,),
            in_specs=[
                pl.BlockSpec((1024, WIDTH), lambda j, tab: (0, 0)),
                pl.BlockSpec((1024, WIDTH), lambda j, tab: (0, half_of(tab, 0) * 2 + j)),
            ],
            out_specs=VMEM_SPEC,
            scratch_shapes=[pltpu.VMEM((WIDTH, WIDTH), BF16)],
        ),
        out_shape=shaped((CHIPS, 192, LANES)),
        compiler_params=params(),
        cost_estimate=cost(2_400_000_000, 8_000_000),
        name="up_grad",
    )(tab, two, grad_up)


def clamped(rows, cols):
    return pl.BlockSpec((rows, cols), lambda i: (jnp.minimum(i, 3), 0))


def mlp_backward_kernel(
    tab, g_ref, d_a, d_b, d_c, d_d, two_hbm, act_ref, slope_ref, out_grad_ref, mid_ref, vec_ref,
    result_ref, grad_mid_ref, branch_ref, grad_up_ref, grad_att_ref, gain_ref, theirs_ref,
    w, w_down, two, kept, part, sem, sem_down, sem_two,
):
    i = pl.program_id(0)

    @pl.when(i == 0)
    def _():
        fetch_pieces(tab, (d_a, d_b, d_c, d_d), 192, w_down, sem_down)
        gain_ref[...] = jnp.zeros_like(gain_ref)
        finish(w_down, sem_down)
        pltpu.make_async_copy(g_ref, w, sem).start()
        pltpu.make_async_copy(two_hbm, two, sem_two).start()

    @pl.when(i < 4)
    def _():
        total = mid_ref[...]
        for j in range(4):
            cols = slice(j * WIDTH, (j + 1) * WIDTH)
            total = total + dot(act_ref[:, cols], down_rows(w_down, j))
            grad_act = dot_last(out_grad_ref[...], down_rows(w_down, j))
            grad_up_ref[:, cols] = (grad_act * slope_ref[:, cols].astype(F32)).astype(BF16)
        result_ref[...] = total.astype(BF16)

        @pl.when(i == 0)
        def _():
            finish(w, sem)

        y = jnp.zeros_like(total)
        for j in range(4):
            cols = slice(j * WIDTH, (j + 1) * WIDTH)
            y = y + dot_last(grad_up_ref[:, cols], w[:, cols])
        theirs = pl.ds(pl.multiple_of(half_of(tab, 1) * 4 * LANES, 128), 4 * LANES)
        kept[rows_of(i, 256), :] = grad_up_ref[:, theirs]
        xhat, scale = ln_stats(mid_ref[...])
        grad = out_grad_ref[...].astype(F32) + ln_back(y, vec_ref[1:2, :], xhat, scale)
        grad_mid_ref[...] = grad
        branch_ref[...] = grad.astype(BF16)
        gain_ref[...] += jnp.sum(y * xhat, axis=0, keepdims=True)
        grad_att_ref[...] = dot_last(branch_ref[...], w[:, FF:]).astype(BF16)

    @pl.when(i == 4)
    def _():
        finish(two, sem_two)

    @pl.when(i >= 4)
    def _():
        cols = pl.ds(pl.multiple_of((i - 4) * WIDTH, WIDTH), WIDTH)
        part[...] = dot_first(two[...], kept[:, cols]).astype(BF16)
        for b in range(2):
            first = pl.multiple_of((2 * (i - 4) + b) * 48, 48)
            store_blocks(tab, 1, theirs_ref, first, part, slice(b * LANES, (b + 1) * LANES))


def mlp_backward(tab, gathered, pieces, two, act, slope, out_grad, mid, vectors):
    row = clamped(256, WIDTH)
    wide = clamped(256, FF)
    return pl.pallas_call(
        mlp_backward_kernel,
        grid=(6,),
        out_shape=(
            shaped((1024, WIDTH)),
            shaped((1024, WIDTH), F32),
            shaped((1024, WIDTH)),
            shaped((1024, FF)),
            shaped((1024, WIDTH)),
            shaped((1, WIDTH), F32),
            shaped((CHIPS, 192, LANES)),
        ),
        in_specs=[SMEM_SPEC] + [ANY_SPEC] * 6 + [wide, wide, row, row, fixed(16, WIDTH)],
        out_specs=(row, row, row, wide, row, fixed(1, WIDTH), VMEM_SPEC),
        scratch_shapes=[
            pltpu.VMEM((WIDTH, FF + WIDTH), BF16),
            pltpu.VMEM((CHIPS, 2, 192, LANES), BF16),
            pltpu.VMEM((1024, WIDTH), BF16),
            pltpu.VMEM((1024, 4 * LANES), BF16),
            pltpu.VMEM((WIDTH, WIDTH), BF16),
        ]
        + [pltpu.SemaphoreType.DMA] * 3,
        compiler_params=params(),
        cost_estimate=cost(18_000_000_000, 50_000_000),
        name="mlp_backward",
    )(tab, gathered, *pieces, two, act, slope, out_grad, mid, vectors)


def attention_backward_rows(k, qkv_ref, probs_ref, grad_att_ref, grad_qkv_ref):
    low_half = lax.broadcasted_iota(jnp.int32, (128, 128), 1) < HEAD_DIM
    rows = slice(128 * k, 128 * k + 128)

    def heads(ref, base):
        return two_heads(ref[rows, base : base + 128], low_half)

    def probs_of(pair):
        first = 256 * (6 * k + pair)
        return probs_ref[first : first + 256, :]

    grad_probs = []
    for pair in range(6):
        base = pair_base(pair) + 2 * LANES
        grad_probs.append(
            dot_last(heads(grad_att_ref, pair * 128), qkv_ref[rows, base : base + 128])
        )
    grad_scores = []
    for pair in range(6):
        probs = probs_of(pair).astype(F32)
        inner = jnp.sum(probs * grad_probs[pair], axis=-1, keepdims=True)
        grad_scores.append((probs * (grad_probs[pair] - inner)).astype(BF16))
    for pair in range(6):
        base = pair_base(pair)
        grad_query = dot(side_by_side(grad_scores[pair]), heads(qkv_ref, base + LANES))
        grad_key = dot_first(grad_scores[pair], heads(qkv_ref, base))
        grad_value = dot_first(probs_of(pair), heads(grad_att_ref, pair * 128))
        grad_query = (grad_query * HEAD_DIM ** (-0.5)).astype(BF16)
        grad_qkv_ref[rows, base : base + 128] = grad_query
        base = base + LANES
        grad_qkv_ref[rows, base : base + 128] = (grad_key * HEAD_DIM ** (-0.5)).astype(BF16)
        base = base + LANES
        grad_qkv_ref[rows, base : base + 128] = grad_value.astype(BF16)


def attention_grad_rows(tab, side, att, branch, normed, grad_qkv, out_ref, part, out_part):
    lanes = lanes_of(half_of(tab, side), LANES)
    out_part[...] = dot_first(att[...], branch[:, lanes]).astype(BF16)
    store_blocks(tab, side, out_ref, 144, out_part, slice(0, LANES))
    part[...] = dot_first(normed[...], grad_qkv[...]).astype(BF16)
    for sec in range(3):
        store_blocks(tab, side, out_ref, 48 * sec, part, slice(sec * LANES, (sec + 1) * LANES))


def attention_backward_kernel(
    tab, att_hbm, branch_hbm, normed_hbm, qkv_ref, probs_ref, grad_att_ref,
    grad_qkv_ref, theirs_ref,
    att, branch, normed, kept, part, out_part, sem_att, sem_branch, sem_normed,
):
    i = pl.program_id(0)
    fetched = (
        (att_hbm, att, sem_att), (branch_hbm, branch, sem_branch), (normed_hbm, normed, sem_normed)
    )

    @pl.when(i == 0)
    def _():
        for src, dst, sem in fetched:
            pltpu.make_async_copy(src, dst, sem).start()

    @pl.when(i < 4)
    def _():
        for k in range(2):
            attention_backward_rows(k, qkv_ref, probs_ref, grad_att_ref, grad_qkv_ref)
        theirs = pl.ds(pl.multiple_of(half_of(tab, 1) * 3 * LANES, 128), 3 * LANES)
        kept[rows_of(i, 256), :] = grad_qkv_ref[:, theirs]

    @pl.when(i == 4)
    def _():
        for _src, dst, sem in fetched:
            finish(dst, sem)
        attention_grad_rows(tab, 1, att, branch, normed, kept, theirs_ref, part, out_part)


def attention_backward(tab, att, branch, normed, qkv, probs, grad_att):
    wide = clamped(256, 3 * WIDTH)
    return pl.pallas_call(
        attention_backward_kernel,
        grid=(5,),
        out_shape=(shaped((1024, 3 * WIDTH)), shaped((CHIPS, 192, LANES))),
        in_specs=[SMEM_SPEC] + [ANY_SPEC] * 3 + [wide, clamped(12 * 256, 128), clamped(256, WIDTH)],
        out_specs=(wide, VMEM_SPEC),
        scratch_shapes=[pltpu.VMEM((1024, WIDTH), BF16)] * 3
        + [
            pltpu.VMEM((1024, 3 * LANES), BF16),
            pltpu.VMEM((WIDTH, 3 * LANES), BF16),
            pltpu.VMEM((WIDTH, LANES), BF16),
        ]
        + [pltpu.SemaphoreType.DMA] * 3,
        compiler_params=params(),
        cost_estimate=cost(11_000_000_000, 22_000_000),
        name="attention_backward",
    )(tab, att, branch, normed, qkv, probs, grad_att)


def attention_grad_kernel(
    tab, att_ref, branch_ref, normed_ref, grad_qkv_ref, out_ref, part, out_part
):
    attention_grad_rows(
        tab, 0, att_ref, branch_ref, normed_ref, grad_qkv_ref, out_ref, part, out_part
    )


def attention_grad(tab, att, branch, normed, grad_qkv):
    def whole(i, tab):
        return (0, 0)

    rows = pl.BlockSpec((1024, WIDTH), whole)
    chosen = pl.BlockSpec((1024, 3 * LANES), lambda i, tab: (0, half_of(tab, 0)))
    return pl.pallas_call(
        attention_grad_kernel,
        grid_spec=pltpu.PrefetchScalarGridSpec(
            num_scalar_prefetch=1,
            grid=(1,),
            in_specs=[rows, rows, rows, chosen],
            out_specs=VMEM_SPEC,
            scratch_shapes=[
                pltpu.VMEM((WIDTH, 3 * LANES), BF16),
                pltpu.VMEM((WIDTH, LANES), BF16),
            ],
        ),
        out_shape=shaped((CHIPS, 192, LANES)),
        compiler_params=params(),
        cost_estimate=cost(2_600_000_000, 10_000_000),
        name="attention_grad",
    )(tab, att, branch, normed, grad_qkv)


def input_backward_kernel(
    tab, g_a, g_b, g_c, g_d, grad_qkv_ref, x_ref, te_ref, vec_ref, grad_mid_ref, gain_two_ref,
    input_ref, small_ref,
    w, sem,
):
    i = pl.program_id(0)

    @pl.when(i == 0)
    def _():
        fetch_pieces(tab, (g_a, g_b, g_c, g_d), 144, w, sem)
        small_ref[8:9, :] = jnp.zeros((1, WIDTH), F32)
        small_ref[9:10, :] = gain_two_ref[...]
        small_ref[10:16, :] = jnp.zeros((6, WIDTH), F32)
        finish(w, sem)

    y = jnp.zeros((256, WIDTH), F32)
    for half in (0, 1):
        cols = slice(half * 3 * LANES, (half + 1) * 3 * LANES)
        y = y + dot_last(grad_qkv_ref[:, cols], qkv_columns(w, half))
    xhat, scale = ln_stats(add_embed(x_ref[...], te_ref, i))
    grad = grad_mid_ref[...] + ln_back(y, vec_ref[0:1, :], xhat, scale)
    input_ref[...] = grad.astype(BF16)
    for s in range(2):
        small_ref[pl.ds(i * 2 + s, 1), :] = jnp.sum(
            grad[128 * s : 128 * s + 128], axis=0, keepdims=True
        )
    small_ref[8:9, :] += jnp.sum(y * xhat, axis=0, keepdims=True)


def input_backward(tab, pieces, grad_qkv, rows, embed, vectors, grad_mid, gain_two):
    row = tiles(256, WIDTH)
    return pl.pallas_call(
        input_backward_kernel,
        grid=(4,),
        out_shape=(shaped((1024, WIDTH)), shaped((16, WIDTH), F32)),
        in_specs=[SMEM_SPEC]
        + [ANY_SPEC] * 4
        + [tiles(256, 3 * WIDTH), row, fixed(8, WIDTH), fixed(16, WIDTH), row, fixed(1, WIDTH)],
        out_specs=(row, fixed(16, WIDTH)),
        scratch_shapes=[pltpu.VMEM((CHIPS, 2, 144, LANES), BF16), pltpu.SemaphoreType.DMA],
        compiler_params=params(),
        cost_estimate=cost(4_000_000_000, 18_000_000),
        name="input_backward",
    )(tab, *pieces, grad_qkv, rows, embed, vectors, grad_mid, gain_two)


def pick(stacked, index):
    return lax.dynamic_index_in_dim(stacked, index, 0, keepdims=False)


def in_core_order(core, own, other, axis):
    return jnp.where(
        core == 0,
        jnp.concatenate([own, other], axis=axis),
        jnp.concatenate([other, own], axis=axis),
    )


def position_table(chip, core):
    index = jnp.arange(72, dtype=jnp.int32)
    order = jnp.bitwise_xor(core, (index // CHIPS) % 2)
    inner = index % CHIPS
    found = jnp.bitwise_xor(inner, chip)
    value = jnp.where(index < 32, inner, found)
    bits = [(value >> b) & 1 for b in range(4)]
    low = 2 * bits[0] + bits[1]
    straight = low + 4 * bits[2] + 8 * bits[3]
    crossed = low + 8 * bits[2] + 4 * bits[3]
    moved = jnp.where(order == 0, crossed, straight)
    moved = jnp.where(index < 32, jnp.bitwise_xor(moved, chip), moved)
    return jnp.where(index < 64, moved, core)


def swap_halves(halves, core):
    return pick(halves, core), core_swap(pick(halves, 1 - core))


def join_rows(own, other, core, blocks):
    shape = (blocks, own.shape[0] // blocks, LANES)
    return in_core_order(core, own.reshape(shape), other.reshape(shape), 1).reshape(-1, LANES)


def split_rows(piece):
    return piece.reshape(4, 2, 24, LANES).transpose(1, 0, 2, 3).reshape(2, 96, LANES)


def pack_extra(time_in, vectors, ints):
    rows = time_in.shape[0]
    filler = jnp.zeros((rows, 128), BF16)
    vec = lax.dynamic_update_slice(filler, vectors, (0, 0))
    num = lax.dynamic_update_slice(filler, ints[None, :], (0, 0))
    return jnp.concatenate([time_in, vec, num], axis=1)


def split_time(timestep, dataset):
    steps = timestep.reshape(-1)
    return jnp.concatenate([steps // 64, steps % 64, dataset.reshape(-1)]).astype(BF16)


def gather_all(x):
    return lax.all_gather(x, AXES, axis=0, tiled=True)


def shards(
    block_input,
    out_grad,
    timestep,
    dataset,
    lengths,
    norm1_gain,
    qkv_weight,
    out_weight,
    norm2_gain,
    up_weight,
    down_weight,
    time_in,
    time_out,
    data_embed,
    devices,
):
    flat = lax.axis_index(AXES)
    gathered = gather_all(jnp.concatenate([up_weight, out_weight], axis=1))
    exchange = devices == 2 * CHIPS
    vectors = jnp.concatenate([norm1_gain[None], norm2_gain[None], data_embed.T], axis=0)
    numbers = split_time(timestep, dataset)
    count = numbers.shape[0] // 3
    if exchange:
        core = flat & 1
        chip = flat >> 1
        tab = position_table(chip, core)
        wide = qkv_weight.reshape(24, 3, 2, LANES).transpose(2, 1, 0, 3).reshape(2, 72, LANES)
        time_halves = time_out.reshape(16, 2, LANES).transpose(1, 0, 2)
        own, other = swap_halves(jnp.concatenate([wide, time_halves], axis=1), core)
        attention_piece = jnp.concatenate(
            [
                join_rows(own[:72], other[:72], core, 3),
                join_rows(own[72:], other[72:], core, 1),
                pack_extra(time_in, vectors, numbers),
            ],
            axis=0,
        )[None]
        own, other = swap_halves(down_weight.reshape(96, 2, LANES).transpose(1, 0, 2), core)
        down_piece = join_rows(own, other, core, 1)[None]
        held = gather_plane(gather_line(attention_piece))
        far = chip_swap(held, 8)
        attention_pieces = (held, far, core_swap(held), core_swap(far))
        down_near = [chip_swap(after(down_piece, far), p) for p in (1, 2, 3)]
        seen = jnp.concatenate([g[:, 176, 256 : 256 + 3 * count] for g in attention_pieces], axis=0)
    else:
        tab = jnp.concatenate(
            [jnp.tile(jnp.arange(CHIPS, dtype=jnp.int32), 4), jnp.zeros((8,), jnp.int32)]
        )
        full_qkv = gather_all(qkv_weight).reshape(CHIPS, 48, 3, 2, LANES)
        full_down = gather_all(down_weight).reshape(CHIPS, 192, 2, LANES)
        full_tin = gather_all(time_in).reshape(CHIPS, 2, 16, 128)
        full_tout = gather_all(time_out).reshape(CHIPS, 32, 2, LANES)
        full_vec = lax.all_gather(vectors, AXES, axis=1, tiled=True).reshape(4, CHIPS, 2, 24)
        seen = gather_all(numbers[None])
        extra = jnp.zeros((CHIPS, 2, 16, LANES), BF16)
        extra = extra.at[:, :, :, :128].set(full_tin)
        extra = extra.at[:, :, 0:4, 128:152].set(full_vec.transpose(1, 2, 0, 3))
        attention_pieces = []
        down_pieces = []
        for half in (0, 1):
            wide = full_qkv[:, :, :, half].transpose(0, 2, 1, 3).reshape(CHIPS, 144, LANES)
            whole = jnp.concatenate([wide, full_tout[:, :, half], extra[:, half]], axis=1)
            attention_pieces += [whole[:8], whole[8:]]
            down_pieces += [full_down[:8, :, half], full_down[8:, :, half]]

    micros, seqs, seq_len, width = block_input.shape
    tokens = micros * seqs * seq_len
    x_rows = block_input.reshape(tokens, width)
    grad_rows = out_grad.reshape(tokens, width)
    features = sinusoid(timestep.reshape(-1), time_in.shape[1] // 2).astype(BF16)
    sets = dataset.reshape(-1, 1).astype(F32)
    normed, qkv, embed, vecs = qkv_forward(tab, attention_pieces, x_rows, features, sets)
    if exchange:
        down_line = jnp.concatenate([down_piece] + [after(x, embed) for x in down_near], axis=0)
        qkv = after(qkv, down_line)
        down_plane = chip_swap(down_line, 4)
    probs, att = attention(lengths.reshape(-1), qkv)
    if exchange:
        down_held = jnp.concatenate([down_line, after(down_plane, att)], axis=0)
        att = after(att, down_held)
        down_far = chip_swap(down_held, 8)
    mid, two, act, slope = up_forward(gathered, att, x_rows, embed, vecs)
    if exchange:
        down_far = after(down_far, two)
        act = after(act, down_far)
        down_pieces = (down_held, down_far, core_swap(down_held), core_swap(down_far))
    down_sum = down_grad(act, grad_rows)
    grad_down = lax.psum_scatter(down_sum, AXES, scatter_dimension=0, tiled=True)
    slope = after(slope, down_sum)

    def backward(slope):
        result, grad_mid, branch, grad_up, grad_att, gain_two, up_theirs = mlp_backward(
            tab, gathered, down_pieces, two, act, slope, grad_rows, mid, vecs
        )
        up_mine = up_grad(tab, two, grad_up)
        if exchange:
            up_sum = Scatter(up_theirs)
            up_sum.parts.append(up_mine)
            grad_att = after(grad_att, *up_sum.send())
        grad_qkv, att_theirs = attention_backward(tab, att, branch, normed, qkv, probs, grad_att)
        if exchange:
            att_sum = Scatter(att_theirs)
            grad_qkv = after(grad_qkv, *up_sum.step(att_theirs))
        att_mine = attention_grad(tab, att, branch, normed, grad_qkv)
        if exchange:
            att_sum.parts.append(att_mine)
            grad_qkv = after(grad_qkv, *att_sum.send(), *up_sum.step(att_mine))
        grad_input, small = input_backward(
            tab, attention_pieces, grad_qkv, x_rows, embed, vecs, grad_mid, gain_two
        )

        small = small.astype(BF16)[None]
        if exchange:
            small_line = gather_line(after(small, *att_sum.step(small)))
            small_line = after(small_line, *att_sum.step(small_line))
            held = gather_plane(small_line)
            far = chip_swap(held, 8)
            every = jnp.concatenate([held, far, core_swap(held), core_swap(far)], axis=0)
        else:
            every = gather_all(small)
        every = every.reshape(devices * 16, width)
        steps = seen[:, :count] * 64 + seen[:, count : 2 * count].astype(F32)
        wave = sinusoid(steps.reshape(-1), time_in.shape[1] // 2).astype(BF16)
        wave = jnp.pad(wave.reshape(devices, count, -1), ((0, 0), (0, 16 - count), (0, 0)))
        wave = wave.reshape(devices * 16, -1)
        which = jnp.pad(seen[:, 2 * count :], ((0, 0), (0, 16 - count))).reshape(-1)
        place = jnp.tile(jnp.arange(16), devices)
        hot = jnp.stack(
            [(place < count) & (which == 0), (place < count) & (which == 1), place == 8, place == 9]
        ).astype(BF16)
        pre = dot_last(wave, time_in)
        gate = 1.0 / (1.0 + jnp.exp(-pre))
        hidden = (pre * gate).astype(BF16)
        grad_tout = dot_first(hidden, every)
        grad_pre = dot_last(every, time_out) * (gate * (1.0 + pre * (1.0 - gate)))
        grad_tin = dot_first(grad_pre.astype(BF16), wave)
        sums = dot(hot, every)
        own_cols = norm1_gain.shape[0]
        sums = lax.dynamic_slice_in_dim(sums, flat * own_cols, own_cols, 1)

        if exchange:
            piece = up_sum.total()
            own, other = swap_halves(split_rows(piece), core)
            both = in_core_order(core, own.reshape(4, 24, LANES), other.reshape(4, 24, LANES), 0)
            grad_up_weight = both.transpose(1, 0, 2).reshape(24, FF)
            piece = att_sum.total()
            own, other = swap_halves(split_rows(piece), core)
            both = in_core_order(core, own.reshape(4, 1, 24, LANES), other.reshape(4, 1, 24, LANES), 1)
            both = both.transpose(2, 0, 1, 3).reshape(24, 4 * WIDTH)
        else:
            scatter = partial(lax.psum_scatter, axis_name=AXES, scatter_dimension=0, tiled=True)
            both = jnp.stack([up_mine, up_theirs]).astype(F32).reshape(2, CHIPS, 4, 48, LANES)
            grad_up_weight = scatter(both.transpose(1, 3, 0, 2, 4).reshape(WIDTH, FF))
            both = jnp.stack([att_mine, att_theirs]).astype(F32).reshape(2, CHIPS, 4, 48, LANES)
            both = scatter(both.transpose(1, 3, 2, 0, 4).reshape(WIDTH, 4 * WIDTH))
        return (
            result.reshape(block_input.shape),
            grad_input.reshape(block_input.shape),
            sums[2],
            both[:, : 3 * WIDTH],
            both[:, 3 * WIDTH :],
            sums[3],
            grad_up_weight,
            grad_tin,
            grad_tout,
            sums[:2].T,
        )

    shapes = jax.eval_shape(backward, slope)
    done = lax.cond(
        flat < devices,
        backward,
        lambda _: jax.tree.map(lambda x: jnp.zeros(x.shape, x.dtype), shapes),
        slope,
    )
    return done[:7] + (grad_down.astype(F32),) + done[7:]


def solution(mesh):
    devices = mesh.shape["dp"] * mesh.shape["fsdp"]
    seq_spec = P(None, AXES, None, None)
    int_spec = P(None, AXES)
    row_spec = P(AXES, None)
    in_specs = (seq_spec, seq_spec, int_spec, int_spec, int_spec, P(AXES), row_spec, row_spec, P(AXES))
    in_specs = in_specs + (row_spec,) * 5
    out_specs = (seq_spec, seq_spec, P(AXES), row_spec, row_spec, P(AXES)) + (row_spec,) * 5
    return jax.shard_map(
        partial(shards, devices=devices),
        mesh=mesh,
        in_specs=in_specs,
        out_specs=out_specs,
        check_vma=False,
    )
```

```python
from functools import partial
import math

import jax
import jax.numpy as jnp
from jax import lax
from jax.experimental import pallas as pl
from jax.experimental.pallas import tpu as pltpu
from jax.sharding import PartitionSpec as P

HEAD_DIM = 64
AXES = ("dp", "fsdp")
LANES = 384
CHIPS = 16
WIDTH = 768
FF = 3072
F32 = jnp.float32
BF16 = jnp.bfloat16
NEG = -1000000000.0


def sinusoid(timestep, half_width):
    frequency = jnp.exp(-math.log(10000.0) * jnp.arange(half_width, dtype=F32) / half_width)
    angles = timestep.astype(F32)[:, None] * frequency[None, :]
    return jnp.concatenate([jnp.cos(angles), jnp.sin(angles)], axis=-1)


def dot(left, right):
    return jnp.dot(left, right, preferred_element_type=F32)


def dot_last(left, right):
    return lax.dot_general(left, right, (((1,), (1,)), ((), ())), preferred_element_type=F32)


def dot_first(left, right):
    return lax.dot_general(left, right, (((0,), (0,)), ((), ())), preferred_element_type=F32)


def positions(masks):
    return [sum(masks[b] for b in range(4) if (p >> b) & 1) for p in range(CHIPS)]


LINE_FIRST = ((2, 1, 8, 4), (2, 1, 4, 8))
LINE_LATER = ((8, 2, 1, 4), (4, 2, 1, 8))


def core_swap(x):
    return lax.ppermute(x, AXES, [(i, i ^ 1) for i in range(2 * CHIPS)])


def chip_swap(x, position, order=LINE_FIRST):
    far = [positions(masks)[position] * 2 for masks in order]
    return lax.ppermute(x, AXES, [(i, i ^ far[i & 1]) for i in range(2 * CHIPS)])


def after(x, *others):
    return lax.optimization_barrier((x,) + others)[0]


def gather_line(piece):
    return jnp.concatenate([piece] + [chip_swap(piece, p) for p in (1, 2, 3)], axis=0)


def gather_plane(held):
    return jnp.concatenate([held, chip_swap(held, 4)], axis=0)


def together(outs, arrivals):
    return lax.optimization_barrier((outs, arrivals))


class Scatter:
    def __init__(self, theirs):
        self.parts = []
        self.steps = [(8,), (4,), (1, 2, 3)]
        self.theirs = theirs

    def swap(self):
        return [core_swap(self.theirs)]

    def land(self, brought, *own):
        self.parts += [*brought, *own]

    def sum(self, start, stop):
        total = self.parts[0][start:stop].astype(F32)
        for part in self.parts[1:]:
            total = total + part[start:stop].astype(F32)
        return total

    def send(self):
        self.at = self.steps.pop(0)
        size = 1 if len(self.at) == 3 else self.at[0]
        self.sent = [self.sum(p, p + size).astype(BF16) for p in self.at]
        return self.sent

    def fly(self):
        return [chip_swap(x, p) for x, p in zip(self.sent, self.at)]

    def total(self):
        return self.sum(0, 1)[0]


VMEM_SPEC = pl.BlockSpec(memory_space=pltpu.VMEM)
SMEM_SPEC = pl.BlockSpec(memory_space=pltpu.SMEM)
ANY_SPEC = pl.BlockSpec(memory_space=pl.ANY)


def tiles(rows, cols):
    return pl.BlockSpec((rows, cols), lambda i: (i, 0))


def columns(rows, cols):
    return pl.BlockSpec((rows, cols), lambda i: (0, i))


def fixed(*shape):
    return pl.BlockSpec(shape, lambda i: (0,) * len(shape))


def shaped(shape, dtype=BF16):
    return pltpu.HBM(shape, dtype)


def params(mib):
    return pltpu.CompilerParams(vmem_limit_bytes=mib * 1024 * 1024)


def kernel_call(*args, **kwargs):
    call = pl.pallas_call(*args, **kwargs)

    def run(*operands):
        return call(
            *[
                x
                if x.dtype == jnp.int32
                else pltpu.with_memory_space_constraint(x, pltpu.HBM)
                for x in operands
            ]
        )

    return run


def cost(flops, nbytes, transcendentals=0):
    return pl.CostEstimate(flops=flops, bytes_accessed=nbytes, transcendentals=transcendentals)


def ln_stats(v):
    center = v - jnp.mean(v, axis=-1, keepdims=True)
    scale = lax.rsqrt(jnp.mean(center * center, axis=-1, keepdims=True) + 1e-05)
    return center * scale, scale


def ln_back(y, gain, xhat, scale):
    yg = y * gain
    return scale * (
        yg - jnp.mean(yg, axis=-1, keepdims=True) - xhat * jnp.mean(yg * xhat, axis=-1, keepdims=True)
    )


def first_core(tab):
    return tab[64]


def each_piece(tab, parts, fn):
    core = first_core(tab)
    for side in (0, 1):
        half = core if side == 0 else 1 - core
        for group in (0, 1):
            part = parts[side * 2 + group]

            def body(q, _, part=part, side=side, group=group, half=half):
                chip = tab[side * CHIPS + group * 8 + q]
                fn(part.at[q], chip, half)
                return 0

            lax.fori_loop(0, 8, body, 0)


def rows_of(chip, size):
    return pl.ds(pl.multiple_of(chip * size, size), size)


def lanes_of(half, size, base=0):
    return pl.ds(pl.multiple_of(half * size + base, 128), LANES)


def fetch_pieces(tab, parts, rows, dst, sem):
    each_piece(
        tab,
        parts,
        lambda src, chip, half: pltpu.make_async_copy(
            src.at[pl.ds(0, rows), :], dst.at[chip, half], sem
        ).start(),
    )


def block(pieces, half, first, rows=48):
    return pieces[:, half, first : first + rows, :].reshape(CHIPS * rows, LANES)


def both_halves(pieces, first, rows=48):
    return jnp.concatenate([block(pieces, h, first, rows) for h in (0, 1)], axis=1)


def down_rows(pieces, j):
    return jnp.concatenate(
        [pieces[4 * j : 4 * j + 4, h].reshape(WIDTH, LANES) for h in (0, 1)], axis=1
    )


def qkv_columns(pieces, half):
    return jnp.concatenate([block(pieces, half, 48 * sec) for sec in range(3)], axis=1)


def finish(ref, sem):
    pltpu.make_async_copy(ref, ref, sem).wait()


def add_embed(x, embed, i):
    seqs = x.shape[0] // 128
    parts = [
        x[128 * k : 128 * k + 128].astype(F32) + embed[pl.ds(i * seqs + k, 1), :]
        for k in range(seqs)
    ]
    return jnp.concatenate(parts, axis=0)


def two_heads(x, low_half):
    none = jnp.zeros_like(x)
    return jnp.concatenate([jnp.where(low_half, x, none), jnp.where(low_half, none, x)], axis=0)


def side_by_side(x):
    return jnp.concatenate([x[:128], x[128:]], axis=1)


def pair_base(pair):
    return (pair // 3) * 3 * LANES + (pair % 3) * 128


def attention_rows(k, length, qkv_ref, probs_ref, att_ref):
    low_half = lax.broadcasted_iota(jnp.int32, (128, 128), 1) < HEAD_DIM
    keep = lax.broadcasted_iota(jnp.int32, (256, 128), 1) < length
    rows = slice(128 * k, 128 * k + 128)
    scores = []
    for pair in range(6):
        base = pair_base(pair)
        query = two_heads(qkv_ref[rows, base : base + 128], low_half)
        key = qkv_ref[rows, base + LANES : base + LANES + 128]
        scores.append(jnp.where(keep, dot_last(query, key) * HEAD_DIM ** (-0.5), NEG))
    probs = []
    for pair in range(6):
        shifted = jnp.exp(scores[pair] - jnp.max(scores[pair], axis=-1, keepdims=True))
        total = jnp.sum(shifted, axis=-1, keepdims=True)
        probs.append((shifted * (1.0 / total)).astype(BF16))
        first = 256 * (6 * k + pair)
        probs_ref[first : first + 256, :] = probs[pair]
    for pair in range(6):
        base = pair_base(pair) + 2 * LANES
        value = two_heads(qkv_ref[rows, base : base + 128], low_half)
        att_ref[rows, pair * 128 : pair * 128 + 128] = dot(
            side_by_side(probs[pair]), value
        ).astype(BF16)


def attention_kernel(
    tab, lens, sets, g_a, g_b, g_c, g_d, x_ref, feat_ref,
    normed_ref, qkv_ref, te_ref, vec_ref, seen_ref, probs_ref, att_ref,
    w, sem,
):
    i = pl.program_id(0)

    @pl.when(i == 0)
    def _():
        fetch_pieces(tab, (g_a, g_b, g_c, g_d), 192, w, sem)
        finish(w, sem)
        lane = lax.broadcasted_iota(jnp.int32, (128, WIDTH), 1)
        spread = (lax.broadcasted_iota(jnp.int32, (128, WIDTH), 0) == lane % 24).astype(BF16)
        vectors = jnp.zeros((16, WIDTH), F32)
        embed = jnp.zeros((8, WIDTH), F32)
        for owner in (0, 1):
            extra = block(w, owner, 176, 16)
            wide = dot(extra[:, 128:256], spread)
            chip = lax.broadcasted_iota(jnp.int32, (256, WIDTH), 0) // 16
            place = lax.broadcasted_iota(jnp.int32, (256, WIDTH), 1) // 24
            wide = jnp.where(place == chip * 2 + owner, wide, 0.0)
            vectors = vectors + jnp.sum(wide.reshape(CHIPS, 16, WIDTH), axis=0)
            pre = dot_last(feat_ref[...], extra[:, 0:128])
            hidden = (pre / (1.0 + jnp.exp(-pre))).astype(BF16)
            embed = embed + dot(hidden, both_halves(w, 144 + 16 * owner, 16))
            seen_ref[owner] = w[:, owner, 176:192, 256:]
        vec_ref[...] = vectors
        for s in range(8):
            chosen = jnp.where(sets[s // 4, s % 4] == 1, vectors[3:4, :], vectors[2:3, :])
            te_ref[s : s + 1, :] = embed[s : s + 1, :] + chosen

    xhat, _unused = ln_stats(add_embed(x_ref[...], te_ref, i))
    normed_ref[...] = (xhat * vec_ref[0:1, :]).astype(BF16)
    for half in (0, 1):
        cols = slice(half * 3 * LANES, (half + 1) * 3 * LANES)
        qkv_ref[:, cols] = dot(normed_ref[...], qkv_columns(w, half)).astype(BF16)
    for k in range(2):
        attention_rows(k, lens[i // 2, i % 2 * 2 + k], qkv_ref, probs_ref, att_ref)


def attention_forward(tab, lens, sets, pieces, rows, features):
    row = tiles(256, WIDTH)
    return kernel_call(
        attention_kernel,
        grid=(4,),
        out_shape=(
            shaped((1024, WIDTH)),
            shaped((1024, 3 * WIDTH)),
            shaped((8, WIDTH), F32),
            shaped((16, WIDTH), F32),
            shaped((2, CHIPS, 16, 128)),
            shaped((48 * 256, 128)),
            shaped((1024, WIDTH)),
        ),
        in_specs=[SMEM_SPEC] * 3 + [ANY_SPEC] * 4 + [row, fixed(8, 128)],
        out_specs=(
            row, tiles(256, 3 * WIDTH), fixed(8, WIDTH), fixed(16, WIDTH),
            fixed(2, CHIPS, 16, 128), tiles(12 * 256, 128), row,
        ),
        scratch_shapes=[pltpu.VMEM((CHIPS, 2, 192, LANES), BF16), pltpu.SemaphoreType.DMA],
        compiler_params=params(26),
        cost_estimate=cost(8_000_000_000, 20_000_000, 1_600_000),
        name="attention_forward",
    )(tab, lens, sets, *pieces, rows, features)


def gelu_parts(u):
    cdf = 0.5 + 0.5 * lax.erf(u * math.sqrt(0.5))
    return cdf, jnp.exp(u * u * -0.5) * (1.0 / math.sqrt(2.0 * math.pi))


def up_columns(pieces, j):
    first = 96 * (j % 2)
    return jnp.concatenate(
        [block(pieces, j // 2, first), block(pieces, j // 2, first + 48)], axis=1
    )


def half_of(tab, side):
    return first_core(tab) if side == 0 else 1 - first_core(tab)


def clamped(rows, cols):
    return pl.BlockSpec((rows, cols), lambda i: (jnp.minimum(i, 3), 0))


def down_grad_rows(tab, side, j, act, out_grad, out_ref):
    lanes = lanes_of(half_of(tab, side), LANES)
    grad = dot_first(act, out_grad[:, lanes]).astype(BF16)
    for k in range(4):
        place = tab[32 + side * CHIPS + j * 4 + k]
        out_ref[place, :, :] = grad[192 * k : 192 * k + 192, :]


def up_kernel(
    tab, u_a, u_b, u_c, u_d, out_grad_hbm, att_ref, x_ref, te_ref, vec_ref,
    mid_ref, two_ref, act_ref, slope_ref, theirs_ref,
    w, out_grad, kept, sem, sem_out_grad,
):
    i = pl.program_id(0)

    @pl.when(i == 0)
    def _():
        fetch_pieces(tab, (u_a, u_b, u_c, u_d), 240, w, sem)
        finish(w, sem)
        pltpu.make_async_copy(out_grad_hbm, out_grad, sem_out_grad).start()

    @pl.when(i < 4)
    def _():
        mid = add_embed(x_ref[...], te_ref, i) + dot(att_ref[...], both_halves(w, 192))
        mid_ref[...] = mid
        xhat, _unused = ln_stats(mid)
        two_ref[...] = (xhat * vec_ref[1:2, :]).astype(BF16)
        for j in range(4):
            cols = slice(j * WIDTH, (j + 1) * WIDTH)
            up = dot(two_ref[...], up_columns(w, j))
            cdf, density = gelu_parts(up)
            activated = (up * cdf).astype(BF16)
            act_ref[:, cols] = activated
            kept[j, rows_of(i, 256), :] = activated
            slope_ref[:, cols] = (cdf + up * density).astype(BF16)

    @pl.when(i == 4)
    def _():
        finish(out_grad, sem_out_grad)

    @pl.when(i >= 4)
    def _():
        down_grad_rows(tab, 1, i - 4, kept[i - 4], out_grad, theirs_ref)


def up_forward(tab, pieces, att, rows, out_grad, embed, vectors):
    row = clamped(256, WIDTH)
    wide = clamped(256, FF)
    return kernel_call(
        up_kernel,
        grid=(8,),
        out_shape=(
            shaped((1024, WIDTH), F32),
            shaped((1024, WIDTH)),
            shaped((1024, FF)),
            shaped((1024, FF)),
            pltpu.VMEM((CHIPS, 192, LANES), BF16),
        ),
        in_specs=[SMEM_SPEC] + [ANY_SPEC] * 5 + [row, row, fixed(8, WIDTH), fixed(16, WIDTH)],
        out_specs=(row, row, wide, wide, VMEM_SPEC),
        scratch_shapes=[
            pltpu.VMEM((CHIPS, 2, 240, LANES), BF16),
            pltpu.VMEM((1024, WIDTH), BF16),
            pltpu.VMEM((4, 1024, WIDTH), BF16),
            pltpu.SemaphoreType.DMA,
            pltpu.SemaphoreType.DMA,
        ],
        compiler_params=params(38),
        cost_estimate=cost(10_000_000_000, 30_000_000, 6_000_000),
        name="up_forward",
    )(tab, *pieces, out_grad, att, rows, embed, vectors)


def down_grad_kernel(tab, act_ref, out_grad_ref, out_ref):
    down_grad_rows(tab, 0, pl.program_id(0), act_ref[...], out_grad_ref, out_ref)


def down_grad(tab, act, out_grad):
    return kernel_call(
        down_grad_kernel,
        grid=(4,),
        out_shape=pltpu.VMEM((CHIPS, 192, LANES), BF16),
        in_specs=[SMEM_SPEC, columns(1024, WIDTH), fixed(1024, WIDTH)],
        out_specs=VMEM_SPEC,
        compiler_params=params(18),
        cost_estimate=cost(3_000_000_000, 10_000_000),
        name="down_grad",
    )(tab, act, out_grad)


def store_blocks(tab, side, target, first, part, lanes):
    for chip in range(CHIPS):
        place = tab[32 + side * CHIPS + chip]
        target[place, pl.ds(first, 48), :] = part[48 * chip : 48 * chip + 48, lanes]


def out_grad_rows(tab, side, att, branch, out_ref, part):
    lanes = lanes_of(half_of(tab, side), LANES)
    part[:, 0:LANES] = dot_first(att[...], branch[:, lanes]).astype(BF16)
    store_blocks(tab, side, out_ref, 192, part, slice(0, LANES))


def up_grad_rows(tab, side, j, two, grad_up, out_ref, part):
    part[...] = dot_first(two, grad_up).astype(BF16)
    for b in range(2):
        first = pl.multiple_of((2 * j + b) * 48, 48)
        store_blocks(tab, side, out_ref, first, part, slice(b * LANES, (b + 1) * LANES))


def up_grad_kernel(
    tab, att_hbm, branch_hbm, two_ref, grad_up_ref, out_ref,
    att, branch, part, sem_att, sem_branch,
):
    j = pl.program_id(0)

    @pl.when(j == 0)
    def _():
        pltpu.make_async_copy(att_hbm, att, sem_att).start()
        pltpu.make_async_copy(branch_hbm, branch, sem_branch).start()

    @pl.when(j < 2)
    def _():
        up_grad_rows(tab, 0, j, two_ref[...], grad_up_ref[...], out_ref, part)

    @pl.when(j == 2)
    def _():
        finish(att, sem_att)
        finish(branch, sem_branch)
        out_grad_rows(tab, 0, att, branch, out_ref, part)


def up_grad(tab, att, branch, two, grad_up):
    return kernel_call(
        up_grad_kernel,
        grid_spec=pltpu.PrefetchScalarGridSpec(
            num_scalar_prefetch=1,
            grid=(3,),
            in_specs=[
                ANY_SPEC,
                ANY_SPEC,
                pl.BlockSpec((1024, WIDTH), lambda j, tab: (0, 0)),
                pl.BlockSpec(
                    (1024, WIDTH), lambda j, tab: (0, half_of(tab, 0) * 2 + jnp.minimum(j, 1))
                ),
            ],
            out_specs=VMEM_SPEC,
            scratch_shapes=[pltpu.VMEM((1024, WIDTH), BF16)] * 2
            + [pltpu.VMEM((WIDTH, WIDTH), BF16)]
            + [pltpu.SemaphoreType.DMA] * 2,
        ),
        out_shape=pltpu.VMEM((CHIPS, 240, LANES), BF16),
        compiler_params=params(22),
        cost_estimate=cost(3_200_000_000, 11_000_000),
        name="up_grad",
    )(tab, att, branch, two, grad_up)


def mlp_backward_kernel(
    tab, down_tab, u_a, u_b, u_c, u_d, d_a, d_b, d_c, d_d, two_hbm, att_hbm,
    slope_ref, out_grad_ref, mid_ref, vec_ref,
    grad_mid_ref, branch_ref, grad_up_ref, grad_att_ref, gain_ref, theirs_ref,
    w, w_down, two, att, kept, kept_branch, part, sem, sem_down, sem_two, sem_att,
):
    i = pl.program_id(0)

    @pl.when(i == 0)
    def _():
        fetch_pieces(down_tab, (d_a, d_b, d_c, d_d), 192, w_down, sem_down)
        gain_ref[...] = jnp.zeros_like(gain_ref)
        finish(w_down, sem_down)
        fetch_pieces(tab, (u_a, u_b, u_c, u_d), 240, w, sem)
        pltpu.make_async_copy(two_hbm, two, sem_two).start()
        pltpu.make_async_copy(att_hbm, att, sem_att).start()

    @pl.when(i < 4)
    def _():
        for j in range(4):
            cols = slice(j * WIDTH, (j + 1) * WIDTH)
            grad_act = dot_last(out_grad_ref[...], down_rows(w_down, j))
            grad_up_ref[:, cols] = (grad_act * slope_ref[:, cols].astype(F32)).astype(BF16)

        @pl.when(i == 0)
        def _():
            finish(w, sem)

        y = jnp.zeros((256, WIDTH), F32)
        for j in range(4):
            cols = slice(j * WIDTH, (j + 1) * WIDTH)
            y = y + dot_last(grad_up_ref[:, cols], up_columns(w, j))
        theirs = pl.ds(pl.multiple_of(half_of(tab, 1) * 4 * LANES, 128), 4 * LANES)
        kept[rows_of(i, 256), :] = grad_up_ref[:, theirs]
        xhat, scale = ln_stats(mid_ref[...])
        grad = out_grad_ref[...].astype(F32) + ln_back(y, vec_ref[1:2, :], xhat, scale)
        grad_mid_ref[...] = grad
        branch_ref[...] = grad.astype(BF16)
        kept_branch[rows_of(i, 256), :] = branch_ref[...]
        gain_ref[...] += jnp.sum(y * xhat, axis=0, keepdims=True)
        grad_att_ref[...] = dot_last(branch_ref[...], both_halves(w, 192)).astype(BF16)

    @pl.when(i == 4)
    def _():
        finish(two, sem_two)
        finish(att, sem_att)
        out_grad_rows(tab, 1, att, kept_branch, theirs_ref, part)

    @pl.when(i >= 4)
    def _():
        cols = pl.ds(pl.multiple_of((i - 4) * WIDTH, WIDTH), WIDTH)
        up_grad_rows(tab, 1, i - 4, two[...], kept[:, cols], theirs_ref, part)


def mlp_backward(tab, down_tab, up_pieces, down_pieces, two, att, slope, out_grad, mid, vectors):
    row = clamped(256, WIDTH)
    wide = clamped(256, FF)
    return kernel_call(
        mlp_backward_kernel,
        grid=(6,),
        out_shape=(
            shaped((1024, WIDTH), F32),
            shaped((1024, WIDTH)),
            shaped((1024, FF)),
            shaped((1024, WIDTH)),
            shaped((1, WIDTH), F32),
            pltpu.VMEM((CHIPS, 240, LANES), BF16),
        ),
        in_specs=[SMEM_SPEC] * 2 + [ANY_SPEC] * 10 + [wide, row, row, fixed(16, WIDTH)],
        out_specs=(row, row, wide, row, fixed(1, WIDTH), VMEM_SPEC),
        scratch_shapes=[
            pltpu.VMEM((CHIPS, 2, 240, LANES), BF16),
            pltpu.VMEM((CHIPS, 2, 192, LANES), BF16),
            pltpu.VMEM((1024, WIDTH), BF16),
            pltpu.VMEM((1024, WIDTH), BF16),
            pltpu.VMEM((1024, 4 * LANES), BF16),
            pltpu.VMEM((1024, WIDTH), BF16),
            pltpu.VMEM((WIDTH, WIDTH), BF16),
        ]
        + [pltpu.SemaphoreType.DMA] * 4,
        compiler_params=params(46),
        cost_estimate=cost(18_000_000_000, 50_000_000),
        name="mlp_backward",
    )(tab, down_tab, *up_pieces, *down_pieces, two, att, slope, out_grad, mid, vectors)


def result_kernel(tab, d_a, d_b, d_c, d_d, act_ref, mid_ref, result_ref, w_down, sem):
    @pl.when(pl.program_id(0) == 0)
    def _():
        fetch_pieces(tab, (d_a, d_b, d_c, d_d), 192, w_down, sem)
        finish(w_down, sem)

    total = mid_ref[...]
    for j in range(4):
        total = total + dot(act_ref[:, j * WIDTH : (j + 1) * WIDTH], down_rows(w_down, j))
    result_ref[...] = total.astype(BF16)


def block_result(tab, pieces, act, mid):
    row = tiles(256, WIDTH)
    return kernel_call(
        result_kernel,
        grid=(4,),
        out_shape=shaped((1024, WIDTH)),
        in_specs=[SMEM_SPEC] + [ANY_SPEC] * 4 + [tiles(256, FF), row],
        out_specs=row,
        scratch_shapes=[pltpu.VMEM((CHIPS, 2, 192, LANES), BF16), pltpu.SemaphoreType.DMA],
        compiler_params=params(22),
        cost_estimate=cost(5_000_000_000, 16_000_000),
        name="block_result",
    )(tab, *pieces, act, mid)


def attention_backward_rows(k, qkv_ref, probs_ref, grad_att_ref, grad_qkv_ref):
    low_half = lax.broadcasted_iota(jnp.int32, (128, 128), 1) < HEAD_DIM
    rows = slice(128 * k, 128 * k + 128)

    def heads(ref, base):
        return two_heads(ref[rows, base : base + 128], low_half)

    def probs_of(pair):
        first = 256 * (6 * k + pair)
        return probs_ref[first : first + 256, :]

    grad_probs = []
    for pair in range(6):
        base = pair_base(pair) + 2 * LANES
        grad_probs.append(
            dot_last(heads(grad_att_ref, pair * 128), qkv_ref[rows, base : base + 128])
        )
    grad_scores = []
    for pair in range(6):
        probs = probs_of(pair).astype(F32)
        inner = jnp.sum(probs * grad_probs[pair], axis=-1, keepdims=True)
        grad_scores.append((probs * (grad_probs[pair] - inner)).astype(BF16))
    for pair in range(6):
        base = pair_base(pair)
        grad_query = dot(side_by_side(grad_scores[pair]), heads(qkv_ref, base + LANES))
        grad_key = dot_first(grad_scores[pair], heads(qkv_ref, base))
        grad_value = dot_first(probs_of(pair), heads(grad_att_ref, pair * 128))
        grad_query = (grad_query * HEAD_DIM ** (-0.5)).astype(BF16)
        grad_qkv_ref[rows, base : base + 128] = grad_query
        base = base + LANES
        grad_qkv_ref[rows, base : base + 128] = (grad_key * HEAD_DIM ** (-0.5)).astype(BF16)
        base = base + LANES
        grad_qkv_ref[rows, base : base + 128] = grad_value.astype(BF16)


def qkv_grad_rows(tab, side, normed, grad_qkv, out_ref, part):
    part[...] = dot_first(normed, grad_qkv).astype(BF16)
    for sec in range(3):
        store_blocks(tab, side, out_ref, 48 * sec, part, slice(sec * LANES, (sec + 1) * LANES))


def attention_backward_kernel(
    tab, normed_hbm, qkv_ref, probs_ref, grad_att_ref, grad_qkv_ref, theirs_ref,
    normed, kept, part, sem,
):
    i = pl.program_id(0)

    @pl.when(i == 0)
    def _():
        pltpu.make_async_copy(normed_hbm, normed, sem).start()

    @pl.when(i < 4)
    def _():
        for k in range(2):
            attention_backward_rows(k, qkv_ref, probs_ref, grad_att_ref, grad_qkv_ref)
        theirs = pl.ds(pl.multiple_of(half_of(tab, 1) * 3 * LANES, 128), 3 * LANES)
        kept[rows_of(i, 256), :] = grad_qkv_ref[:, theirs]

    @pl.when(i == 4)
    def _():
        finish(normed, sem)
        qkv_grad_rows(tab, 1, normed[...], kept[...], theirs_ref, part)


def attention_backward(tab, normed, qkv, probs, grad_att):
    wide = clamped(256, 3 * WIDTH)
    return kernel_call(
        attention_backward_kernel,
        grid=(5,),
        out_shape=(shaped((1024, 3 * WIDTH)), pltpu.VMEM((CHIPS, 144, LANES), BF16)),
        in_specs=[SMEM_SPEC, ANY_SPEC, wide, clamped(12 * 256, 128), clamped(256, WIDTH)],
        out_specs=(wide, VMEM_SPEC),
        scratch_shapes=[
            pltpu.VMEM((1024, WIDTH), BF16),
            pltpu.VMEM((1024, 3 * LANES), BF16),
            pltpu.VMEM((WIDTH, 3 * LANES), BF16),
            pltpu.SemaphoreType.DMA,
        ],
        compiler_params=params(28),
        cost_estimate=cost(11_000_000_000, 22_000_000),
        name="attention_backward",
    )(tab, normed, qkv, probs, grad_att)


def qkv_grad_kernel(tab, normed_ref, grad_qkv_ref, out_ref, part):
    qkv_grad_rows(tab, 0, normed_ref[...], grad_qkv_ref[...], out_ref, part)


def qkv_grad(tab, normed, grad_qkv):
    return kernel_call(
        qkv_grad_kernel,
        grid_spec=pltpu.PrefetchScalarGridSpec(
            num_scalar_prefetch=1,
            grid=(1,),
            in_specs=[
                pl.BlockSpec((1024, WIDTH), lambda i, tab: (0, 0)),
                pl.BlockSpec((1024, 3 * LANES), lambda i, tab: (0, half_of(tab, 0))),
            ],
            out_specs=VMEM_SPEC,
            scratch_shapes=[pltpu.VMEM((WIDTH, 3 * LANES), BF16)],
        ),
        out_shape=pltpu.VMEM((CHIPS, 144, LANES), BF16),
        compiler_params=params(22),
        cost_estimate=cost(2_000_000_000, 7_000_000),
        name="qkv_grad",
    )(tab, normed, grad_qkv)


def input_backward_kernel(
    tab, g_a, g_b, g_c, g_d, grad_qkv_ref, x_ref, te_ref, vec_ref, grad_mid_ref, gain_two_ref,
    input_ref, small_ref,
    w, sem,
):
    i = pl.program_id(0)

    @pl.when(i == 0)
    def _():
        fetch_pieces(tab, (g_a, g_b, g_c, g_d), 144, w, sem)
        small_ref[8:9, :] = jnp.zeros((1, WIDTH), F32)
        small_ref[9:10, :] = gain_two_ref[...]
        small_ref[10:16, :] = jnp.zeros((6, WIDTH), F32)
        finish(w, sem)

    y = jnp.zeros((256, WIDTH), F32)
    for half in (0, 1):
        cols = slice(half * 3 * LANES, (half + 1) * 3 * LANES)
        y = y + dot_last(grad_qkv_ref[:, cols], qkv_columns(w, half))
    xhat, scale = ln_stats(add_embed(x_ref[...], te_ref, i))
    grad = grad_mid_ref[...] + ln_back(y, vec_ref[0:1, :], xhat, scale)
    input_ref[...] = grad.astype(BF16)
    for s in range(2):
        small_ref[pl.ds(i * 2 + s, 1), :] = jnp.sum(
            grad[128 * s : 128 * s + 128], axis=0, keepdims=True
        )
    small_ref[8:9, :] += jnp.sum(y * xhat, axis=0, keepdims=True)


def input_backward(tab, pieces, grad_qkv, rows, embed, vectors, grad_mid, gain_two):
    row = tiles(256, WIDTH)
    return kernel_call(
        input_backward_kernel,
        grid=(4,),
        out_shape=(shaped((1024, WIDTH)), shaped((16, WIDTH), F32)),
        in_specs=[SMEM_SPEC]
        + [ANY_SPEC] * 4
        + [tiles(256, 3 * WIDTH), row, fixed(8, WIDTH), fixed(16, WIDTH), row, fixed(1, WIDTH)],
        out_specs=(row, fixed(16, WIDTH)),
        scratch_shapes=[pltpu.VMEM((CHIPS, 2, 144, LANES), BF16), pltpu.SemaphoreType.DMA],
        compiler_params=params(24),
        cost_estimate=cost(4_000_000_000, 18_000_000),
        name="input_backward",
    )(tab, *pieces, grad_qkv, rows, embed, vectors, grad_mid, gain_two)


def time_grads_kernel(tab, *refs):
    count = len(refs) - 10
    parts = refs[:count]
    wave_ref, hot_ref, hidden_ref, slope_ref, time_out_ref = refs[count : count + 5]
    tin_ref, tout_ref, sums_ref, every, sem = refs[count + 5 :]
    if count == 1:
        pltpu.make_async_copy(parts[0], every, sem).start()
    else:

        def fetch(src, chip, half):
            pltpu.make_async_copy(src, every.at[half * CHIPS + chip], sem).start()

        each_piece(tab, parts, fetch)
    finish(every, sem)
    grads = every[...].reshape(-1, WIDTH)
    tout_ref[...] = dot_first(hidden_ref[...], grads)
    grad_pre = dot_last(grads, time_out_ref[...]) * slope_ref[...]
    tin_ref[...] = dot_first(grad_pre.astype(BF16), wave_ref[...])
    sums_ref[...] = dot(hot_ref[...], grads)


def time_grads(tab, parts, wave, hot, hidden, slope, time_out):
    rows, width = time_out.shape
    devices = wave.shape[0] // 16
    return kernel_call(
        time_grads_kernel,
        out_shape=(
            shaped((rows, wave.shape[1]), F32), shaped((rows, width), F32), shaped((16, width), F32)
        ),
        in_specs=[SMEM_SPEC] + [ANY_SPEC] * len(parts) + [VMEM_SPEC] * 5,
        out_specs=(VMEM_SPEC,) * 3,
        scratch_shapes=[pltpu.VMEM((devices, 16, width), BF16), pltpu.SemaphoreType.DMA],
        compiler_params=params(40),
        cost_estimate=cost(50_000_000, 2_000_000),
        name="time_grads",
    )(tab, *parts, wave, hot, hidden, slope, time_out)


def pick(stacked, index):
    return lax.dynamic_index_in_dim(stacked, index, 0, keepdims=False)


def in_core_order(core, own, other, axis):
    return jnp.where(
        core == 0,
        jnp.concatenate([own, other], axis=axis),
        jnp.concatenate([other, own], axis=axis),
    )


def position_table(chip, core, order):
    index = jnp.arange(72, dtype=jnp.int32)
    side = jnp.bitwise_xor(core, (index // CHIPS) % 2)
    inner = index % CHIPS
    distance = jnp.bitwise_xor(inner, chip)
    there = jnp.zeros_like(index)
    back = jnp.zeros_like(index)
    for bit in range(4):
        mask = jnp.where(side == 0, order[0][bit], order[1][bit])
        there = there + jnp.where((inner >> bit) & 1 == 1, mask, 0)
        back = back + jnp.where(jnp.bitwise_and(distance, mask) != 0, 1 << bit, 0)
    moved = jnp.where(index < 32, jnp.bitwise_xor(there, chip), back)
    return jnp.where(index < 64, moved, core)


def lane_blocks(x, starts, step):
    return [
        jnp.concatenate([x[:, k + h * step : k + h * step + LANES] for k in starts], axis=0)
        for h in (0, 1)
    ]


def whole_columns(core, own, other, blocks):
    halves = (jnp.where(core == 0, own, other), jnp.where(core == 0, other, own))
    return [[half[24 * b : 24 * b + 24] for b in range(blocks)] for half in halves]


def swap_halves(halves, core):
    own = jnp.where(core == 0, halves[0], halves[1])
    return own, core_swap(jnp.where(core == 0, halves[1], halves[0]))


def join_rows(own, other, core, blocks):
    shape = (blocks, own.shape[0] // blocks, LANES)
    return in_core_order(core, own.reshape(shape), other.reshape(shape), 1).reshape(-1, LANES)


def split_rows(piece, blocks):
    rows = piece.reshape(blocks, 2, 24, LANES).transpose(1, 0, 2, 3)
    return rows.reshape(2, blocks * 24, LANES)


def pack_extra(time_in, vectors, ints):
    rows = time_in.shape[0]
    filler = jnp.zeros((rows, 128), BF16)
    vec = lax.dynamic_update_slice(filler, vectors, (0, 0))
    num = lax.dynamic_update_slice(filler, ints[None, :], (0, 0))
    return jnp.concatenate([time_in, vec, num], axis=1)


def split_time(timestep, dataset):
    steps = timestep.reshape(-1)
    return jnp.concatenate([steps // 64, steps % 64, dataset.reshape(-1)]).astype(BF16)


def gather_all(x):
    return lax.all_gather(x, AXES, axis=0, tiled=True)


def shards(
    block_input,
    out_grad,
    timestep,
    dataset,
    lengths,
    norm1_gain,
    qkv_weight,
    out_weight,
    norm2_gain,
    up_weight,
    down_weight,
    time_in,
    time_out,
    data_embed,
    devices,
):
    flat = lax.axis_index(AXES)
    exchange = devices == 2 * CHIPS
    vectors = jnp.concatenate([norm1_gain[None], norm2_gain[None], data_embed.T], axis=0)
    numbers = split_time(timestep, dataset)
    count = numbers.shape[0] // 3
    micros, seqs, seq_len, width = block_input.shape
    tokens = micros * seqs * seq_len
    x_rows = block_input.reshape(tokens, width)
    grad_rows = out_grad.reshape(tokens, width)
    features = sinusoid(timestep.reshape(-1), time_in.shape[1] // 2).astype(BF16)
    if exchange:
        core = flat & 1
        chip = flat >> 1

        wide = lane_blocks(qkv_weight, (0, WIDTH, 2 * WIDTH), LANES)
        slim = lane_blocks(time_out, (0,), LANES)
        own, other = swap_halves(
            [jnp.concatenate([x, y], axis=0) for x, y in zip(wide, slim)], core
        )
        attention_piece = jnp.concatenate(
            [
                join_rows(own[:72], other[:72], core, 3),
                join_rows(own[72:], other[72:], core, 1),
                pack_extra(time_in, vectors, numbers),
            ],
            axis=0,
        )[None]
        near = [chip_swap(attention_piece, p) for p in (1, 2, 3)]
        up_weight, out_weight, down_weight, flat = lax.optimization_barrier(
            (up_weight, out_weight, down_weight, flat, attention_piece)
        )[:4]
        tab = position_table(flat >> 1, flat & 1, LINE_FIRST)
        down_tab = position_table(flat >> 1, flat & 1, LINE_LATER)
        wide = lane_blocks(up_weight, range(0, 4 * LANES, LANES), 4 * LANES)
        slim = lane_blocks(out_weight, (0,), LANES)
        own, other = swap_halves(
            [jnp.concatenate([x, y], axis=0) for x, y in zip(wide, slim)], core
        )
        up_piece = jnp.concatenate(
            [join_rows(own[:96], other[:96], core, 4), join_rows(own[96:], other[96:], core, 1)],
            axis=0,
        )[None]
        own, other = swap_halves(lane_blocks(down_weight, (0,), LANES), core)
        down_piece = join_rows(own, other, core, 1)[None]
        down_pair = jnp.concatenate([down_piece, chip_swap(down_piece, 1, LINE_LATER)], axis=0)
        ready = (up_piece, down_pair, tab, down_tab, features)
        line = after(jnp.concatenate([attention_piece] + near, axis=0), *ready)
        plane = chip_swap(line, 4)
        up_near = [chip_swap(after(up_piece, line), p) for p in (1, 2, 3)]
        held = jnp.concatenate([line, plane], axis=0)
        far = chip_swap(held, 8)
        up_line = jnp.concatenate([up_piece] + [after(x, held) for x in up_near], axis=0)
        far = after(far, up_line)
        attention_pieces = (held, far, core_swap(held), core_swap(far))
        up_plane = chip_swap(after(up_line, far), 4)
        down_near = [chip_swap(after(down_pair, up_line), p, LINE_LATER) for p in (2, 4, 6)]
        up_held = jnp.concatenate([up_line, up_plane], axis=0)
        up_far = chip_swap(up_held, 8)
    else:
        tab = jnp.concatenate(
            [jnp.tile(jnp.arange(CHIPS, dtype=jnp.int32), 4), jnp.zeros((8,), jnp.int32)]
        )
        down_tab = tab
        full_qkv = gather_all(qkv_weight).reshape(CHIPS, 48, 3, 2, LANES)
        full_out = gather_all(out_weight).reshape(CHIPS, 48, 2, LANES)
        full_up = gather_all(up_weight).reshape(CHIPS, 48, 2, 4, LANES)
        full_down = gather_all(down_weight).reshape(CHIPS, 192, 2, LANES)
        full_tin = gather_all(time_in).reshape(CHIPS, 2, 16, 128)
        full_tout = gather_all(time_out).reshape(CHIPS, 32, 2, LANES)
        full_vec = lax.all_gather(vectors, AXES, axis=1, tiled=True).reshape(4, CHIPS, 2, 24)
        numbers_all = gather_all(numbers[None])
        extra = jnp.zeros((CHIPS, 2, 16, LANES), BF16)
        extra = extra.at[:, :, :, :128].set(full_tin)
        extra = extra.at[:, :, 0:4, 128:152].set(full_vec.transpose(1, 2, 0, 3))
        attention_pieces = []
        down_pieces = []
        up_pieces = []
        for half in (0, 1):
            wide = full_qkv[:, :, :, half].transpose(0, 2, 1, 3).reshape(CHIPS, 144, LANES)
            whole = jnp.concatenate([wide, full_tout[:, :, half], extra[:, half]], axis=1)
            attention_pieces += [whole[:8], whole[8:]]
            down_pieces += [full_down[:8, :, half], full_down[8:, :, half]]
            wide = full_up[:, :, half].transpose(0, 2, 1, 3).reshape(CHIPS, 192, LANES)
            whole = jnp.concatenate([wide, full_out[:, :, half]], axis=1)
            up_pieces += [whole[:8], whole[8:]]

    arrivals = []
    if exchange:
        x_rows = after(x_rows, up_held)
        arrivals = [up_far, down_near]
    forward = attention_forward(tab, lengths, dataset, attention_pieces, x_rows, features)
    (normed, qkv, embed, vecs, seen, probs, att), arrivals = together(forward, arrivals)
    seen = seen[:, :, 0, : 3 * count].reshape(2 * CHIPS, 3 * count) if exchange else numbers_all
    steps = seen[:, :count] * 64 + seen[:, count : 2 * count].astype(F32)
    wave = sinusoid(steps.reshape(-1), time_in.shape[1] // 2).astype(BF16)
    wave = jnp.pad(wave.reshape(devices, count, -1), ((0, 0), (0, 16 - count), (0, 0)))
    wave = wave.reshape(devices * 16, -1)
    which = jnp.pad(seen[:, 2 * count :], ((0, 0), (0, 16 - count))).reshape(-1)
    place = jnp.tile(jnp.arange(16), devices)
    hot = jnp.stack(
        [(place < count) & (which == 0), (place < count) & (which == 1), place == 8, place == 9]
    )
    hot = jnp.pad(hot.astype(BF16), ((0, 12), (0, 0)))
    pre = dot_last(wave, time_in)
    gate = 1.0 / (1.0 + jnp.exp(-pre))
    hidden = (pre * gate).astype(BF16)
    slope_pre = gate * (1.0 + pre * (1.0 - gate))
    if exchange:
        up_far, down_near = arrivals
        up_pieces = (up_held, up_far, core_swap(up_held), core_swap(up_far))
        down_held = jnp.concatenate([down_pair] + down_near, axis=0)
        att, wave, hot, hidden, slope_pre, down_held = lax.optimization_barrier(
            (att, wave, hot, hidden, slope_pre, down_held)
        )
        arrivals = chip_swap(down_held, 8, LINE_LATER)
    forward = up_forward(tab, up_pieces, att, x_rows, grad_rows, embed, vecs)
    (mid, two, act, slope, down_theirs), arrivals = together(forward, arrivals)
    if exchange:
        down_far = arrivals
        down_sum = Scatter(down_theirs)
        arrivals = [core_swap(down_held), core_swap(down_far)], down_sum.swap()
    down_mine, arrivals = together(down_grad(tab, act, grad_rows), arrivals)
    if exchange:
        down_pieces = (down_held, down_far, *arrivals[0])
        down_sum.land(arrivals[1], down_mine)
        slope = after(slope, *down_sum.send())
        arrivals = down_sum.fly()
    backward = mlp_backward(
        tab, down_tab, up_pieces, down_pieces, two, att, slope, grad_rows, mid, vecs
    )
    backward, arrivals = together(backward, arrivals)
    grad_mid, branch, grad_up, grad_att, gain_two, up_theirs = backward
    if exchange:
        down_sum.land(arrivals)
        up_sum = Scatter(up_theirs)
        grad_up = after(grad_up, *down_sum.send())
        arrivals = down_sum.fly(), up_sum.swap()
    up_mine, arrivals = together(up_grad(tab, att, branch, two, grad_up), arrivals)
    if exchange:
        down_sum.land(arrivals[0])
        up_sum.land(arrivals[1], up_mine)
        grad_att = after(grad_att, *up_sum.send(), *down_sum.send())
        arrivals = up_sum.fly(), down_sum.fly()
    backward = attention_backward(tab, normed, qkv, probs, grad_att)
    (grad_qkv, att_theirs), arrivals = together(backward, arrivals)
    if exchange:
        up_sum.land(arrivals[0])
        down_sum.land(arrivals[1])
        down_total = down_sum.total()
        att_sum = Scatter(att_theirs)
        grad_qkv = after(grad_qkv, *up_sum.send(), down_total)
        arrivals = up_sum.fly(), att_sum.swap()
    att_mine, arrivals = together(qkv_grad(tab, normed, grad_qkv), arrivals)
    if exchange:
        up_sum.land(arrivals[0])
        att_sum.land(arrivals[1], att_mine)
        grad_qkv = after(grad_qkv, *att_sum.send(), *up_sum.send())
        arrivals = att_sum.fly(), up_sum.fly()
    backward = input_backward(
        tab, attention_pieces, grad_qkv, x_rows, embed, vecs, grad_mid, gain_two
    )
    (grad_input, small), arrivals = together(backward, arrivals)

    small = small.astype(BF16)[None]
    if exchange:
        att_sum.land(arrivals[0])
        up_sum.land(arrivals[1])
        mid = after(mid, *att_sum.send(), small)
        arrivals = att_sum.fly(), [chip_swap(small, p) for p in (1, 2, 3)]
    result, arrivals = together(block_result(down_tab, down_pieces, act, mid), arrivals)
    if exchange:
        att_sum.land(arrivals[0])
        small_line = jnp.concatenate([small] + arrivals[1], axis=0)
        small_line = after(small_line, *att_sum.send())
        held = gather_plane(small_line)
        far = chip_swap(held, 8)
        every = (held, far, core_swap(held), core_swap(far))
        att_sum.land(att_sum.fly())
    else:
        every = (gather_all(small),)
    grad_tin, grad_tout, sums = time_grads(tab, every, wave, hot, hidden, slope_pre, time_out)
    own_cols = norm1_gain.shape[0]
    sums = lax.dynamic_slice_in_dim(sums, flat * own_cols, own_cols, 1)

    if exchange:
        own, other = swap_halves(after(down_total, result).reshape(2, 96, LANES), core)
        grad_down = in_core_order(core, own, other, 1)
        piece = after(up_sum.total(), result)
        out_rows = piece[192:].reshape(2, 24, LANES)
        own, other = swap_halves(
            jnp.concatenate([split_rows(piece[:192], 4), out_rows], axis=1), core
        )
        left, right = whole_columns(core, own, other, 5)
        grad_up_weight = jnp.concatenate(left[:4] + right[:4], axis=1)
        grad_out = jnp.concatenate([left[4], right[4]], axis=1)
        own, other = swap_halves(split_rows(att_sum.total(), 3), core)
        left, right = whole_columns(core, own, other, 3)
        grad_qkv_weight = jnp.concatenate(
            [side[sec] for sec in range(3) for side in (left, right)], axis=1
        )
    else:
        scatter = partial(lax.psum_scatter, axis_name=AXES, scatter_dimension=0, tiled=True)
        both = jnp.stack([down_mine, down_theirs]).astype(F32)
        grad_down = scatter(both.transpose(1, 2, 0, 3).reshape(FF, WIDTH))
        both = jnp.stack([up_mine, up_theirs]).astype(F32)
        grad_out = scatter(both[:, :, 192:].transpose(1, 2, 0, 3).reshape(WIDTH, WIDTH))
        both = both[:, :, :192].reshape(2, CHIPS, 4, 48, LANES)
        grad_up_weight = scatter(both.transpose(1, 3, 0, 2, 4).reshape(WIDTH, FF))
        both = jnp.stack([att_mine, att_theirs]).astype(F32).reshape(2, CHIPS, 3, 48, LANES)
        grad_qkv_weight = scatter(both.transpose(1, 3, 2, 0, 4).reshape(WIDTH, 3 * WIDTH))

    return (
        result.reshape(block_input.shape),
        grad_input.reshape(block_input.shape),
        sums[2],
        grad_qkv_weight,
        grad_out,
        sums[3],
        grad_up_weight,
        grad_down,
        grad_tin,
        grad_tout,
        sums[:2].T,
    )


def solution(mesh):
    devices = mesh.shape["dp"] * mesh.shape["fsdp"]
    seq_spec = P(None, AXES, None, None)
    int_spec = P(None, AXES)
    row_spec = P(AXES, None)
    in_specs = (seq_spec, seq_spec, int_spec, int_spec, int_spec, P(AXES), row_spec, row_spec, P(AXES))
    in_specs = in_specs + (row_spec,) * 5
    out_specs = (seq_spec, seq_spec, P(AXES), row_spec, row_spec, P(AXES)) + (row_spec,) * 5
    return jax.shard_map(
        partial(shards, devices=devices),
        mesh=mesh,
        in_specs=in_specs,
        out_specs=out_specs,
        check_vma=False,
    )
```

```python
from functools import partial
import math

import jax
import jax.numpy as jnp
from jax import lax
from jax.experimental import pallas as pl
from jax.experimental.pallas import tpu as pltpu
from jax.sharding import PartitionSpec as P

HEAD_DIM = 64
AXES = ("dp", "fsdp")
LANES = 384
CHIPS = 16
WIDTH = 768
FF = 3072
F32 = jnp.float32
BF16 = jnp.bfloat16
NEG = -1000000000.0


def sinusoid(timestep, half_width):
    frequency = jnp.exp(-math.log(10000.0) * jnp.arange(half_width, dtype=F32) / half_width)
    angles = timestep.astype(F32)[:, None] * frequency[None, :]
    return jnp.concatenate([jnp.cos(angles), jnp.sin(angles)], axis=-1)


def dot(left, right):
    return jnp.dot(left, right, preferred_element_type=F32)


def dot_last(left, right):
    return lax.dot_general(left, right, (((1,), (1,)), ((), ())), preferred_element_type=F32)


def dot_first(left, right):
    return lax.dot_general(left, right, (((0,), (0,)), ((), ())), preferred_element_type=F32)


def positions(masks):
    return [sum(masks[b] for b in range(4) if (p >> b) & 1) for p in range(CHIPS)]


LINE_FIRST = ((2, 1, 8, 4), (2, 1, 4, 8))
LINE_LATER = ((8, 2, 1, 4), (4, 2, 1, 8))


def core_swap(x):
    return lax.ppermute(x, AXES, [(i, i ^ 1) for i in range(2 * CHIPS)])


def chip_swap(x, position, order=LINE_FIRST):
    far = [positions(masks)[position] * 2 for masks in order]
    return lax.ppermute(x, AXES, [(i, i ^ far[i & 1]) for i in range(2 * CHIPS)])


def after(x, *others):
    return lax.optimization_barrier((x,) + others)[0]


def gather_line(piece):
    return jnp.concatenate([piece] + [chip_swap(piece, p) for p in (1, 2, 3)], axis=0)


def gather_plane(held):
    return jnp.concatenate([held, chip_swap(held, 4)], axis=0)


def together(outs, arrivals):
    return lax.optimization_barrier((outs, arrivals))


class Scatter:
    def __init__(self, theirs):
        self.parts = []
        self.steps = [(8,), (4,), (1, 2, 3)]
        self.theirs = theirs

    def swap(self):
        return [core_swap(self.theirs)]

    def land(self, brought, *own):
        self.parts += [*brought, *own]

    def sum(self, start, stop):
        total = self.parts[0][start:stop].astype(F32)
        for part in self.parts[1:]:
            total = total + part[start:stop].astype(F32)
        return total

    def send(self):
        self.at = self.steps.pop(0)
        size = 1 if len(self.at) == 3 else self.at[0]
        self.sent = [self.sum(p, p + size).astype(BF16) for p in self.at]
        self.parts = [self.sum(0, size)]
        return [*self.sent, self.parts[0]]

    def fly(self):
        return [chip_swap(x, p) for x, p in zip(self.sent, self.at)]

    def total(self):
        return self.sum(0, 1)[0]


VMEM_SPEC = pl.BlockSpec(memory_space=pltpu.VMEM)
SMEM_SPEC = pl.BlockSpec(memory_space=pltpu.SMEM)
ANY_SPEC = pl.BlockSpec(memory_space=pl.ANY)


def tiles(rows, cols):
    return pl.BlockSpec((rows, cols), lambda i: (i, 0))


def columns(rows, cols):
    return pl.BlockSpec((rows, cols), lambda i: (0, i))


def fixed(*shape):
    return pl.BlockSpec(shape, lambda i: (0,) * len(shape))


def shaped(shape, dtype=BF16):
    return pltpu.HBM(shape, dtype)


def local(shape, dtype=BF16):
    return pltpu.VMEM(shape, dtype)


def params(mib):
    return pltpu.CompilerParams(vmem_limit_bytes=mib * 1024 * 1024)


def kernel_call(kernel, **kwargs):
    call = pl.pallas_call(kernel, **kwargs)
    if "grid_spec" in kwargs:
        grid_spec = kwargs["grid_spec"]
        specs = [SMEM_SPEC] * grid_spec.num_scalar_prefetch + list(grid_spec.in_specs)
    else:
        specs = kwargs["in_specs"]

    def place(x, spec):
        if spec is SMEM_SPEC:
            return x
        space = pltpu.VMEM if spec is VMEM_SPEC else pltpu.HBM
        return pltpu.with_memory_space_constraint(x, space)

    def run(*operands):
        return call(*[place(x, spec) for x, spec in zip(operands, specs, strict=True)])

    return run


def cost(flops, nbytes, transcendentals=0):
    return pl.CostEstimate(flops=flops, bytes_accessed=nbytes, transcendentals=transcendentals)


def ln_stats(v):
    center = v - jnp.mean(v, axis=-1, keepdims=True)
    scale = lax.rsqrt(jnp.mean(center * center, axis=-1, keepdims=True) + 1e-05)
    return center * scale, scale


def ln_back(y, gain, xhat, scale):
    yg = y * gain
    return scale * (
        yg - jnp.mean(yg, axis=-1, keepdims=True) - xhat * jnp.mean(yg * xhat, axis=-1, keepdims=True)
    )


def first_core(tab):
    return tab[64]


def each_piece(tab, parts, fn):
    core = first_core(tab)
    for side in (0, 1):
        half = core if side == 0 else 1 - core
        for group in (0, 1):
            part = parts[side * 2 + group]

            def body(q, _, part=part, side=side, group=group, half=half):
                chip = tab[side * CHIPS + group * 8 + q]
                fn(part.at[q], chip, half)
                return 0

            lax.fori_loop(0, 8, body, 0)


def rows_of(chip, size):
    return pl.ds(pl.multiple_of(chip * size, size), size)


def lanes_of(half, size, base=0):
    return pl.ds(pl.multiple_of(half * size + base, 128), LANES)


def fetch_pieces(tab, parts, rows, dst, sem, first=0):
    each_piece(
        tab,
        parts,
        lambda src, chip, half: pltpu.make_async_copy(
            src.at[pl.ds(first, rows), :], dst.at[chip, half], sem
        ).start(),
    )


def block(pieces, half, first, rows=48):
    return pieces[:, half, first : first + rows, :].reshape(CHIPS * rows, LANES)


def both_halves(pieces, first, rows=48):
    return jnp.concatenate([block(pieces, h, first, rows) for h in (0, 1)], axis=1)


def down_rows(pieces, j):
    return jnp.concatenate(
        [pieces[4 * j : 4 * j + 4, h].reshape(WIDTH, LANES) for h in (0, 1)], axis=1
    )


def qkv_columns(pieces, half):
    return jnp.concatenate([block(pieces, half, 48 * sec) for sec in range(3)], axis=1)


def finish(ref, sem):
    pltpu.make_async_copy(ref, ref, sem).wait()


def add_embed(x, embed, i):
    seqs = x.shape[0] // 128
    parts = [
        x[128 * k : 128 * k + 128].astype(F32) + embed[pl.ds(i * seqs + k, 1), :]
        for k in range(seqs)
    ]
    return jnp.concatenate(parts, axis=0)


def two_heads(x, low_half):
    none = jnp.zeros_like(x)
    return jnp.concatenate([jnp.where(low_half, x, none), jnp.where(low_half, none, x)], axis=0)


def side_by_side(x):
    return jnp.concatenate([x[:128], x[128:]], axis=1)


def pair_base(pair):
    return (pair // 3) * 3 * LANES + (pair % 3) * 128


def attention_rows(k, length, qkv_ref, probs_ref, att_ref):
    low_half = lax.broadcasted_iota(jnp.int32, (128, 128), 1) < HEAD_DIM
    keep = lax.broadcasted_iota(jnp.int32, (256, 128), 1) < length
    rows = slice(128 * k, 128 * k + 128)
    scores = []
    for pair in range(6):
        base = pair_base(pair)
        query = two_heads(qkv_ref[rows, base : base + 128], low_half)
        key = qkv_ref[rows, base + LANES : base + LANES + 128]
        scores.append(jnp.where(keep, dot_last(query, key) * HEAD_DIM ** (-0.5), NEG))
    probs = []
    for pair in range(6):
        shifted = jnp.exp(scores[pair] - jnp.max(scores[pair], axis=-1, keepdims=True))
        total = jnp.sum(shifted, axis=-1, keepdims=True)
        probs.append((shifted * (1.0 / total)).astype(BF16))
        first = 256 * (6 * k + pair)
        probs_ref[first : first + 256, :] = probs[pair]
    for pair in range(6):
        base = pair_base(pair) + 2 * LANES
        value = two_heads(qkv_ref[rows, base : base + 128], low_half)
        att_ref[rows, pair * 128 : pair * 128 + 128] = dot(
            side_by_side(probs[pair]), value
        ).astype(BF16)


def attention_kernel(
    tab, lens, sets, g_a, g_b, g_c, g_d, x_ref, feat_ref,
    normed_ref, qkv_ref, te_ref, vec_ref, seen_ref, probs_ref, att_ref,
    w, w_time, sem, sem_time,
):
    i = pl.program_id(0)

    @pl.when(i == 0)
    def _():
        fetch_pieces(tab, (g_a, g_b, g_c, g_d), 48, w_time, sem_time, 144)
        fetch_pieces(tab, (g_a, g_b, g_c, g_d), 144, w, sem)
        finish(w_time, sem_time)
        lane = lax.broadcasted_iota(jnp.int32, (128, WIDTH), 1)
        spread = (lax.broadcasted_iota(jnp.int32, (128, WIDTH), 0) == lane % 24).astype(BF16)
        vectors = jnp.zeros((16, WIDTH), F32)
        embed = jnp.zeros((8, WIDTH), F32)
        for owner in (0, 1):
            extra = block(w_time, owner, 32, 16)
            wide = dot(extra[:, 128:256], spread)
            chip = lax.broadcasted_iota(jnp.int32, (256, WIDTH), 0) // 16
            place = lax.broadcasted_iota(jnp.int32, (256, WIDTH), 1) // 24
            wide = jnp.where(place == chip * 2 + owner, wide, 0.0)
            vectors = vectors + jnp.sum(wide.reshape(CHIPS, 16, WIDTH), axis=0)
            pre = dot_last(feat_ref[...], extra[:, 0:128])
            hidden = (pre / (1.0 + jnp.exp(-pre))).astype(BF16)
            embed = embed + dot(hidden, both_halves(w_time, 16 * owner, 16))
            seen_ref[owner] = w_time[:, owner, 32:48, 256:]
        vec_ref[...] = vectors
        for s in range(8):
            chosen = jnp.where(sets[s // 4, s % 4] == 1, vectors[3:4, :], vectors[2:3, :])
            te_ref[s : s + 1, :] = embed[s : s + 1, :] + chosen

    xhat, _unused = ln_stats(add_embed(x_ref[...], te_ref, i))
    normed_ref[...] = (xhat * vec_ref[0:1, :]).astype(BF16)

    @pl.when(i == 0)
    def _():
        finish(w, sem)

    for half in (0, 1):
        cols = slice(half * 3 * LANES, (half + 1) * 3 * LANES)
        qkv_ref[:, cols] = dot(normed_ref[...], qkv_columns(w, half)).astype(BF16)
    for k in range(2):
        attention_rows(k, lens[i // 2, i % 2 * 2 + k], qkv_ref, probs_ref, att_ref)


def attention_forward(tab, lens, sets, pieces, rows, features):
    row = tiles(256, WIDTH)
    return kernel_call(
        attention_kernel,
        grid=(4,),
        out_shape=(
            shaped((1024, WIDTH)),
            shaped((1024, 3 * WIDTH)),
            shaped((8, WIDTH), F32),
            shaped((16, WIDTH), F32),
            shaped((2, CHIPS, 16, 128)),
            shaped((48 * 256, 128)),
            shaped((1024, WIDTH)),
        ),
        in_specs=[SMEM_SPEC] * 3 + [ANY_SPEC] * 4 + [row, fixed(8, 128)],
        out_specs=(
            row, tiles(256, 3 * WIDTH), fixed(8, WIDTH), fixed(16, WIDTH),
            fixed(2, CHIPS, 16, 128), tiles(12 * 256, 128), row,
        ),
        scratch_shapes=[
            pltpu.VMEM((CHIPS, 2, 144, LANES), BF16),
            pltpu.VMEM((CHIPS, 2, 48, LANES), BF16),
            pltpu.SemaphoreType.DMA,
            pltpu.SemaphoreType.DMA,
        ],
        compiler_params=params(26),
        cost_estimate=cost(8_000_000_000, 20_000_000, 1_600_000),
        name="attention_forward",
    )(tab, lens, sets, *pieces, rows, features)


def gelu_parts(u):
    cdf = 0.5 + 0.5 * lax.erf(u * math.sqrt(0.5))
    return cdf, jnp.exp(u * u * -0.5) * (1.0 / math.sqrt(2.0 * math.pi))


def up_columns(pieces, j):
    first = 96 * (j % 2)
    return jnp.concatenate(
        [block(pieces, j // 2, first), block(pieces, j // 2, first + 48)], axis=1
    )


def half_of(tab, side):
    return first_core(tab) if side == 0 else 1 - first_core(tab)


def clamped(rows, cols):
    return pl.BlockSpec((rows, cols), lambda i: (jnp.minimum(i, 3), 0))


def down_grad_rows(tab, side, j, act, out_grad, out_ref):
    lanes = lanes_of(half_of(tab, side), LANES)
    grad = dot_first(act, out_grad[:, lanes]).astype(BF16)
    for k in range(4):
        place = tab[32 + side * CHIPS + j * 4 + k]
        out_ref[place, :, :] = grad[192 * k : 192 * k + 192, :]


def up_kernel(
    tab, u_a, u_b, u_c, u_d, out_grad_ref, att_ref, x_ref, te_ref, vec_ref,
    mid_ref, two_ref, act_ref, slope_ref, theirs_ref,
    w, sem,
):
    i = pl.program_id(0)

    @pl.when(i == 0)
    def _():
        fetch_pieces(tab, (u_a, u_b, u_c, u_d), 240, w, sem)
        finish(w, sem)

    @pl.when(i < 4)
    def _():
        rows = rows_of(i, 256)
        mid = add_embed(x_ref[...], te_ref, i) + dot(att_ref[...], both_halves(w, 192))
        mid_ref[...] = mid
        xhat, _unused = ln_stats(mid)
        two = (xhat * vec_ref[1:2, :]).astype(BF16)
        two_ref[...] = two
        for j in range(4):
            up = dot(two, up_columns(w, j))
            cdf, density = gelu_parts(up)
            act_ref[j, rows, :] = (up * cdf).astype(BF16)
            slope_ref[j, rows, :] = (cdf + up * density).astype(BF16)

    @pl.when(i >= 4)
    def _():
        down_grad_rows(tab, 1, i - 4, act_ref[i - 4], out_grad_ref, theirs_ref)


def up_forward(tab, pieces, att, rows, out_grad, embed, vectors):
    row = clamped(256, WIDTH)
    return kernel_call(
        up_kernel,
        grid=(8,),
        out_shape=(
            shaped((1024, WIDTH), F32),
            shaped((1024, WIDTH)),
            local((4, 1024, WIDTH)),
            local((4, 1024, WIDTH)),
            local((CHIPS, 192, LANES)),
        ),
        in_specs=[SMEM_SPEC]
        + [ANY_SPEC] * 4
        + [VMEM_SPEC, row, row, fixed(8, WIDTH), fixed(16, WIDTH)],
        out_specs=(row, row) + (VMEM_SPEC,) * 3,
        scratch_shapes=[pltpu.VMEM((CHIPS, 2, 240, LANES), BF16), pltpu.SemaphoreType.DMA],
        compiler_params=params(26),
        cost_estimate=cost(10_000_000_000, 30_000_000, 6_000_000),
        name="up_forward",
    )(tab, *pieces, out_grad, att, rows, embed, vectors)


def down_grad_kernel(tab, act_ref, out_grad_ref, out_ref, act_hbm, sem):
    j = pl.program_id(0)

    @pl.when(j == 0)
    def _():
        pltpu.make_async_copy(act_ref, act_hbm, sem).start()

    down_grad_rows(tab, 0, j, act_ref[j], out_grad_ref, out_ref)

    @pl.when(j == 3)
    def _():
        pltpu.make_async_copy(act_ref, act_hbm, sem).wait()


def down_grad(tab, act, out_grad):
    return kernel_call(
        down_grad_kernel,
        grid=(4,),
        out_shape=(local((CHIPS, 192, LANES)), shaped((4, 1024, WIDTH))),
        in_specs=[SMEM_SPEC] + [VMEM_SPEC] * 2,
        out_specs=(VMEM_SPEC, ANY_SPEC),
        scratch_shapes=[pltpu.SemaphoreType.DMA],
        compiler_params=params(12),
        cost_estimate=cost(3_000_000_000, 10_000_000),
        name="down_grad",
    )(tab, act, out_grad)


def store_blocks(tab, side, target, first, part, lanes):
    for chip in range(CHIPS):
        place = tab[32 + side * CHIPS + chip]
        target[place, pl.ds(first, 48), :] = part[48 * chip : 48 * chip + 48, lanes]


def out_grad_rows(tab, side, att, branch, out_ref, part):
    lanes = lanes_of(half_of(tab, side), LANES)
    part[:, 0:LANES] = dot_first(att[...], branch[:, lanes]).astype(BF16)
    store_blocks(tab, side, out_ref, 192, part, slice(0, LANES))


def up_grad_rows(tab, side, j, two, grad_up, out_ref, part):
    part[...] = dot_first(two, grad_up).astype(BF16)
    for b in range(2):
        first = pl.multiple_of((2 * j + b) * 48, 48)
        store_blocks(tab, side, out_ref, first, part, slice(b * LANES, (b + 1) * LANES))


def up_grad_kernel(
    tab, att_hbm, two_hbm, branch_ref, grad_up_ref, out_ref, att, two, part, sem_att, sem_two
):
    j = pl.program_id(0)

    @pl.when(j == 0)
    def _():
        pltpu.make_async_copy(att_hbm, att, sem_att).start()
        pltpu.make_async_copy(two_hbm, two, sem_two).start()
        finish(att, sem_att)
        out_grad_rows(tab, 0, att, branch_ref, out_ref, part)
        finish(two, sem_two)

    @pl.when(j > 0)
    def _():
        up_grad_rows(tab, 0, j - 1, two[...], grad_up_ref[j - 1], out_ref, part)


def up_grad(tab, att, branch, two, grad_up):
    return kernel_call(
        up_grad_kernel,
        grid=(3,),
        out_shape=local((CHIPS, 240, LANES)),
        in_specs=[SMEM_SPEC] + [ANY_SPEC] * 2 + [VMEM_SPEC] * 2,
        out_specs=VMEM_SPEC,
        scratch_shapes=[pltpu.VMEM((1024, WIDTH), BF16)] * 2
        + [pltpu.VMEM((WIDTH, WIDTH), BF16)]
        + [pltpu.SemaphoreType.DMA] * 2,
        compiler_params=params(16),
        cost_estimate=cost(3_200_000_000, 11_000_000),
        name="up_grad",
    )(tab, att, two, branch, grad_up)


def mlp_backward_kernel(
    tab, later_tab, u_a, u_b, u_c, u_d, d_a, d_b, d_c, d_d,
    two_hbm, att_hbm, slope_ref, out_grad_ref, mid_ref, vec_ref,
    grad_mid_ref, branch_ref, mine_up_ref, grad_att_ref, gain_ref, theirs_ref,
    w, w_down, two, att, theirs_up, grad_up, part, sem, sem_down, sem_two, sem_att,
):
    i = pl.program_id(0)

    @pl.when(i == 0)
    def _():
        fetch_pieces(later_tab, (d_a, d_b, d_c, d_d), 192, w_down, sem_down)
        gain_ref[...] = jnp.zeros_like(gain_ref)
        finish(w_down, sem_down)
        fetch_pieces(tab, (u_a, u_b, u_c, u_d), 240, w, sem)
        pltpu.make_async_copy(two_hbm, two, sem_two).start()
        pltpu.make_async_copy(att_hbm, att, sem_att).start()

    @pl.when(i < 4)
    def _():
        rows = rows_of(i, 256)
        for j in range(4):
            grad_act = dot_last(out_grad_ref[rows, :], down_rows(w_down, j))
            grad_up[j] = (grad_act * slope_ref[j, rows, :].astype(F32)).astype(BF16)

        @pl.when(i == 0)
        def _():
            finish(w, sem)

        y = jnp.zeros((256, WIDTH), F32)
        for j in range(4):
            y = y + dot_last(grad_up[j], up_columns(w, j))
        mine = half_of(tab, 0)
        for j in range(2):
            mine_up_ref[j, rows, :] = grad_up[2 * mine + j]
            theirs_up[j, rows, :] = grad_up[2 - 2 * mine + j]
        xhat, scale = ln_stats(mid_ref[...])
        grad = out_grad_ref[rows, :].astype(F32) + ln_back(y, vec_ref[1:2, :], xhat, scale)
        grad_mid_ref[...] = grad
        branch = grad.astype(BF16)
        branch_ref[rows, :] = branch
        gain_ref[...] += jnp.sum(y * xhat, axis=0, keepdims=True)
        grad_att_ref[rows, :] = dot_last(branch, both_halves(w, 192)).astype(BF16)

    @pl.when(i == 4)
    def _():
        finish(two, sem_two)
        finish(att, sem_att)
        out_grad_rows(tab, 1, att, branch_ref, theirs_ref, part)

    @pl.when(i >= 4)
    def _():
        up_grad_rows(tab, 1, i - 4, two[...], theirs_up[i - 4], theirs_ref, part)


def mlp_backward(
    tab, later_tab, up_pieces, down_pieces, two, att, slope, out_grad, mid, vectors
):
    return kernel_call(
        mlp_backward_kernel,
        grid=(6,),
        out_shape=(
            shaped((1024, WIDTH), F32),
            local((1024, WIDTH)),
            local((2, 1024, WIDTH)),
            local((1024, WIDTH)),
            local((1, WIDTH), F32),
            local((CHIPS, 240, LANES)),
        ),
        in_specs=[SMEM_SPEC] * 2
        + [ANY_SPEC] * 10
        + [VMEM_SPEC] * 2
        + [clamped(256, WIDTH), fixed(16, WIDTH)],
        out_specs=(clamped(256, WIDTH),) + (VMEM_SPEC,) * 5,
        scratch_shapes=[
            pltpu.VMEM((CHIPS, 2, 240, LANES), BF16),
            pltpu.VMEM((CHIPS, 2, 192, LANES), BF16),
            pltpu.VMEM((1024, WIDTH), BF16),
            pltpu.VMEM((1024, WIDTH), BF16),
            pltpu.VMEM((2, 1024, WIDTH), BF16),
            pltpu.VMEM((4, 256, WIDTH), BF16),
            pltpu.VMEM((WIDTH, WIDTH), BF16),
        ]
        + [pltpu.SemaphoreType.DMA] * 4,
        compiler_params=params(38),
        cost_estimate=cost(18_000_000_000, 50_000_000),
        name="mlp_backward",
    )(tab, later_tab, *up_pieces, *down_pieces, two, att, slope, out_grad, mid, vectors)


def attention_backward_rows(k, first_row, qkv_ref, probs_ref, grad_att_ref, grad_qkv_ref):
    low_half = lax.broadcasted_iota(jnp.int32, (128, 128), 1) < HEAD_DIM
    rows = slice(128 * k, 128 * k + 128)
    whole_rows = pl.ds(pl.multiple_of(first_row, 128), 128)

    def heads(ref, base):
        where = whole_rows if ref is grad_att_ref else rows
        return two_heads(ref[where, base : base + 128], low_half)

    def probs_of(pair):
        first = 256 * (6 * k + pair)
        return probs_ref[first : first + 256, :]

    grad_probs = []
    for pair in range(6):
        base = pair_base(pair) + 2 * LANES
        grad_probs.append(
            dot_last(heads(grad_att_ref, pair * 128), qkv_ref[rows, base : base + 128])
        )
    grad_scores = []
    for pair in range(6):
        probs = probs_of(pair).astype(F32)
        inner = jnp.sum(probs * grad_probs[pair], axis=-1, keepdims=True)
        grad_scores.append((probs * (grad_probs[pair] - inner)).astype(BF16))
    for pair in range(6):
        base = pair_base(pair)
        grad_query = dot(side_by_side(grad_scores[pair]), heads(qkv_ref, base + LANES))
        grad_key = dot_first(grad_scores[pair], heads(qkv_ref, base))
        grad_value = dot_first(probs_of(pair), heads(grad_att_ref, pair * 128))
        grad_query = (grad_query * HEAD_DIM ** (-0.5)).astype(BF16)
        grad_qkv_ref[rows, base : base + 128] = grad_query
        base = base + LANES
        grad_qkv_ref[rows, base : base + 128] = (grad_key * HEAD_DIM ** (-0.5)).astype(BF16)
        base = base + LANES
        grad_qkv_ref[rows, base : base + 128] = grad_value.astype(BF16)


def qkv_grad_rows(tab, side, normed, grad_qkv, out_ref, part):
    part[...] = dot_first(normed, grad_qkv).astype(BF16)
    for sec in range(3):
        store_blocks(tab, side, out_ref, 48 * sec, part, slice(sec * LANES, (sec + 1) * LANES))


def attention_backward_kernel(
    tab, normed_hbm, qkv_ref, probs_ref, grad_att_ref, grad_qkv_ref, mine_ref, theirs_ref,
    normed, kept, part, sem,
):
    i = pl.program_id(0)

    @pl.when(i == 0)
    def _():
        pltpu.make_async_copy(normed_hbm, normed, sem).start()

    @pl.when(i < 4)
    def _():
        for k in range(2):
            attention_backward_rows(
                k, i * 256 + 128 * k, qkv_ref, probs_ref, grad_att_ref, grad_qkv_ref
            )
        for side, target in enumerate((mine_ref, kept)):
            lanes = pl.ds(pl.multiple_of(half_of(tab, side) * 3 * LANES, 128), 3 * LANES)
            target[rows_of(i, 256), :] = grad_qkv_ref[:, lanes]

    @pl.when(i == 4)
    def _():
        finish(normed, sem)
        qkv_grad_rows(tab, 1, normed[...], kept[...], theirs_ref, part)


def attention_backward(tab, normed, qkv, probs, grad_att):
    wide = clamped(256, 3 * WIDTH)
    return kernel_call(
        attention_backward_kernel,
        grid=(5,),
        out_shape=(
            shaped((1024, 3 * WIDTH)), local((1024, 3 * LANES)), local((CHIPS, 144, LANES))
        ),
        in_specs=[SMEM_SPEC, ANY_SPEC, wide, clamped(12 * 256, 128), VMEM_SPEC],
        out_specs=(wide, VMEM_SPEC, VMEM_SPEC),
        scratch_shapes=[
            pltpu.VMEM((1024, WIDTH), BF16),
            pltpu.VMEM((1024, 3 * LANES), BF16),
            pltpu.VMEM((WIDTH, 3 * LANES), BF16),
            pltpu.SemaphoreType.DMA,
        ],
        compiler_params=params(28),
        cost_estimate=cost(11_000_000_000, 22_000_000),
        name="attention_backward",
    )(tab, normed, qkv, probs, grad_att)


def qkv_grad_kernel(
    tab, later_tab, d_a, d_b, d_c, d_d, normed_ref, grad_qkv_ref, act_ref, mid_ref,
    out_ref, result_ref,
    part, w_down, sem,
):
    i = pl.program_id(0)

    @pl.when(i == 0)
    def _():
        fetch_pieces(later_tab, (d_a, d_b, d_c, d_d), 192, w_down, sem)
        qkv_grad_rows(tab, 0, normed_ref[...], grad_qkv_ref[...], out_ref, part)
        finish(w_down, sem)

    @pl.when(i > 0)
    def _():
        total = mid_ref[...]
        for j in range(4):
            total = total + dot(act_ref[j], down_rows(w_down, j))
        result_ref[...] = total.astype(BF16)


def qkv_grad(tab, later_tab, pieces, normed, grad_qkv, act, mid):
    row = pl.BlockSpec((256, WIDTH), lambda i: (jnp.maximum(i - 1, 0), 0))
    wide = pl.BlockSpec((4, 256, WIDTH), lambda i: (0, jnp.maximum(i - 1, 0), 0))
    return kernel_call(
        qkv_grad_kernel,
        grid=(5,),
        out_shape=(local((CHIPS, 144, LANES)), shaped((1024, WIDTH))),
        in_specs=[SMEM_SPEC] * 2 + [ANY_SPEC] * 4 + [fixed(1024, WIDTH), VMEM_SPEC, wide, row],
        out_specs=(VMEM_SPEC, row),
        scratch_shapes=[
            pltpu.VMEM((WIDTH, 3 * LANES), BF16),
            pltpu.VMEM((CHIPS, 2, 192, LANES), BF16),
            pltpu.SemaphoreType.DMA,
        ],
        compiler_params=params(26),
        cost_estimate=cost(7_000_000_000, 22_000_000),
        name="qkv_grad",
    )(tab, later_tab, *pieces, normed, grad_qkv, act, mid)


def input_backward_kernel(
    tab, g_a, g_b, g_c, g_d, grad_qkv_ref, x_ref, te_ref, vec_ref, grad_mid_ref, gain_two_ref,
    input_ref, small_ref,
    w, sem,
):
    i = pl.program_id(0)

    @pl.when(i == 0)
    def _():
        fetch_pieces(tab, (g_a, g_b, g_c, g_d), 144, w, sem)
        small_ref[8:9, :] = jnp.zeros((1, WIDTH), F32)
        small_ref[9:10, :] = gain_two_ref[...]
        small_ref[10:16, :] = jnp.zeros((6, WIDTH), F32)
        finish(w, sem)

    y = jnp.zeros((256, WIDTH), F32)
    for half in (0, 1):
        cols = slice(half * 3 * LANES, (half + 1) * 3 * LANES)
        y = y + dot_last(grad_qkv_ref[:, cols], qkv_columns(w, half))
    xhat, scale = ln_stats(add_embed(x_ref[...], te_ref, i))
    grad = grad_mid_ref[...] + ln_back(y, vec_ref[0:1, :], xhat, scale)
    input_ref[...] = grad.astype(BF16)
    for s in range(2):
        small_ref[pl.ds(i * 2 + s, 1), :] = jnp.sum(
            grad[128 * s : 128 * s + 128], axis=0, keepdims=True
        )
    small_ref[8:9, :] += jnp.sum(y * xhat, axis=0, keepdims=True)


def input_backward(tab, pieces, grad_qkv, rows, embed, vectors, grad_mid, gain_two):
    row = tiles(256, WIDTH)
    return kernel_call(
        input_backward_kernel,
        grid=(4,),
        out_shape=(shaped((1024, WIDTH)), local((16, WIDTH), F32)),
        in_specs=[SMEM_SPEC]
        + [ANY_SPEC] * 4
        + [tiles(256, 3 * WIDTH), row, fixed(8, WIDTH), fixed(16, WIDTH), row, VMEM_SPEC],
        out_specs=(row, VMEM_SPEC),
        scratch_shapes=[pltpu.VMEM((CHIPS, 2, 144, LANES), BF16), pltpu.SemaphoreType.DMA],
        compiler_params=params(20),
        cost_estimate=cost(4_000_000_000, 18_000_000),
        name="input_backward",
    )(tab, *pieces, grad_qkv, rows, embed, vectors, grad_mid, gain_two)


def time_grads_kernel(tab, *refs):
    count = len(refs) - 10
    parts = refs[:count]
    wave_ref, hot_ref, hidden_ref, slope_ref, time_out_ref = refs[count : count + 5]
    tin_ref, tout_ref, sums_ref, every, sem = refs[count + 5 :]
    if count == 1:
        pltpu.make_async_copy(parts[0], every, sem).start()
    else:

        def fetch(src, chip, half):
            pltpu.make_async_copy(src, every.at[half * CHIPS + chip], sem).start()

        each_piece(tab, parts, fetch)
    finish(every, sem)
    grads = every[...].reshape(-1, WIDTH)
    tout_ref[...] = dot_first(hidden_ref[...], grads)
    grad_pre = dot_last(grads, time_out_ref[...]) * slope_ref[...]
    tin_ref[...] = dot_first(grad_pre.astype(BF16), wave_ref[...])
    sums_ref[...] = dot(hot_ref[...], grads)


def time_grads(tab, parts, wave, hot, hidden, slope, time_out):
    rows, width = time_out.shape
    devices = wave.shape[0] // 16
    return kernel_call(
        time_grads_kernel,
        out_shape=(
            shaped((rows, wave.shape[1]), F32), shaped((rows, width), F32), local((16, width), F32)
        ),
        in_specs=[SMEM_SPEC] + [ANY_SPEC] * len(parts) + [VMEM_SPEC] * 5,
        out_specs=(VMEM_SPEC,) * 3,
        scratch_shapes=[pltpu.VMEM((devices, 16, width), BF16), pltpu.SemaphoreType.DMA],
        compiler_params=params(40),
        cost_estimate=cost(50_000_000, 2_000_000),
        name="time_grads",
    )(tab, *parts, wave, hot, hidden, slope, time_out)


def pick(stacked, index):
    return lax.dynamic_index_in_dim(stacked, index, 0, keepdims=False)


def in_core_order(core, own, other, axis):
    return jnp.where(
        core == 0,
        jnp.concatenate([own, other], axis=axis),
        jnp.concatenate([other, own], axis=axis),
    )


def position_table(chip, core, order):
    index = jnp.arange(72, dtype=jnp.int32)
    side = jnp.bitwise_xor(core, (index // CHIPS) % 2)
    inner = index % CHIPS
    distance = jnp.bitwise_xor(inner, chip)
    there = jnp.zeros_like(index)
    back = jnp.zeros_like(index)
    for bit in range(4):
        mask = jnp.where(side == 0, order[0][bit], order[1][bit])
        there = there + jnp.where((inner >> bit) & 1 == 1, mask, 0)
        back = back + jnp.where(jnp.bitwise_and(distance, mask) != 0, 1 << bit, 0)
    moved = jnp.where(index < 32, jnp.bitwise_xor(there, chip), back)
    return jnp.where(index < 64, moved, core)


def lane_blocks(x, starts, step):
    return [
        jnp.concatenate([x[:, k + h * step : k + h * step + LANES] for k in starts], axis=0)
        for h in (0, 1)
    ]


def whole_columns(core, own, other, blocks):
    halves = (jnp.where(core == 0, own, other), jnp.where(core == 0, other, own))
    return [[half[24 * b : 24 * b + 24] for b in range(blocks)] for half in halves]


def swap_halves(halves, core):
    own = jnp.where(core == 0, halves[0], halves[1])
    return own, core_swap(jnp.where(core == 0, halves[1], halves[0]))


def join_rows(own, other, core, blocks):
    shape = (blocks, own.shape[0] // blocks, LANES)
    return in_core_order(core, own.reshape(shape), other.reshape(shape), 1).reshape(-1, LANES)


def split_rows(piece, blocks):
    rows = piece.reshape(blocks, 2, 24, LANES).transpose(1, 0, 2, 3)
    return rows.reshape(2, blocks * 24, LANES)


def pack_extra(time_in, vectors, ints):
    rows = time_in.shape[0]
    filler = jnp.zeros((rows, 128), BF16)
    vec = lax.dynamic_update_slice(filler, vectors, (0, 0))
    num = lax.dynamic_update_slice(filler, ints[None, :], (0, 0))
    return jnp.concatenate([time_in, vec, num], axis=1)


def split_time(timestep, dataset):
    steps = timestep.reshape(-1)
    return jnp.concatenate([steps // 64, steps % 64, dataset.reshape(-1)]).astype(BF16)


def gather_all(x):
    return lax.all_gather(x, AXES, axis=0, tiled=True)


def shards(
    block_input,
    out_grad,
    timestep,
    dataset,
    lengths,
    norm1_gain,
    qkv_weight,
    out_weight,
    norm2_gain,
    up_weight,
    down_weight,
    time_in,
    time_out,
    data_embed,
    devices,
):
    flat = lax.axis_index(AXES)
    exchange = devices == 2 * CHIPS
    vectors = jnp.concatenate([norm1_gain[None], norm2_gain[None], data_embed.T], axis=0)
    numbers = split_time(timestep, dataset)
    count = numbers.shape[0] // 3
    micros, seqs, seq_len, width = block_input.shape
    tokens = micros * seqs * seq_len
    x_rows = block_input.reshape(tokens, width)
    grad_rows = out_grad.reshape(tokens, width)
    features = sinusoid(timestep.reshape(-1), time_in.shape[1] // 2).astype(BF16)
    if exchange:
        core = flat & 1
        chip = flat >> 1

        wide = lane_blocks(qkv_weight, (0, WIDTH, 2 * WIDTH), LANES)
        slim = lane_blocks(time_out, (0,), LANES)
        own, other = swap_halves(
            [jnp.concatenate([x, y], axis=0) for x, y in zip(wide, slim)], core
        )
        attention_piece = jnp.concatenate(
            [
                join_rows(own[:72], other[:72], core, 3),
                join_rows(own[72:], other[72:], core, 1),
                pack_extra(time_in, vectors, numbers),
            ],
            axis=0,
        )[None]
        near = [chip_swap(attention_piece, p) for p in (1, 2, 3)]
        up_weight, out_weight, down_weight, flat = lax.optimization_barrier(
            (up_weight, out_weight, down_weight, flat, attention_piece)
        )[:4]
        tab = position_table(flat >> 1, flat & 1, LINE_FIRST)
        later_tab = position_table(flat >> 1, flat & 1, LINE_LATER)
        wide = lane_blocks(up_weight, range(0, 4 * LANES, LANES), 4 * LANES)
        slim = lane_blocks(out_weight, (0,), LANES)
        own, other = swap_halves(
            [jnp.concatenate([x, y], axis=0) for x, y in zip(wide, slim)], core
        )
        up_piece = jnp.concatenate(
            [join_rows(own[:96], other[:96], core, 4), join_rows(own[96:], other[96:], core, 1)],
            axis=0,
        )[None]
        own, other = swap_halves(lane_blocks(down_weight, (0,), LANES), core)
        down_piece = join_rows(own, other, core, 1)[None]
        down_pair = jnp.concatenate([down_piece, chip_swap(down_piece, 1, LINE_LATER)], axis=0)
        ready = (up_piece, down_pair, tab, later_tab, features)
        line = after(jnp.concatenate([attention_piece] + near, axis=0), *ready)
        plane = chip_swap(line, 4)
        up_near = [chip_swap(after(up_piece, line), p) for p in (1, 2)]
        plane, up_near = together(plane, up_near)
        held = jnp.concatenate([line, plane], axis=0)
        far = chip_swap(held, 8)
        up_near.append(chip_swap(after(up_piece, plane), 3))
        up_line = jnp.concatenate([up_piece] + up_near, axis=0)
        up_plane = chip_swap(up_line, 4)
        down_near = [chip_swap(after(down_pair, up_line), 2, LINE_LATER)]
        (far, up_plane), down_near = together((far, up_plane), down_near)
        attention_pieces = (held, far, core_swap(held), core_swap(far))
        up_held = jnp.concatenate([up_line, up_plane], axis=0)
        up_far = chip_swap(up_held, 8)
        down_last = [chip_swap(after(down_pair, up_held), p, LINE_LATER) for p in (4, 6)]
    else:
        tab = jnp.concatenate(
            [jnp.tile(jnp.arange(CHIPS, dtype=jnp.int32), 4), jnp.zeros((8,), jnp.int32)]
        )
        later_tab = tab
        full_qkv = gather_all(qkv_weight).reshape(CHIPS, 48, 3, 2, LANES)
        full_out = gather_all(out_weight).reshape(CHIPS, 48, 2, LANES)
        full_up = gather_all(up_weight).reshape(CHIPS, 48, 2, 4, LANES)
        full_down = gather_all(down_weight).reshape(CHIPS, 192, 2, LANES)
        full_tin = gather_all(time_in).reshape(CHIPS, 2, 16, 128)
        full_tout = gather_all(time_out).reshape(CHIPS, 32, 2, LANES)
        full_vec = lax.all_gather(vectors, AXES, axis=1, tiled=True).reshape(4, CHIPS, 2, 24)
        numbers_all = gather_all(numbers[None])
        extra = jnp.zeros((CHIPS, 2, 16, LANES), BF16)
        extra = extra.at[:, :, :, :128].set(full_tin)
        extra = extra.at[:, :, 0:4, 128:152].set(full_vec.transpose(1, 2, 0, 3))
        attention_pieces = []
        down_pieces = []
        up_pieces = []
        for half in (0, 1):
            wide = full_qkv[:, :, :, half].transpose(0, 2, 1, 3).reshape(CHIPS, 144, LANES)
            whole = jnp.concatenate([wide, full_tout[:, :, half], extra[:, half]], axis=1)
            attention_pieces += [whole[:8], whole[8:]]
            down_pieces += [full_down[:8, :, half], full_down[8:, :, half]]
            wide = full_up[:, :, half].transpose(0, 2, 1, 3).reshape(CHIPS, 192, LANES)
            whole = jnp.concatenate([wide, full_out[:, :, half]], axis=1)
            up_pieces += [whole[:8], whole[8:]]

    arrivals = []
    if exchange:
        x_rows = after(x_rows, up_held)
        arrivals = [up_far]
    forward = attention_forward(tab, lengths, dataset, attention_pieces, x_rows, features)
    (normed, qkv, embed, vecs, seen, probs, att), arrivals = together(forward, arrivals)
    seen = seen[:, :, 0, : 3 * count].reshape(2 * CHIPS, 3 * count) if exchange else numbers_all
    steps = seen[:, :count] * 64 + seen[:, count : 2 * count].astype(F32)
    wave = sinusoid(steps.reshape(-1), time_in.shape[1] // 2).astype(BF16)
    wave = jnp.pad(wave.reshape(devices, count, -1), ((0, 0), (0, 16 - count), (0, 0)))
    wave = wave.reshape(devices * 16, -1)
    which = jnp.pad(seen[:, 2 * count :], ((0, 0), (0, 16 - count))).reshape(-1)
    place = jnp.tile(jnp.arange(16), devices)
    hot = jnp.stack(
        [(place < count) & (which == 0), (place < count) & (which == 1), place == 8, place == 9]
    )
    hot = jnp.pad(hot.astype(BF16), ((0, 12), (0, 0)))
    pre = dot_last(wave, time_in)
    gate = 1.0 / (1.0 + jnp.exp(-pre))
    hidden = (pre * gate).astype(BF16)
    slope_pre = gate * (1.0 + pre * (1.0 - gate))
    if exchange:
        (up_far,) = arrivals
        down_near = down_near + [after(x, embed) for x in down_last]
        up_pieces = (up_held, up_far, core_swap(up_held), core_swap(up_far))
        down_held = jnp.concatenate([down_pair] + down_near, axis=0)
        att, wave, hot, hidden, slope_pre, down_held = lax.optimization_barrier(
            (att, wave, hot, hidden, slope_pre, down_held)
        )
        arrivals = chip_swap(down_held, 8, LINE_LATER)
    forward = up_forward(tab, up_pieces, att, x_rows, grad_rows, embed, vecs)
    (mid, two, act, slope, down_theirs), arrivals = together(forward, arrivals)
    if exchange:
        down_far = arrivals
        down_sum = Scatter(down_theirs)
        arrivals = [core_swap(down_held), core_swap(down_far)], down_sum.swap()
    (down_mine, act), arrivals = together(down_grad(tab, act, grad_rows), arrivals)
    if exchange:
        down_pieces = (down_held, down_far, *arrivals[0])
        down_sum.land(arrivals[1], down_mine)
        slope = after(slope, *down_sum.send())
        arrivals = down_sum.fly()
    backward = mlp_backward(
        tab, later_tab, up_pieces, down_pieces, two, att, slope, grad_rows, mid, vecs
    )
    backward, arrivals = together(backward, arrivals)
    grad_mid, branch, grad_up, grad_att, gain_two, up_theirs = backward
    if exchange:
        down_sum.land(arrivals)
        up_sum = Scatter(up_theirs)
        grad_up = after(grad_up, *down_sum.send())
        arrivals = down_sum.fly(), up_sum.swap()
    up_mine, arrivals = together(up_grad(tab, att, branch, two, grad_up), arrivals)
    if exchange:
        down_sum.land(arrivals[0])
        up_sum.land(arrivals[1], up_mine)
        grad_att = after(grad_att, *up_sum.send(), *down_sum.send())
        arrivals = up_sum.fly(), down_sum.fly()
    backward = attention_backward(tab, normed, qkv, probs, grad_att)
    (grad_qkv, mine_qkv, att_theirs), arrivals = together(backward, arrivals)
    if exchange:
        up_sum.land(arrivals[0])
        down_sum.land(arrivals[1])
        down_total = down_sum.total()
        att_sum = Scatter(att_theirs)
        mine_qkv = after(mine_qkv, *up_sum.send(), down_total)
        arrivals = up_sum.fly(), att_sum.swap()
    backward = qkv_grad(tab, later_tab, down_pieces, normed, mine_qkv, act, mid)
    (att_mine, result), arrivals = together(backward, arrivals)
    if exchange:
        up_sum.land(arrivals[0])
        att_sum.land(arrivals[1], att_mine)
        grad_qkv = after(grad_qkv, *att_sum.send(), *up_sum.send())
        arrivals = att_sum.fly(), up_sum.fly()
    backward = input_backward(
        tab, attention_pieces, grad_qkv, x_rows, embed, vecs, grad_mid, gain_two
    )
    (grad_input, small), arrivals = together(backward, arrivals)

    small = small.astype(BF16)[None]
    if exchange:
        att_sum.land(arrivals[0])
        up_sum.land(arrivals[1])
        att_sum.send()
        brought, near = together(att_sum.fly(), [chip_swap(small, p) for p in (1, 2, 3)])
        att_sum.land(brought)
        small_line = jnp.concatenate([small] + near, axis=0)
        held = gather_plane(small_line)
        att_sum.send()
        far = chip_swap(held, 8)
        every = (held, far, core_swap(held), core_swap(far))
        att_sum.land(att_sum.fly())
    else:
        every = (gather_all(small),)
    grad_tin, grad_tout, sums = time_grads(tab, every, wave, hot, hidden, slope_pre, time_out)
    own_cols = norm1_gain.shape[0]
    sums = lax.dynamic_slice_in_dim(sums, flat * own_cols, own_cols, 1)

    if exchange:
        own, other = swap_halves(after(down_total, small_line).reshape(2, 96, LANES), core)
        grad_down = in_core_order(core, own, other, 1)
        piece = after(up_sum.total(), small_line)
        out_rows = piece[192:].reshape(2, 24, LANES)
        own, other = swap_halves(
            jnp.concatenate([split_rows(piece[:192], 4), out_rows], axis=1), core
        )
        left, right = whole_columns(core, own, other, 5)
        grad_up_weight = jnp.concatenate(left[:4] + right[:4], axis=1)
        grad_out = jnp.concatenate([left[4], right[4]], axis=1)
        own, other = swap_halves(split_rows(att_sum.total(), 3), core)
        left, right = whole_columns(core, own, other, 3)
        grad_qkv_weight = jnp.concatenate(
            [side[sec] for sec in range(3) for side in (left, right)], axis=1
        )
    else:
        scatter = partial(lax.psum_scatter, axis_name=AXES, scatter_dimension=0, tiled=True)
        both = jnp.stack([down_mine, down_theirs]).astype(F32)
        grad_down = scatter(both.transpose(1, 2, 0, 3).reshape(FF, WIDTH))
        both = jnp.stack([up_mine, up_theirs]).astype(F32)
        grad_out = scatter(both[:, :, 192:].transpose(1, 2, 0, 3).reshape(WIDTH, WIDTH))
        both = both[:, :, :192].reshape(2, CHIPS, 4, 48, LANES)
        grad_up_weight = scatter(both.transpose(1, 3, 0, 2, 4).reshape(WIDTH, FF))
        both = jnp.stack([att_mine, att_theirs]).astype(F32).reshape(2, CHIPS, 3, 48, LANES)
        grad_qkv_weight = scatter(both.transpose(1, 3, 2, 0, 4).reshape(WIDTH, 3 * WIDTH))

    return (
        result.reshape(block_input.shape),
        grad_input.reshape(block_input.shape),
        sums[2],
        grad_qkv_weight,
        grad_out,
        sums[3],
        grad_up_weight,
        grad_down,
        grad_tin,
        grad_tout,
        sums[:2].T,
    )


def solution(mesh):
    devices = mesh.shape["dp"] * mesh.shape["fsdp"]
    seq_spec = P(None, AXES, None, None)
    int_spec = P(None, AXES)
    row_spec = P(AXES, None)
    in_specs = (seq_spec, seq_spec, int_spec, int_spec, int_spec, P(AXES), row_spec, row_spec, P(AXES))
    in_specs = in_specs + (row_spec,) * 5
    out_specs = (seq_spec, seq_spec, P(AXES), row_spec, row_spec, P(AXES)) + (row_spec,) * 5
    return jax.shard_map(
        partial(shards, devices=devices),
        mesh=mesh,
        in_specs=in_specs,
        out_specs=out_specs,
        check_vma=False,
    )
```

```python
from functools import partial
import math

import jax
import jax.numpy as jnp
from jax import lax
from jax.experimental import pallas as pl
from jax.experimental.pallas import tpu as pltpu
from jax.sharding import PartitionSpec as P

HEAD_DIM = 64
AXES = ("dp", "fsdp")
LANES = 384
CHIPS = 16
WIDTH = 768
FF = 3072
F32 = jnp.float32
BF16 = jnp.bfloat16
NEG = -1000000000.0


def sinusoid(timestep, half_width):
    frequency = jnp.exp(-math.log(10000.0) * jnp.arange(half_width, dtype=F32) / half_width)
    angles = timestep.astype(F32)[:, None] * frequency[None, :]
    return jnp.concatenate([jnp.cos(angles), jnp.sin(angles)], axis=-1)


def dot(left, right):
    return jnp.dot(left, right, preferred_element_type=F32)


def dot_last(left, right):
    return lax.dot_general(left, right, (((1,), (1,)), ((), ())), preferred_element_type=F32)


def dot_first(left, right):
    return lax.dot_general(left, right, (((0,), (0,)), ((), ())), preferred_element_type=F32)


def positions(masks):
    return [sum(masks[b] for b in range(4) if (p >> b) & 1) for p in range(CHIPS)]


LINE_FIRST = ((2, 1, 8, 4), (2, 1, 4, 8))
LINE_LATER = ((8, 2, 1, 4), (4, 2, 1, 8))


def core_swap(x):
    return lax.ppermute(x, AXES, [(i, i ^ 1) for i in range(2 * CHIPS)])


def chip_swap(x, position, order=LINE_FIRST):
    far = [positions(masks)[position] * 2 for masks in order]
    return lax.ppermute(x, AXES, [(i, i ^ far[i & 1]) for i in range(2 * CHIPS)])


def after(x, *others):
    return lax.optimization_barrier((x,) + others)[0]


def gather_line(piece):
    return jnp.concatenate([piece] + [chip_swap(piece, p) for p in (1, 2, 3)], axis=0)


def gather_plane(held):
    return jnp.concatenate([held, chip_swap(held, 4)], axis=0)


def together(outs, arrivals):
    return lax.optimization_barrier((outs, arrivals))


class Scatter:
    def __init__(self, theirs):
        self.parts = []
        self.steps = [(8,), (4,), (1, 2, 3)]
        self.theirs = theirs

    def swap(self):
        return [core_swap(self.theirs)]

    def land(self, brought, *own):
        self.parts += [*brought, *own]

    def sum(self, start, stop):
        total = self.parts[0][start:stop].astype(F32)
        for part in self.parts[1:]:
            total = total + part[start:stop].astype(F32)
        return total

    def send(self):
        self.at = self.steps.pop(0)
        size = 1 if len(self.at) == 3 else self.at[0]
        self.sent = [self.sum(p, p + size).astype(BF16) for p in self.at]
        self.parts = [self.sum(0, size)]
        return [*self.sent, self.parts[0]]

    def fly(self):
        return [chip_swap(x, p) for x, p in zip(self.sent, self.at)]

    def total(self):
        return self.sum(0, 1)[0]


VMEM_SPEC = pl.BlockSpec(memory_space=pltpu.VMEM)
SMEM_SPEC = pl.BlockSpec(memory_space=pltpu.SMEM)
ANY_SPEC = pl.BlockSpec(memory_space=pl.ANY)


def tiles(rows, cols):
    return pl.BlockSpec((rows, cols), lambda i: (i, 0))


def columns(rows, cols):
    return pl.BlockSpec((rows, cols), lambda i: (0, i))


def fixed(*shape):
    return pl.BlockSpec(shape, lambda i: (0,) * len(shape))


def shaped(shape, dtype=BF16):
    return pltpu.HBM(shape, dtype)


def local(shape, dtype=BF16):
    return pltpu.VMEM(shape, dtype)


def params(mib):
    return pltpu.CompilerParams(vmem_limit_bytes=mib * 1024 * 1024)


def kernel_call(kernel, **kwargs):
    call = pl.pallas_call(kernel, **kwargs)
    if "grid_spec" in kwargs:
        grid_spec = kwargs["grid_spec"]
        specs = [SMEM_SPEC] * grid_spec.num_scalar_prefetch + list(grid_spec.in_specs)
    else:
        specs = kwargs["in_specs"]

    def place(x, spec):
        if spec is SMEM_SPEC:
            return x
        space = pltpu.VMEM if spec is VMEM_SPEC else pltpu.HBM
        return pltpu.with_memory_space_constraint(x, space)

    def run(*operands):
        return call(*[place(x, spec) for x, spec in zip(operands, specs, strict=True)])

    return run


def cost(flops, nbytes, transcendentals=0):
    return pl.CostEstimate(flops=flops, bytes_accessed=nbytes, transcendentals=transcendentals)


def ln_stats(v):
    center = v - jnp.mean(v, axis=-1, keepdims=True)
    scale = lax.rsqrt(jnp.mean(center * center, axis=-1, keepdims=True) + 1e-05)
    return center * scale, scale


def ln_back(y, gain, xhat, scale):
    yg = y * gain
    return scale * (
        yg - jnp.mean(yg, axis=-1, keepdims=True) - xhat * jnp.mean(yg * xhat, axis=-1, keepdims=True)
    )


def first_core(tab):
    return tab[64]


def each_piece(tab, parts, fn):
    core = first_core(tab)
    for side in (0, 1):
        half = core if side == 0 else 1 - core
        for group in (0, 1):
            part = parts[side * 2 + group]

            def body(q, _, part=part, side=side, group=group, half=half):
                chip = tab[side * CHIPS + group * 8 + q]
                fn(part.at[q], chip, half)
                return 0

            lax.fori_loop(0, 8, body, 0)


def rows_of(chip, size):
    return pl.ds(pl.multiple_of(chip * size, size), size)


def lanes_of(half, size, base=0):
    return pl.ds(pl.multiple_of(half * size + base, 128), LANES)


def fetch_pieces(tab, parts, rows, dst, sem, first=0):
    each_piece(
        tab,
        parts,
        lambda src, chip, half: pltpu.make_async_copy(
            src.at[pl.ds(first, rows), :], dst.at[chip, half], sem
        ).start(),
    )


def block(pieces, half, first, rows=48):
    return pieces[:, half, first : first + rows, :].reshape(CHIPS * rows, LANES)


def both_halves(pieces, first, rows=48):
    return jnp.concatenate([block(pieces, h, first, rows) for h in (0, 1)], axis=1)


def down_rows(pieces, j):
    chips = pl.ds(4 * j, 4)
    return jnp.concatenate([pieces[chips, h].reshape(WIDTH, LANES) for h in (0, 1)], axis=1)


def qkv_columns(pieces, half):
    return jnp.concatenate([block(pieces, half, 48 * sec) for sec in range(3)], axis=1)


def finish(ref, sem):
    pltpu.make_async_copy(ref, ref, sem).wait()


def add_embed(x, embed, i):
    seqs = x.shape[0] // 128
    parts = [
        x[128 * k : 128 * k + 128].astype(F32) + embed[pl.ds(i * seqs + k, 1), :]
        for k in range(seqs)
    ]
    return jnp.concatenate(parts, axis=0)


def two_heads(x, low_half):
    none = jnp.zeros_like(x)
    return jnp.concatenate([jnp.where(low_half, x, none), jnp.where(low_half, none, x)], axis=0)


def side_by_side(x):
    return jnp.concatenate([x[:128], x[128:]], axis=1)


def pair_base(pair):
    return (pair // 3) * 3 * LANES + (pair % 3) * 128


def attention_tile(lengths, qkv_ref, probs_ref, att_ref):
    low_half = lax.broadcasted_iota(jnp.int32, (128, 128), 1) < HEAD_DIM
    lane = lax.broadcasted_iota(jnp.int32, (256, 128), 1)
    keep = [lane < length for length in lengths]
    units = [(k, pair) for k in range(2) for pair in range(6)]

    def part(k, pair, section):
        base = pair_base(pair) + section * LANES
        return qkv_ref[128 * k : 128 * k + 128, base : base + 128]

    scores = []
    for k, pair in units:
        query = two_heads(part(k, pair, 0), low_half)
        score = dot_last(query, part(k, pair, 1)) * HEAD_DIM ** (-0.5)
        scores.append(jnp.where(keep[k], score, NEG))
    probs = []
    for (k, pair), score in zip(units, scores):
        shifted = jnp.exp(score - jnp.max(score, axis=-1, keepdims=True))
        total = jnp.sum(shifted, axis=-1, keepdims=True)
        probs.append((shifted * (1.0 / total)).astype(BF16))
        first = 256 * (6 * k + pair)
        probs_ref[first : first + 256, :] = probs[-1]
    for (k, pair), prob in zip(units, probs):
        value = two_heads(part(k, pair, 2), low_half)
        att_ref[128 * k : 128 * k + 128, pair * 128 : pair * 128 + 128] = dot(
            side_by_side(prob), value
        ).astype(BF16)


def attention_kernel(
    tab, lens, sets, g_a, g_b, g_c, g_d, x_ref, feat_ref,
    normed_ref, qkv_ref, te_ref, vec_ref, seen_ref, probs_ref, att_ref,
    w, w_time, sem, sem_time,
):
    i = pl.program_id(0)

    @pl.when(i == 0)
    def _():
        fetch_pieces(tab, (g_a, g_b, g_c, g_d), 48, w_time, sem_time, 144)
        fetch_pieces(tab, (g_a, g_b, g_c, g_d), 144, w, sem)
        finish(w_time, sem_time)
        lane = lax.broadcasted_iota(jnp.int32, (128, WIDTH), 1)
        spread = (lax.broadcasted_iota(jnp.int32, (128, WIDTH), 0) == lane % 24).astype(BF16)
        vectors = jnp.zeros((16, WIDTH), F32)
        embed = jnp.zeros((8, WIDTH), F32)
        for owner in (0, 1):
            extra = block(w_time, owner, 32, 16)
            wide = dot(extra[:, 128:256], spread)
            chip = lax.broadcasted_iota(jnp.int32, (256, WIDTH), 0) // 16
            place = lax.broadcasted_iota(jnp.int32, (256, WIDTH), 1) // 24
            wide = jnp.where(place == chip * 2 + owner, wide, 0.0)
            vectors = vectors + jnp.sum(wide.reshape(CHIPS, 16, WIDTH), axis=0)
            pre = dot_last(feat_ref[...], extra[:, 0:128])
            hidden = (pre / (1.0 + jnp.exp(-pre))).astype(BF16)
            embed = embed + dot(hidden, both_halves(w_time, 16 * owner, 16))
            seen_ref[owner] = w_time[:, owner, 32:48, 256:]
        vec_ref[...] = vectors
        for s in range(8):
            chosen = jnp.where(sets[s // 4, s % 4] == 1, vectors[3:4, :], vectors[2:3, :])
            te_ref[s : s + 1, :] = embed[s : s + 1, :] + chosen

    xhat, _unused = ln_stats(add_embed(x_ref[...], te_ref, i))
    normed_ref[...] = (xhat * vec_ref[0:1, :]).astype(BF16)

    @pl.when(i == 0)
    def _():
        finish(w, sem)

    for half in (0, 1):
        cols = slice(half * 3 * LANES, (half + 1) * 3 * LANES)
        qkv_ref[:, cols] = dot(normed_ref[...], qkv_columns(w, half)).astype(BF16)
    lengths = [lens[i // 2, i % 2 * 2 + k] for k in range(2)]
    attention_tile(lengths, qkv_ref, probs_ref, att_ref)


def attention_forward(tab, lens, sets, pieces, rows, features):
    row = tiles(256, WIDTH)
    return kernel_call(
        attention_kernel,
        grid=(4,),
        out_shape=(
            shaped((1024, WIDTH)),
            shaped((1024, 3 * WIDTH)),
            shaped((8, WIDTH), F32),
            shaped((16, WIDTH), F32),
            shaped((2, CHIPS, 16, 128)),
            shaped((48 * 256, 128)),
            shaped((1024, WIDTH)),
        ),
        in_specs=[SMEM_SPEC] * 3 + [ANY_SPEC] * 4 + [row, fixed(8, 128)],
        out_specs=(
            row, tiles(256, 3 * WIDTH), fixed(8, WIDTH), fixed(16, WIDTH),
            fixed(2, CHIPS, 16, 128), tiles(12 * 256, 128), row,
        ),
        scratch_shapes=[
            pltpu.VMEM((CHIPS, 2, 144, LANES), BF16),
            pltpu.VMEM((CHIPS, 2, 48, LANES), BF16),
            pltpu.SemaphoreType.DMA,
            pltpu.SemaphoreType.DMA,
        ],
        compiler_params=params(26),
        cost_estimate=cost(8_000_000_000, 20_000_000, 1_600_000),
        name="attention_forward",
    )(tab, lens, sets, *pieces, rows, features)


def gelu_parts(u):
    cdf = 0.5 + 0.5 * lax.erf(u * math.sqrt(0.5))
    return cdf, jnp.exp(u * u * -0.5) * (1.0 / math.sqrt(2.0 * math.pi))


def up_columns(pieces, half, j):
    return jnp.concatenate(
        [block(pieces, half, 96 * j), block(pieces, half, 96 * j + 48)], axis=1
    )


def half_of(tab, side):
    return first_core(tab) if side == 0 else 1 - first_core(tab)


def clamped(rows, cols):
    return pl.BlockSpec((rows, cols), lambda i: (jnp.minimum(i, 3), 0))


def down_grad_rows(tab, side, j, act, out_grad, out_ref):
    lanes = lanes_of(half_of(tab, side), LANES)
    grad = dot_first(act, out_grad[:, lanes]).astype(BF16)
    for k in range(4):
        place = tab[32 + side * CHIPS + j * 4 + k]
        out_ref[place, :, :] = grad[192 * k : 192 * k + 192, :]


def up_kernel(
    tab, u_a, u_b, u_c, u_d, out_grad_ref, att_ref, x_ref, te_ref, vec_ref,
    mid_ref, two_ref, act_ref, slope_ref, theirs_ref,
    w, w_out, sem, sem_out,
):
    i = pl.program_id(0)
    parts = (u_a, u_b, u_c, u_d)

    def token_rows(arrived):
        rows = rows_of(i, 256)
        mid = add_embed(x_ref[...], te_ref, i) + dot(att_ref[...], both_halves(w_out, 0))
        mid_ref[...] = mid
        xhat, _unused = ln_stats(mid)
        two = (xhat * vec_ref[1:2, :]).astype(BF16)
        two_ref[...] = two
        arrived()
        for j in range(4):
            up = dot(two, up_columns(w, j // 2, j % 2))
            cdf, density = gelu_parts(up)
            act_ref[j, rows, :] = (up * cdf).astype(BF16)
            slope_ref[j, rows, :] = (cdf + up * density).astype(BF16)

    @pl.when(i == 0)
    def _():
        fetch_pieces(tab, parts, 48, w_out, sem_out, 192)
        fetch_pieces(tab, parts, 192, w, sem)
        finish(w_out, sem_out)
        token_rows(lambda: finish(w, sem))

    @pl.when((i > 0) & (i < 4))
    def _():
        token_rows(lambda: None)

    @pl.when(i >= 4)
    def _():
        down_grad_rows(tab, 1, i - 4, act_ref[i - 4], out_grad_ref, theirs_ref)


def up_forward(tab, pieces, att, rows, out_grad, embed, vectors):
    row = clamped(256, WIDTH)
    return kernel_call(
        up_kernel,
        grid=(8,),
        out_shape=(
            shaped((1024, WIDTH), F32),
            shaped((1024, WIDTH)),
            local((4, 1024, WIDTH)),
            local((4, 1024, WIDTH)),
            local((CHIPS, 192, LANES)),
        ),
        in_specs=[SMEM_SPEC]
        + [ANY_SPEC] * 4
        + [VMEM_SPEC, row, row, fixed(8, WIDTH), fixed(16, WIDTH)],
        out_specs=(row, row) + (VMEM_SPEC,) * 3,
        scratch_shapes=[
            pltpu.VMEM((CHIPS, 2, 192, LANES), BF16),
            pltpu.VMEM((CHIPS, 2, 48, LANES), BF16),
            pltpu.SemaphoreType.DMA,
            pltpu.SemaphoreType.DMA,
        ],
        compiler_params=params(26),
        cost_estimate=cost(10_000_000_000, 30_000_000, 6_000_000),
        name="up_forward",
    )(tab, *pieces, out_grad, att, rows, embed, vectors)


def down_grad_kernel(tab, act_ref, out_grad_ref, _slope, out_ref, act_hbm, _slope_out, sem):
    j = pl.program_id(0)

    @pl.when(j == 0)
    def _():
        pltpu.make_async_copy(act_ref, act_hbm, sem).start()

    down_grad_rows(tab, 0, j, act_ref[j], out_grad_ref, out_ref)

    @pl.when(j == 3)
    def _():
        pltpu.make_async_copy(act_ref, act_hbm, sem).wait()


def down_grad(tab, act, out_grad, slope):
    return kernel_call(
        down_grad_kernel,
        grid=(4,),
        out_shape=(
            local((CHIPS, 192, LANES)), shaped((4, 1024, WIDTH)), local((4, 1024, WIDTH))
        ),
        in_specs=[SMEM_SPEC] + [VMEM_SPEC] * 3,
        out_specs=(VMEM_SPEC, ANY_SPEC, VMEM_SPEC),
        input_output_aliases={3: 2},
        scratch_shapes=[pltpu.SemaphoreType.DMA],
        compiler_params=params(12),
        cost_estimate=cost(3_000_000_000, 10_000_000),
        name="down_grad",
    )(tab, act, out_grad, slope)


def store_blocks(tab, side, target, first, part, lanes):
    for chip in range(CHIPS):
        place = tab[32 + side * CHIPS + chip]
        target[place, pl.ds(first, 48), :] = part[48 * chip : 48 * chip + 48, lanes]


def out_grad_rows(tab, side, att, branch, out_ref, part):
    lanes = lanes_of(half_of(tab, side), LANES)
    part[:, 0:LANES] = dot_first(att[...], branch[:, lanes]).astype(BF16)
    store_blocks(tab, side, out_ref, 192, part, slice(0, LANES))


def up_grad_rows(tab, side, j, two, grad_up, out_ref, part):
    part[...] = dot_first(two, grad_up).astype(BF16)
    for b in range(2):
        first = pl.multiple_of((2 * j + b) * 48, 48)
        store_blocks(tab, side, out_ref, first, part, slice(b * LANES, (b + 1) * LANES))


def up_grad_kernel(
    tab, att_hbm, two_hbm, branch_ref, grad_up_ref, out_ref, att, two, part, sem_att, sem_two
):
    j = pl.program_id(0)

    @pl.when(j == 0)
    def _():
        pltpu.make_async_copy(att_hbm, att, sem_att).start()
        pltpu.make_async_copy(two_hbm, two, sem_two).start()
        finish(att, sem_att)
        out_grad_rows(tab, 0, att, branch_ref, out_ref, part)
        finish(two, sem_two)

    @pl.when(j > 0)
    def _():
        up_grad_rows(tab, 0, j - 1, two[...], grad_up_ref[j - 1], out_ref, part)


def up_grad(tab, att, branch, two, grad_up):
    return kernel_call(
        up_grad_kernel,
        grid=(3,),
        out_shape=local((CHIPS, 240, LANES)),
        in_specs=[SMEM_SPEC] + [ANY_SPEC] * 2 + [VMEM_SPEC] * 2,
        out_specs=VMEM_SPEC,
        scratch_shapes=[pltpu.VMEM((1024, WIDTH), BF16)] * 2
        + [pltpu.VMEM((WIDTH, WIDTH), BF16)]
        + [pltpu.SemaphoreType.DMA] * 2,
        compiler_params=params(16),
        cost_estimate=cost(3_200_000_000, 11_000_000),
        name="up_grad",
    )(tab, att, two, branch, grad_up)


def mlp_backward_kernel(
    tab, later_tab, u_a, u_b, u_c, u_d, d_a, d_b, d_c, d_d,
    two_hbm, att_hbm, slope_ref, out_grad_ref, mid_ref, vec_ref,
    grad_mid_ref, branch_ref, mine_up_ref, grad_att_ref, gain_ref, theirs_ref,
    w, w_down, two, att, theirs_up, part, sem, sem_down, sem_two, sem_att,
):
    i = pl.program_id(0)
    grad_up = [
        (half_of(tab, side), j, target)
        for side, target in enumerate((mine_up_ref, theirs_up))
        for j in range(2)
    ]

    @pl.when(i == 0)
    def _():
        fetch_pieces(later_tab, (d_a, d_b, d_c, d_d), 192, w_down, sem_down)
        gain_ref[...] = jnp.zeros_like(gain_ref)
        finish(w_down, sem_down)
        fetch_pieces(tab, (u_a, u_b, u_c, u_d), 240, w, sem)

    @pl.when(i < 4)
    def _():
        rows = rows_of(i, 256)
        for half, j, target in grad_up:
            grad_act = dot_last(out_grad_ref[rows, :], down_rows(w_down, 2 * half + j))
            slope = slope_ref[2 * half + j, rows, :].astype(F32)
            target[j, rows, :] = (grad_act * slope).astype(BF16)

    @pl.when(i == 4)
    def _():
        finish(w, sem)
        pltpu.make_async_copy(two_hbm, two, sem_two).start()
        pltpu.make_async_copy(att_hbm, att, sem_att).start()

    @pl.when((i >= 4) & (i < 8))
    def _():
        rows = rows_of(i - 4, 256)
        y = jnp.zeros((256, WIDTH), F32)
        for half, j, target in grad_up:
            y = y + dot_last(target[j, rows, :], up_columns(w, half, j))
        xhat, scale = ln_stats(mid_ref[...])
        grad = out_grad_ref[rows, :].astype(F32) + ln_back(y, vec_ref[1:2, :], xhat, scale)
        grad_mid_ref[...] = grad
        branch = grad.astype(BF16)
        branch_ref[rows, :] = branch
        gain_ref[...] += jnp.sum(y * xhat, axis=0, keepdims=True)
        grad_att_ref[rows, :] = dot_last(branch, both_halves(w, 192)).astype(BF16)

    @pl.when(i == 8)
    def _():
        finish(two, sem_two)
        finish(att, sem_att)
        out_grad_rows(tab, 1, att, branch_ref, theirs_ref, part)

    @pl.when(i >= 8)
    def _():
        up_grad_rows(tab, 1, i - 8, two[...], theirs_up[i - 8], theirs_ref, part)


def mlp_backward(
    tab, later_tab, up_pieces, down_pieces, two, att, slope, out_grad, mid, vectors
):
    row = pl.BlockSpec((256, WIDTH), lambda i: (jnp.clip(i - 4, 0, 3), 0))
    return kernel_call(
        mlp_backward_kernel,
        grid=(10,),
        out_shape=(
            shaped((1024, WIDTH), F32),
            local((1024, WIDTH)),
            local((2, 1024, WIDTH)),
            local((1024, WIDTH)),
            local((1, WIDTH), F32),
            local((CHIPS, 240, LANES)),
        ),
        in_specs=[SMEM_SPEC] * 2
        + [ANY_SPEC] * 10
        + [VMEM_SPEC] * 2
        + [row, fixed(16, WIDTH)],
        out_specs=(row,) + (VMEM_SPEC,) * 5,
        scratch_shapes=[
            pltpu.VMEM((CHIPS, 2, 240, LANES), BF16),
            pltpu.VMEM((CHIPS, 2, 192, LANES), BF16),
            pltpu.VMEM((1024, WIDTH), BF16),
            pltpu.VMEM((1024, WIDTH), BF16),
            pltpu.VMEM((2, 1024, WIDTH), BF16),
            pltpu.VMEM((WIDTH, WIDTH), BF16),
        ]
        + [pltpu.SemaphoreType.DMA] * 4,
        compiler_params=params(38),
        cost_estimate=cost(18_000_000_000, 50_000_000),
        name="mlp_backward",
    )(tab, later_tab, *up_pieces, *down_pieces, two, att, slope, out_grad, mid, vectors)


def attention_backward_tile(first_row, qkv_ref, probs_ref, grad_att_ref, grad_qkv_ref):
    low_half = lax.broadcasted_iota(jnp.int32, (128, 128), 1) < HEAD_DIM
    units = [(k, pair) for k in range(2) for pair in range(6)]

    def rows(k):
        return slice(128 * k, 128 * k + 128)

    def part(k, pair, section):
        base = pair_base(pair) + section * LANES
        return qkv_ref[rows(k), base : base + 128]

    def up(k, pair):
        whole = pl.ds(pl.multiple_of(first_row + 128 * k, 128), 128)
        return two_heads(grad_att_ref[whole, pair * 128 : pair * 128 + 128], low_half)

    def probs_of(k, pair):
        first = 256 * (6 * k + pair)
        return probs_ref[first : first + 256, :]

    def store(k, pair, section, value):
        base = pair_base(pair) + section * LANES
        grad_qkv_ref[rows(k), base : base + 128] = value.astype(BF16)

    grad_probs = [dot_last(up(k, pair), part(k, pair, 2)) for k, pair in units]
    grad_scores = []
    for (k, pair), grad in zip(units, grad_probs):
        probs = probs_of(k, pair).astype(F32)
        inner = jnp.sum(probs * grad, axis=-1, keepdims=True)
        grad_scores.append((probs * (grad - inner)).astype(BF16))
    for (k, pair), grad in zip(units, grad_scores):
        grad_query = dot(side_by_side(grad), two_heads(part(k, pair, 1), low_half))
        store(k, pair, 0, grad_query * HEAD_DIM ** (-0.5))
        grad_key = dot_first(grad, two_heads(part(k, pair, 0), low_half))
        store(k, pair, 1, grad_key * HEAD_DIM ** (-0.5))
        store(k, pair, 2, dot_first(probs_of(k, pair), up(k, pair)))


def qkv_grad_rows(tab, side, normed, grad_qkv, out_ref, part):
    part[...] = dot_first(normed, grad_qkv).astype(BF16)
    for sec in range(3):
        store_blocks(tab, side, out_ref, 48 * sec, part, slice(sec * LANES, (sec + 1) * LANES))


def attention_backward_kernel(
    tab, normed_hbm, qkv_ref, probs_ref, grad_att_ref, grad_qkv_ref, mine_ref, theirs_ref,
    normed, kept, part, sem,
):
    i = pl.program_id(0)

    @pl.when(i == 0)
    def _():
        pltpu.make_async_copy(normed_hbm, normed, sem).start()

    @pl.when(i < 4)
    def _():
        attention_backward_tile(i * 256, qkv_ref, probs_ref, grad_att_ref, grad_qkv_ref)
        for side, target in enumerate((mine_ref, kept)):
            lanes = pl.ds(pl.multiple_of(half_of(tab, side) * 3 * LANES, 128), 3 * LANES)
            target[rows_of(i, 256), :] = grad_qkv_ref[:, lanes]

    @pl.when(i == 4)
    def _():
        finish(normed, sem)
        qkv_grad_rows(tab, 1, normed[...], kept[...], theirs_ref, part)


def attention_backward(tab, normed, qkv, probs, grad_att):
    wide = clamped(256, 3 * WIDTH)
    return kernel_call(
        attention_backward_kernel,
        grid=(5,),
        out_shape=(
            shaped((1024, 3 * WIDTH)), local((1024, 3 * LANES)), local((CHIPS, 144, LANES))
        ),
        in_specs=[SMEM_SPEC, ANY_SPEC, wide, clamped(12 * 256, 128), VMEM_SPEC],
        out_specs=(wide, VMEM_SPEC, VMEM_SPEC),
        scratch_shapes=[
            pltpu.VMEM((1024, WIDTH), BF16),
            pltpu.VMEM((1024, 3 * LANES), BF16),
            pltpu.VMEM((WIDTH, 3 * LANES), BF16),
            pltpu.SemaphoreType.DMA,
        ],
        compiler_params=params(28),
        cost_estimate=cost(11_000_000_000, 22_000_000),
        name="attention_backward",
    )(tab, normed, qkv, probs, grad_att)


def qkv_grad_kernel(
    tab, later_tab, d_a, d_b, d_c, d_d, normed_ref, grad_qkv_ref, act_ref, mid_ref,
    out_ref, result_ref,
    part, w_down, sem,
):
    i = pl.program_id(0)

    @pl.when(i == 0)
    def _():
        fetch_pieces(later_tab, (d_a, d_b, d_c, d_d), 192, w_down, sem)
        qkv_grad_rows(tab, 0, normed_ref[...], grad_qkv_ref[...], out_ref, part)
        finish(w_down, sem)

    @pl.when(i > 0)
    def _():
        total = mid_ref[...]
        for j in range(4):
            total = total + dot(act_ref[j], down_rows(w_down, j))
        result_ref[...] = total.astype(BF16)


def qkv_grad(tab, later_tab, pieces, normed, grad_qkv, act, mid):
    row = pl.BlockSpec((256, WIDTH), lambda i: (jnp.maximum(i - 1, 0), 0))
    wide = pl.BlockSpec((4, 256, WIDTH), lambda i: (0, jnp.maximum(i - 1, 0), 0))
    return kernel_call(
        qkv_grad_kernel,
        grid=(5,),
        out_shape=(local((CHIPS, 144, LANES)), shaped((1024, WIDTH))),
        in_specs=[SMEM_SPEC] * 2 + [ANY_SPEC] * 4 + [fixed(1024, WIDTH), VMEM_SPEC, wide, row],
        out_specs=(VMEM_SPEC, row),
        scratch_shapes=[
            pltpu.VMEM((WIDTH, 3 * LANES), BF16),
            pltpu.VMEM((CHIPS, 2, 192, LANES), BF16),
            pltpu.SemaphoreType.DMA,
        ],
        compiler_params=params(26),
        cost_estimate=cost(7_000_000_000, 22_000_000),
        name="qkv_grad",
    )(tab, later_tab, *pieces, normed, grad_qkv, act, mid)


def input_backward_kernel(
    tab, g_a, g_b, g_c, g_d, grad_qkv_ref, x_ref, te_ref, vec_ref, grad_mid_ref, gain_two_ref,
    input_ref, small_ref,
    w, sem,
):
    i = pl.program_id(0)

    @pl.when(i == 0)
    def _():
        fetch_pieces(tab, (g_a, g_b, g_c, g_d), 144, w, sem)
        small_ref[8:9, :] = jnp.zeros((1, WIDTH), F32)
        small_ref[9:10, :] = gain_two_ref[...]
        small_ref[10:16, :] = jnp.zeros((6, WIDTH), F32)
        finish(w, sem)

    y = jnp.zeros((256, WIDTH), F32)
    for half in (0, 1):
        cols = slice(half * 3 * LANES, (half + 1) * 3 * LANES)
        y = y + dot_last(grad_qkv_ref[:, cols], qkv_columns(w, half))
    xhat, scale = ln_stats(add_embed(x_ref[...], te_ref, i))
    grad = grad_mid_ref[...] + ln_back(y, vec_ref[0:1, :], xhat, scale)
    input_ref[...] = grad.astype(BF16)
    for s in range(2):
        small_ref[pl.ds(i * 2 + s, 1), :] = jnp.sum(
            grad[128 * s : 128 * s + 128], axis=0, keepdims=True
        )
    small_ref[8:9, :] += jnp.sum(y * xhat, axis=0, keepdims=True)


def input_backward(tab, pieces, grad_qkv, rows, embed, vectors, grad_mid, gain_two):
    row = tiles(256, WIDTH)
    return kernel_call(
        input_backward_kernel,
        grid=(4,),
        out_shape=(shaped((1024, WIDTH)), local((16, WIDTH), F32)),
        in_specs=[SMEM_SPEC]
        + [ANY_SPEC] * 4
        + [tiles(256, 3 * WIDTH), row, fixed(8, WIDTH), fixed(16, WIDTH), row, VMEM_SPEC],
        out_specs=(row, VMEM_SPEC),
        scratch_shapes=[pltpu.VMEM((CHIPS, 2, 144, LANES), BF16), pltpu.SemaphoreType.DMA],
        compiler_params=params(20),
        cost_estimate=cost(4_000_000_000, 18_000_000),
        name="input_backward",
    )(tab, *pieces, grad_qkv, rows, embed, vectors, grad_mid, gain_two)


def finish_kernel(
    tab, e_a, e_b, e_c, e_d, wave_ref, hot_ref, hidden_ref, slope_ref, time_out_ref,
    down_ref, down_other, up_ref, up_other, qkv_ref, qkv_other,
    tin_out, tout_out, one_out, two_out, data_out, down_out, up_out, out_out, qkv_out,
    every, sem,
):
    each_piece(
        tab,
        (e_a, e_b, e_c, e_d),
        lambda src, chip, half: pltpu.make_async_copy(
            src, every.at[half * CHIPS + chip], sem
        ).start(),
    )
    core = first_core(tab)
    for half, down, up, qkv in (
        (core, down_ref, up_ref, qkv_ref), (1 - core, down_other, up_other, qkv_other)
    ):
        down_out[:, lanes_of(half, LANES)] = down[pl.ds(pl.multiple_of(96 * core, 8), 96), :]
        for b in range(4):
            up_out[:, lanes_of(half, 4 * LANES, b * LANES)] = up[pl.ds(pl.multiple_of(48 * b + 24 * core, 8), 24), :]
        out_out[:, lanes_of(half, LANES)] = up[pl.ds(pl.multiple_of(192 + 24 * core, 8), 24), :]
        for sec in range(3):
            qkv_out[:, lanes_of(half, LANES, sec * WIDTH)] = qkv[pl.ds(pl.multiple_of(48 * sec + 24 * core, 8), 24), :]
    finish(every, sem)
    grads = every[...].reshape(-1, WIDTH)
    tout_out[...] = dot_first(hidden_ref[...], grads)
    grad_pre = dot_last(grads, time_out_ref[...]) * slope_ref[...]
    tin_out[...] = dot_first(grad_pre.astype(BF16), wave_ref[...])
    first = tab[68] * 24
    lane = lax.broadcasted_iota(jnp.int32, (WIDTH, 128), 0)
    place = lax.broadcasted_iota(jnp.int32, (WIDTH, 128), 1)
    own = dot(grads, ((lane == place + first) & (place < 24)).astype(BF16)).astype(BF16)
    sums = dot(hot_ref[...], own)
    data_out[...] = sums[0:2, 0:24]
    one_out[...] = sums[2:3, 0:24]
    two_out[...] = sums[3:4, 0:24]


def finish_grads(tab, parts, wave, hot, hidden, slope, time_out, pieces):
    rows, width = time_out.shape
    return kernel_call(
        finish_kernel,
        out_shape=(
            shaped((rows, wave.shape[1]), F32),
            shaped((rows, width), F32),
            shaped((1, 24), F32),
            shaped((1, 24), F32),
            shaped((2, 24), F32),
            shaped((96, WIDTH), F32),
            shaped((24, FF), F32),
            shaped((24, WIDTH), F32),
            shaped((24, 3 * WIDTH), F32),
        ),
        in_specs=[SMEM_SPEC] + [ANY_SPEC] * 4 + [VMEM_SPEC] * 11,
        out_specs=(VMEM_SPEC,) * 9,
        scratch_shapes=[pltpu.VMEM((2 * CHIPS, 16, width), BF16), pltpu.SemaphoreType.DMA],
        compiler_params=params(16),
        cost_estimate=cost(50_000_000, 4_000_000),
        name="finish_grads",
    )(tab, *parts, wave, hot, hidden, slope, time_out, *pieces)


def pick(stacked, index):
    return lax.dynamic_index_in_dim(stacked, index, 0, keepdims=False)


def in_core_order(core, own, other, axis):
    return jnp.where(
        core == 0,
        jnp.concatenate([own, other], axis=axis),
        jnp.concatenate([other, own], axis=axis),
    )


def position_table(chip, core, order):
    index = jnp.arange(72, dtype=jnp.int32)
    side = jnp.bitwise_xor(core, (index // CHIPS) % 2)
    inner = index % CHIPS
    distance = jnp.bitwise_xor(inner, chip)
    there = jnp.zeros_like(index)
    back = jnp.zeros_like(index)
    for bit in range(4):
        mask = jnp.where(side == 0, order[0][bit], order[1][bit])
        there = there + jnp.where((inner >> bit) & 1 == 1, mask, 0)
        back = back + jnp.where(jnp.bitwise_and(distance, mask) != 0, 1 << bit, 0)
    moved = jnp.where(index < 32, jnp.bitwise_xor(there, chip), back)
    return jnp.where(index < 64, moved, jnp.where(index < 68, core, 2 * chip + core))


def lane_blocks(x, starts, step):
    return [
        jnp.concatenate([x[:, k + h * step : k + h * step + LANES] for k in starts], axis=0)
        for h in (0, 1)
    ]


def swap_halves(halves, core):
    own = jnp.where(core == 0, halves[0], halves[1])
    return own, core_swap(jnp.where(core == 0, halves[1], halves[0]))


def join_rows(own, other, core, blocks):
    shape = (blocks, own.shape[0] // blocks, LANES)
    return in_core_order(core, own.reshape(shape), other.reshape(shape), 1).reshape(-1, LANES)


def pack_extra(time_in, vectors, ints):
    rows = time_in.shape[0]
    filler = jnp.zeros((rows, 128), BF16)
    vec = lax.dynamic_update_slice(filler, vectors, (0, 0))
    num = lax.dynamic_update_slice(filler, ints[None, :], (0, 0))
    return jnp.concatenate([time_in, vec, num], axis=1)


def split_time(timestep, dataset):
    steps = timestep.reshape(-1)
    return jnp.concatenate([steps // 64, steps % 64, dataset.reshape(-1)]).astype(BF16)


def gather_all(x):
    return lax.all_gather(x, AXES, axis=0, tiled=True)


def shards(
    block_input,
    out_grad,
    timestep,
    dataset,
    lengths,
    norm1_gain,
    qkv_weight,
    out_weight,
    norm2_gain,
    up_weight,
    down_weight,
    time_in,
    time_out,
    data_embed,
    devices,
):
    flat = lax.axis_index(AXES)
    exchange = devices == 2 * CHIPS
    vectors = jnp.concatenate([norm1_gain[None], norm2_gain[None], data_embed.T], axis=0)
    numbers = split_time(timestep, dataset)
    count = numbers.shape[0] // 3
    micros, seqs, seq_len, width = block_input.shape
    tokens = micros * seqs * seq_len
    x_rows = block_input.reshape(tokens, width)
    grad_rows = out_grad.reshape(tokens, width)
    features = sinusoid(timestep.reshape(-1), time_in.shape[1] // 2).astype(BF16)
    if exchange:
        core = flat & 1
        chip = flat >> 1

        wide = lane_blocks(qkv_weight, (0, WIDTH, 2 * WIDTH), LANES)
        slim = lane_blocks(time_out, (0,), LANES)
        own, other = swap_halves(
            [jnp.concatenate([x, y], axis=0) for x, y in zip(wide, slim)], core
        )
        attention_piece = jnp.concatenate(
            [
                join_rows(own[:72], other[:72], core, 3),
                join_rows(own[72:], other[72:], core, 1),
                pack_extra(time_in, vectors, numbers),
            ],
            axis=0,
        )[None]
        near = [chip_swap(attention_piece, p) for p in (1, 2, 3)]
        up_weight, out_weight, down_weight, flat = lax.optimization_barrier(
            (up_weight, out_weight, down_weight, flat, attention_piece)
        )[:4]
        tab = position_table(flat >> 1, flat & 1, LINE_FIRST)
        later_tab = position_table(flat >> 1, flat & 1, LINE_LATER)
        wide = lane_blocks(up_weight, range(0, 4 * LANES, LANES), 4 * LANES)
        slim = lane_blocks(out_weight, (0,), LANES)
        own, other = swap_halves(
            [jnp.concatenate([x, y], axis=0) for x, y in zip(wide, slim)], core
        )
        up_piece = jnp.concatenate(
            [join_rows(own[:96], other[:96], core, 4), join_rows(own[96:], other[96:], core, 1)],
            axis=0,
        )[None]
        own, other = swap_halves(lane_blocks(down_weight, (0,), LANES), core)
        down_piece = join_rows(own, other, core, 1)[None]
        down_pair = jnp.concatenate([down_piece, chip_swap(down_piece, 1, LINE_LATER)], axis=0)
        ready = (up_piece, down_pair, tab, later_tab, features)
        line = after(jnp.concatenate([attention_piece] + near, axis=0), *ready)
        plane = chip_swap(line, 4)
        up_near = [chip_swap(after(up_piece, line), p) for p in (1, 2)]
        plane, up_near = together(plane, up_near)
        held = jnp.concatenate([line, plane], axis=0)
        far = chip_swap(held, 8)
        up_near.append(chip_swap(after(up_piece, plane), 3))
        up_line = lax.optimization_barrier(jnp.concatenate([up_piece] + up_near, axis=0))
        up_plane = chip_swap(up_line, 4)
        down_near = [chip_swap(after(down_pair, up_line), p, LINE_LATER) for p in (2, 4)]
        (far, up_plane), down_near = together((far, up_plane), down_near)
        attention_pieces = (held, far, core_swap(held), core_swap(far))
        up_held = jnp.concatenate([up_line, up_plane], axis=0)
        up_far = chip_swap(up_held, 8)
        down_last = chip_swap(after(down_pair, up_held), 6, LINE_LATER)
    else:
        tab = jnp.concatenate(
            [jnp.tile(jnp.arange(CHIPS, dtype=jnp.int32), 4), jnp.zeros((8,), jnp.int32)]
        )
        later_tab = tab
        full_qkv = gather_all(qkv_weight).reshape(CHIPS, 48, 3, 2, LANES)
        full_out = gather_all(out_weight).reshape(CHIPS, 48, 2, LANES)
        full_up = gather_all(up_weight).reshape(CHIPS, 48, 2, 4, LANES)
        full_down = gather_all(down_weight).reshape(CHIPS, 192, 2, LANES)
        full_tin = gather_all(time_in).reshape(CHIPS, 2, 16, 128)
        full_tout = gather_all(time_out).reshape(CHIPS, 32, 2, LANES)
        full_vec = lax.all_gather(vectors, AXES, axis=1, tiled=True).reshape(4, CHIPS, 2, 24)
        numbers_all = gather_all(numbers[None])
        extra = jnp.zeros((CHIPS, 2, 16, LANES), BF16)
        extra = extra.at[:, :, :, :128].set(full_tin)
        extra = extra.at[:, :, 0:4, 128:152].set(full_vec.transpose(1, 2, 0, 3))
        attention_pieces = []
        down_pieces = []
        up_pieces = []
        for half in (0, 1):
            wide = full_qkv[:, :, :, half].transpose(0, 2, 1, 3).reshape(CHIPS, 144, LANES)
            whole = jnp.concatenate([wide, full_tout[:, :, half], extra[:, half]], axis=1)
            attention_pieces += [whole[:8], whole[8:]]
            down_pieces += [full_down[:8, :, half], full_down[8:, :, half]]
            wide = full_up[:, :, half].transpose(0, 2, 1, 3).reshape(CHIPS, 192, LANES)
            whole = jnp.concatenate([wide, full_out[:, :, half]], axis=1)
            up_pieces += [whole[:8], whole[8:]]

    arrivals = []
    if exchange:
        x_rows = after(x_rows, up_held)
        arrivals = [up_far]
    forward = attention_forward(tab, lengths, dataset, attention_pieces, x_rows, features)
    (normed, qkv, embed, vecs, seen, probs, att), arrivals = together(forward, arrivals)
    seen = seen[:, :, 0, : 3 * count].reshape(2 * CHIPS, 3 * count) if exchange else numbers_all
    steps = seen[:, :count] * 64 + seen[:, count : 2 * count].astype(F32)
    wave = sinusoid(steps.reshape(-1), time_in.shape[1] // 2).astype(BF16)
    wave = jnp.pad(wave.reshape(devices, count, -1), ((0, 0), (0, 16 - count), (0, 0)))
    wave = wave.reshape(devices * 16, -1)
    which = jnp.pad(seen[:, 2 * count :], ((0, 0), (0, 16 - count))).reshape(-1)
    place = jnp.tile(jnp.arange(16), devices)
    hot = jnp.stack(
        [(place < count) & (which == 0), (place < count) & (which == 1), place == 8, place == 9]
    )
    hot = jnp.pad(hot.astype(BF16), ((0, 12), (0, 0)))
    pre = dot_last(wave, time_in)
    gate = 1.0 / (1.0 + jnp.exp(-pre))
    hidden = (pre * gate).astype(BF16)
    slope_pre = gate * (1.0 + pre * (1.0 - gate))
    if exchange:
        (up_far,) = arrivals
        down_near = [after(x, embed) for x in [down_pair] + down_near + [down_last]]
        up_pieces = (up_held, up_far, core_swap(up_held), core_swap(up_far))
        down_held = jnp.concatenate(down_near, axis=0)
        att, wave, hot, hidden, slope_pre, down_held = lax.optimization_barrier(
            (att, wave, hot, hidden, slope_pre, down_held)
        )
        arrivals = chip_swap(down_held, 8, LINE_LATER)
    forward = up_forward(tab, up_pieces, att, x_rows, grad_rows, embed, vecs)
    (mid, two, act, slope, down_theirs), arrivals = together(forward, arrivals)
    if exchange:
        down_far = arrivals
        down_sum = Scatter(down_theirs)
        arrivals = [core_swap(down_held), core_swap(down_far)], down_sum.swap()
    (down_mine, act, slope), arrivals = together(down_grad(tab, act, grad_rows, slope), arrivals)
    if exchange:
        down_pieces = (down_held, down_far, *arrivals[0])
        down_sum.land(arrivals[1], down_mine)
        slope = after(slope, *down_sum.send())
        arrivals = down_sum.fly()
    backward = mlp_backward(
        tab, later_tab, up_pieces, down_pieces, two, att, slope, grad_rows, mid, vecs
    )
    backward, arrivals = together(backward, arrivals)
    grad_mid, branch, grad_up, grad_att, gain_two, up_theirs = backward
    if exchange:
        down_sum.land(arrivals)
        up_sum = Scatter(up_theirs)
        grad_up = after(grad_up, *down_sum.send())
        arrivals = down_sum.fly(), up_sum.swap()
    up_mine, arrivals = together(up_grad(tab, att, branch, two, grad_up), arrivals)
    if exchange:
        down_sum.land(arrivals[0])
        up_sum.land(arrivals[1], up_mine)
        grad_att = after(grad_att, *up_sum.send(), *down_sum.send())
        arrivals = up_sum.fly(), down_sum.fly()
    backward = attention_backward(tab, normed, qkv, probs, grad_att)
    (grad_qkv, mine_qkv, att_theirs), arrivals = together(backward, arrivals)
    if exchange:
        up_sum.land(arrivals[0])
        down_sum.land(arrivals[1])
        down_total = down_sum.total()
        att_sum = Scatter(att_theirs)
        mine_qkv = after(mine_qkv, *up_sum.send(), down_total)
        arrivals = up_sum.fly(), att_sum.swap()
    backward = qkv_grad(tab, later_tab, down_pieces, normed, mine_qkv, act, mid)
    (att_mine, result), arrivals = together(backward, arrivals)
    if exchange:
        up_sum.land(arrivals[0])
        att_sum.land(arrivals[1], att_mine)
        grad_qkv = after(grad_qkv, *att_sum.send(), *up_sum.send())
        *up_near, up_last = up_sum.fly()
        arrivals = att_sum.fly(), up_near
    backward = input_backward(
        tab, attention_pieces, grad_qkv, x_rows, embed, vecs, grad_mid, gain_two
    )
    (grad_input, small), arrivals = together(backward, arrivals)

    small = small.astype(BF16)[None]
    if exchange:
        att_sum.land(arrivals[0])
        up_sum.land(arrivals[1])
        att_sum.send()
        near = [chip_swap(small, p) for p in (1, 2, 3)]
        brought, near = together(att_sum.fly(), near)
        att_sum.land(brought)
        small_line = jnp.concatenate([small] + near, axis=0)
        held = gather_plane(small_line)
        att_sum.send()
        far = chip_swap(held, 8)
        every = (held, far, core_swap(held), core_swap(far))
        brought, up_last = together(att_sum.fly(), up_last)
        att_sum.land(brought)
        up_sum.land([up_last])
        sums = after(down_total, small_line), after(up_sum.total(), small_line), att_sum.total()
        pieces = [x for total in sums for x in (total, core_swap(total))]
        finished = finish_grads(
            tab, every, wave, hot, hidden, slope_pre, time_out, pieces
        )
        grad_tin, grad_tout, gain_one, gain_two, grad_data, *weights = finished
        grad_down, grad_up_weight, grad_out, grad_qkv_weight = weights
    else:
        every = gather_all(small).reshape(devices * 16, width)
        grad_tout = dot_first(hidden, every)
        grad_pre = dot_last(every, time_out) * slope_pre
        grad_tin = dot_first(grad_pre.astype(BF16), wave)
        own_cols = norm1_gain.shape[0]
        sums = lax.dynamic_slice_in_dim(dot(hot, every), flat * own_cols, own_cols, 1)
        grad_data, gain_one, gain_two = sums[0:2], sums[2], sums[3]
        scatter = partial(lax.psum_scatter, axis_name=AXES, scatter_dimension=0, tiled=True)
        both = jnp.stack([down_mine, down_theirs]).astype(F32)
        grad_down = scatter(both.transpose(1, 2, 0, 3).reshape(FF, WIDTH))
        both = jnp.stack([up_mine, up_theirs]).astype(F32)
        grad_out = scatter(both[:, :, 192:].transpose(1, 2, 0, 3).reshape(WIDTH, WIDTH))
        both = both[:, :, :192].reshape(2, CHIPS, 4, 48, LANES)
        grad_up_weight = scatter(both.transpose(1, 3, 0, 2, 4).reshape(WIDTH, FF))
        both = jnp.stack([att_mine, att_theirs]).astype(F32).reshape(2, CHIPS, 3, 48, LANES)
        grad_qkv_weight = scatter(both.transpose(1, 3, 2, 0, 4).reshape(WIDTH, 3 * WIDTH))

    return (
        result.reshape(block_input.shape),
        grad_input.reshape(block_input.shape),
        gain_one.reshape(-1),
        grad_qkv_weight,
        grad_out,
        gain_two.reshape(-1),
        grad_up_weight,
        grad_down,
        grad_tin,
        grad_tout,
        grad_data.T,
    )


def solution(mesh):
    devices = mesh.shape["dp"] * mesh.shape["fsdp"]
    seq_spec = P(None, AXES, None, None)
    int_spec = P(None, AXES)
    row_spec = P(AXES, None)
    in_specs = (seq_spec, seq_spec, int_spec, int_spec, int_spec, P(AXES), row_spec, row_spec, P(AXES))
    in_specs = in_specs + (row_spec,) * 5
    out_specs = (seq_spec, seq_spec, P(AXES), row_spec, row_spec, P(AXES)) + (row_spec,) * 5
    return jax.shard_map(
        partial(shards, devices=devices),
        mesh=mesh,
        in_specs=in_specs,
        out_specs=out_specs,
        check_vma=False,
    )
```

```python
from functools import partial
import math

import jax
import jax.numpy as jnp
from jax import lax
from jax.experimental import pallas as pl
from jax.experimental.pallas import tpu as pltpu
from jax.sharding import PartitionSpec as P

HEAD_DIM = 64
AXES = ("dp", "fsdp")
LANES = 384
CHIPS = 16
WIDTH = 768
FF = 3072
F32 = jnp.float32
BF16 = jnp.bfloat16
NEG = -1000000000.0


def sinusoid(timestep, half_width):
    frequency = jnp.exp(-math.log(10000.0) * jnp.arange(half_width, dtype=F32) / half_width)
    angles = timestep.astype(F32)[:, None] * frequency[None, :]
    return jnp.concatenate([jnp.cos(angles), jnp.sin(angles)], axis=-1)


def dot(left, right):
    return jnp.dot(left, right, preferred_element_type=F32)


def dot_last(left, right):
    return lax.dot_general(left, right, (((1,), (1,)), ((), ())), preferred_element_type=F32)


def dot_first(left, right):
    return lax.dot_general(left, right, (((0,), (0,)), ((), ())), preferred_element_type=F32)


def positions(masks):
    return [sum(masks[b] for b in range(4) if (p >> b) & 1) for p in range(CHIPS)]


LINE_FIRST = ((2, 1, 8, 4), (2, 1, 4, 8))
LINE_LATER = ((8, 2, 1, 4), (4, 2, 1, 8))


def core_swap(x):
    return lax.ppermute(x, AXES, [(i, i ^ 1) for i in range(2 * CHIPS)])


def chip_swap(x, position, order=LINE_FIRST):
    far = [positions(masks)[position] * 2 for masks in order]
    return lax.ppermute(x, AXES, [(i, i ^ far[i & 1]) for i in range(2 * CHIPS)])


def after(x, *others):
    return lax.optimization_barrier((x,) + others)[0]


def gather_line(piece):
    return jnp.concatenate([piece] + [chip_swap(piece, p) for p in (1, 2, 3)], axis=0)


def gather_plane(held):
    return jnp.concatenate([held, chip_swap(held, 4)], axis=0)


def together(outs, arrivals):
    return lax.optimization_barrier((outs, arrivals))


class Scatter:
    def __init__(self, theirs):
        self.parts = []
        self.steps = [(8,), (4,), (1, 2, 3)]
        self.theirs = theirs

    def swap(self):
        return [core_swap(self.theirs)]

    def land(self, brought, *own):
        self.parts += [*brought, *own]

    def sum(self, start, stop):
        total = self.parts[0][start:stop].astype(F32)
        for part in self.parts[1:]:
            total = total + part[start:stop].astype(F32)
        return total

    def send(self):
        self.at = self.steps.pop(0)
        size = 1 if len(self.at) == 3 else self.at[0]
        self.sent = [self.sum(p, p + size).astype(BF16) for p in self.at]
        self.parts = [self.sum(0, size)]
        return [*self.sent, self.parts[0]]

    def fly(self):
        return [chip_swap(x, p) for x, p in zip(self.sent, self.at)]

    def total(self):
        return self.sum(0, 1)[0]


VMEM_SPEC = pl.BlockSpec(memory_space=pltpu.VMEM)
SMEM_SPEC = pl.BlockSpec(memory_space=pltpu.SMEM)
ANY_SPEC = pl.BlockSpec(memory_space=pl.ANY)


def tiles(rows, cols):
    return pl.BlockSpec((rows, cols), lambda i: (i, 0))


def columns(rows, cols):
    return pl.BlockSpec((rows, cols), lambda i: (0, i))


def fixed(*shape):
    return pl.BlockSpec(shape, lambda i: (0,) * len(shape))


def shaped(shape, dtype=BF16):
    return pltpu.HBM(shape, dtype)


def local(shape, dtype=BF16):
    return pltpu.VMEM(shape, dtype)


def params(mib):
    return pltpu.CompilerParams(vmem_limit_bytes=mib * 1024 * 1024)


def kernel_call(kernel, **kwargs):
    call = pl.pallas_call(kernel, **kwargs)
    if "grid_spec" in kwargs:
        grid_spec = kwargs["grid_spec"]
        specs = [SMEM_SPEC] * grid_spec.num_scalar_prefetch + list(grid_spec.in_specs)
    else:
        specs = kwargs["in_specs"]

    def place(x, spec):
        if spec is SMEM_SPEC:
            return x
        space = pltpu.VMEM if spec is VMEM_SPEC else pltpu.HBM
        return pltpu.with_memory_space_constraint(x, space)

    def run(*operands):
        return call(*[place(x, spec) for x, spec in zip(operands, specs, strict=True)])

    return run


def cost(flops, nbytes, transcendentals=0):
    return pl.CostEstimate(flops=flops, bytes_accessed=nbytes, transcendentals=transcendentals)


def ln_stats(v):
    center = v - jnp.mean(v, axis=-1, keepdims=True)
    scale = lax.rsqrt(jnp.mean(center * center, axis=-1, keepdims=True) + 1e-05)
    return center * scale, scale


def ln_back(y, gain, xhat, scale):
    yg = y * gain
    return scale * (
        yg - jnp.mean(yg, axis=-1, keepdims=True) - xhat * jnp.mean(yg * xhat, axis=-1, keepdims=True)
    )


def first_core(tab):
    return tab[64]


def each_piece(tab, parts, fn):
    core = first_core(tab)
    for side in (0, 1):
        half = core if side == 0 else 1 - core
        for group in (0, 1):
            part = parts[side * 2 + group]

            def body(q, _, part=part, side=side, group=group, half=half):
                chip = tab[side * CHIPS + group * 8 + q]
                fn(part.at[q], chip, half)
                return 0

            lax.fori_loop(0, 8, body, 0)


def rows_of(chip, size):
    return pl.ds(pl.multiple_of(chip * size, size), size)


def lanes_of(half, size, base=0):
    return pl.ds(pl.multiple_of(half * size + base, 128), LANES)


def fetch_pieces(tab, parts, rows, dst, sem, first=0):
    each_piece(
        tab,
        parts,
        lambda src, chip, half: pltpu.make_async_copy(
            src.at[pl.ds(first, rows), :], dst.at[chip, half], sem
        ).start(),
    )


def block(pieces, half, first, rows=48):
    return pieces[:, half, first : first + rows, :].reshape(CHIPS * rows, LANES)


def both_halves(pieces, first, rows=48):
    return jnp.concatenate([block(pieces, h, first, rows) for h in (0, 1)], axis=1)


def down_rows(pieces, j):
    chips = pl.ds(4 * j, 4)
    return jnp.concatenate([pieces[chips, h].reshape(WIDTH, LANES) for h in (0, 1)], axis=1)


def qkv_columns(pieces, half):
    return jnp.concatenate([block(pieces, half, 48 * sec) for sec in range(3)], axis=1)


def finish(ref, sem):
    pltpu.make_async_copy(ref, ref, sem).wait()


def add_embed(x, embed, i):
    seqs = x.shape[0] // 128
    parts = [
        x[128 * k : 128 * k + 128].astype(F32) + embed[pl.ds(i * seqs + k, 1), :]
        for k in range(seqs)
    ]
    return jnp.concatenate(parts, axis=0)


def two_heads(x, low_half):
    none = jnp.zeros_like(x)
    return jnp.concatenate([jnp.where(low_half, x, none), jnp.where(low_half, none, x)], axis=0)


def side_by_side(x):
    return jnp.concatenate([x[:128], x[128:]], axis=1)


def pair_base(pair):
    return (pair // 3) * 3 * LANES + (pair % 3) * 128


def attention_tile(lengths, qkv_ref, probs_ref, att_ref):
    low_half = lax.broadcasted_iota(jnp.int32, (128, 128), 1) < HEAD_DIM
    lane = lax.broadcasted_iota(jnp.int32, (256, 128), 1)
    keep = [lane < length for length in lengths]
    units = [(k, pair) for k in range(2) for pair in range(6)]

    def part(k, pair, section):
        base = pair_base(pair) + section * LANES
        return qkv_ref[128 * k : 128 * k + 128, base : base + 128]

    scores = []
    for k, pair in units:
        query = two_heads(part(k, pair, 0), low_half)
        score = dot_last(query, part(k, pair, 1)) * HEAD_DIM ** (-0.5)
        scores.append(jnp.where(keep[k], score, NEG))
    probs = []
    for (k, pair), score in zip(units, scores):
        shifted = jnp.exp(score - jnp.max(score, axis=-1, keepdims=True))
        total = jnp.sum(shifted, axis=-1, keepdims=True)
        probs.append((shifted * (1.0 / total)).astype(BF16))
        first = 256 * (6 * k + pair)
        probs_ref[first : first + 256, :] = probs[-1]
    for (k, pair), prob in zip(units, probs):
        value = two_heads(part(k, pair, 2), low_half)
        att_ref[128 * k : 128 * k + 128, pair * 128 : pair * 128 + 128] = dot(
            side_by_side(prob), value
        ).astype(BF16)


def attention_kernel(
    tab, lens, sets, g_a, g_b, g_c, g_d, x_ref, feat_ref,
    normed_ref, qkv_ref, te_ref, vec_ref, seen_ref, probs_ref, att_ref,
    w, w_time, sem, sem_time,
):
    i = pl.program_id(0)

    @pl.when(i == 0)
    def _():
        fetch_pieces(tab, (g_a, g_b, g_c, g_d), 48, w_time, sem_time, 144)
        fetch_pieces(tab, (g_a, g_b, g_c, g_d), 144, w, sem)
        finish(w_time, sem_time)
        lane = lax.broadcasted_iota(jnp.int32, (128, WIDTH), 1)
        spread = (lax.broadcasted_iota(jnp.int32, (128, WIDTH), 0) == lane % 24).astype(BF16)
        vectors = jnp.zeros((16, WIDTH), F32)
        embed = jnp.zeros((8, WIDTH), F32)
        for owner in (0, 1):
            extra = block(w_time, owner, 32, 16)
            wide = dot(extra[:, 128:256], spread)
            chip = lax.broadcasted_iota(jnp.int32, (256, WIDTH), 0) // 16
            place = lax.broadcasted_iota(jnp.int32, (256, WIDTH), 1) // 24
            wide = jnp.where(place == chip * 2 + owner, wide, 0.0)
            vectors = vectors + jnp.sum(wide.reshape(CHIPS, 16, WIDTH), axis=0)
            pre = dot_last(feat_ref[...], extra[:, 0:128])
            hidden = (pre / (1.0 + jnp.exp(-pre))).astype(BF16)
            embed = embed + dot(hidden, both_halves(w_time, 16 * owner, 16))
            seen_ref[owner] = w_time[:, owner, 32:48, 256:]
        vec_ref[...] = vectors
        for s in range(8):
            chosen = jnp.where(sets[s // 4, s % 4] == 1, vectors[3:4, :], vectors[2:3, :])
            te_ref[s : s + 1, :] = embed[s : s + 1, :] + chosen

    xhat, _unused = ln_stats(add_embed(x_ref[...], te_ref, i))
    normed_ref[...] = (xhat * vec_ref[0:1, :]).astype(BF16)

    @pl.when(i == 0)
    def _():
        finish(w, sem)

    for half in (0, 1):
        cols = slice(half * 3 * LANES, (half + 1) * 3 * LANES)
        qkv_ref[:, cols] = dot(normed_ref[...], qkv_columns(w, half)).astype(BF16)
    lengths = [lens[i // 2, i % 2 * 2 + k] for k in range(2)]
    attention_tile(lengths, qkv_ref, probs_ref, att_ref)


def attention_forward(tab, lens, sets, pieces, rows, features):
    row = tiles(256, WIDTH)
    return kernel_call(
        attention_kernel,
        grid=(4,),
        out_shape=(
            shaped((1024, WIDTH)),
            shaped((1024, 3 * WIDTH)),
            shaped((8, WIDTH), F32),
            shaped((16, WIDTH), F32),
            shaped((2, CHIPS, 16, 128)),
            shaped((48 * 256, 128)),
            shaped((1024, WIDTH)),
        ),
        in_specs=[SMEM_SPEC] * 3 + [ANY_SPEC] * 4 + [row, fixed(8, 128)],
        out_specs=(
            row, tiles(256, 3 * WIDTH), fixed(8, WIDTH), fixed(16, WIDTH),
            fixed(2, CHIPS, 16, 128), tiles(12 * 256, 128), row,
        ),
        scratch_shapes=[
            pltpu.VMEM((CHIPS, 2, 144, LANES), BF16),
            pltpu.VMEM((CHIPS, 2, 48, LANES), BF16),
            pltpu.SemaphoreType.DMA,
            pltpu.SemaphoreType.DMA,
        ],
        compiler_params=params(26),
        cost_estimate=cost(8_000_000_000, 20_000_000, 1_600_000),
        name="attention_forward",
    )(tab, lens, sets, *pieces, rows, features)


def gelu_parts(u):
    cdf = 0.5 + 0.5 * lax.erf(u * math.sqrt(0.5))
    return cdf, jnp.exp(u * u * -0.5) * (1.0 / math.sqrt(2.0 * math.pi))


def up_columns(pieces, half, j):
    return jnp.concatenate(
        [block(pieces, half, 96 * j), block(pieces, half, 96 * j + 48)], axis=1
    )


def half_of(tab, side):
    return first_core(tab) if side == 0 else 1 - first_core(tab)


def clamped(rows, cols):
    return pl.BlockSpec((rows, cols), lambda i: (jnp.minimum(i, 3), 0))


def down_grad_rows(tab, side, j, act, out_grad, out_ref):
    lanes = lanes_of(half_of(tab, side), LANES)
    grad = dot_first(act, out_grad[:, lanes]).astype(BF16)
    for k in range(4):
        place = tab[32 + side * CHIPS + j * 4 + k]
        out_ref[place, :, :] = grad[192 * k : 192 * k + 192, :]


def up_kernel(
    tab, u_a, u_b, u_c, u_d, out_grad_ref, att_ref, x_ref, te_ref, vec_ref,
    mid_ref, two_ref, act_ref, slope_ref, theirs_ref,
    w, w_out, sem, sem_out,
):
    i = pl.program_id(0)
    parts = (u_a, u_b, u_c, u_d)

    def token_rows(arrived):
        rows = rows_of(i, 512)
        mid = add_embed(x_ref[...], te_ref, i) + dot(att_ref[...], both_halves(w_out, 0))
        mid_ref[...] = mid
        xhat, _unused = ln_stats(mid)
        two = (xhat * vec_ref[1:2, :]).astype(BF16)
        two_ref[...] = two
        arrived()
        for j in range(4):
            up = dot(two, up_columns(w, j // 2, j % 2))
            cdf, density = gelu_parts(up)
            act_ref[j, rows, :] = (up * cdf).astype(BF16)
            slope_ref[j, rows, :] = (cdf + up * density).astype(BF16)

    @pl.when(i == 0)
    def _():
        fetch_pieces(tab, parts, 48, w_out, sem_out, 192)
        fetch_pieces(tab, parts, 192, w, sem)
        finish(w_out, sem_out)
        token_rows(lambda: finish(w, sem))

    @pl.when((i > 0) & (i < 2))
    def _():
        token_rows(lambda: None)

    @pl.when(i >= 2)
    def _():
        down_grad_rows(tab, 1, i - 2, act_ref[i - 2], out_grad_ref, theirs_ref)


def up_forward(tab, pieces, att, rows, out_grad, embed, vectors):
    row = pl.BlockSpec((512, WIDTH), lambda i: (jnp.minimum(i, 1), 0))
    return kernel_call(
        up_kernel,
        grid=(6,),
        out_shape=(
            shaped((1024, WIDTH), F32),
            shaped((1024, WIDTH)),
            local((4, 1024, WIDTH)),
            local((4, 1024, WIDTH)),
            local((CHIPS, 192, LANES)),
        ),
        in_specs=[SMEM_SPEC]
        + [ANY_SPEC] * 4
        + [VMEM_SPEC, row, row, fixed(8, WIDTH), fixed(16, WIDTH)],
        out_specs=(row, row) + (VMEM_SPEC,) * 3,
        scratch_shapes=[
            pltpu.VMEM((CHIPS, 2, 192, LANES), BF16),
            pltpu.VMEM((CHIPS, 2, 48, LANES), BF16),
            pltpu.SemaphoreType.DMA,
            pltpu.SemaphoreType.DMA,
        ],
        compiler_params=params(28),
        cost_estimate=cost(10_000_000_000, 30_000_000, 6_000_000),
        name="up_forward",
    )(tab, *pieces, out_grad, att, rows, embed, vectors)


def down_grad_kernel(tab, act_ref, out_grad_ref, _slope, out_ref, act_hbm, _slope_out, sem):
    j = pl.program_id(0)

    @pl.when(j == 0)
    def _():
        pltpu.make_async_copy(act_ref, act_hbm, sem).start()

    down_grad_rows(tab, 0, j, act_ref[j], out_grad_ref, out_ref)

    @pl.when(j == 3)
    def _():
        pltpu.make_async_copy(act_ref, act_hbm, sem).wait()


def down_grad(tab, act, out_grad, slope):
    return kernel_call(
        down_grad_kernel,
        grid=(4,),
        out_shape=(
            local((CHIPS, 192, LANES)), shaped((4, 1024, WIDTH)), local((4, 1024, WIDTH))
        ),
        in_specs=[SMEM_SPEC] + [VMEM_SPEC] * 3,
        out_specs=(VMEM_SPEC, ANY_SPEC, VMEM_SPEC),
        input_output_aliases={3: 2},
        scratch_shapes=[pltpu.SemaphoreType.DMA],
        compiler_params=params(12),
        cost_estimate=cost(3_000_000_000, 10_000_000),
        name="down_grad",
    )(tab, act, out_grad, slope)


def store_blocks(tab, side, target, first, part, lanes):
    for chip in range(CHIPS):
        place = tab[32 + side * CHIPS + chip]
        target[place, pl.ds(first, 48), :] = part[48 * chip : 48 * chip + 48, lanes]


def out_grad_rows(tab, side, att, branch, out_ref, part):
    lanes = lanes_of(half_of(tab, side), LANES)
    part[:, 0:LANES] = dot_first(att[...], branch[:, lanes]).astype(BF16)
    store_blocks(tab, side, out_ref, 192, part, slice(0, LANES))


def up_grad_rows(tab, side, j, two, grad_up, out_ref, part):
    part[...] = dot_first(two, grad_up).astype(BF16)
    for b in range(2):
        first = pl.multiple_of((2 * j + b) * 48, 48)
        store_blocks(tab, side, out_ref, first, part, slice(b * LANES, (b + 1) * LANES))


def up_grad_kernel(
    tab, att_hbm, two_hbm, branch_ref, grad_up_ref, out_ref, att, two, part, sem_att, sem_two
):
    j = pl.program_id(0)

    @pl.when(j == 0)
    def _():
        pltpu.make_async_copy(att_hbm, att, sem_att).start()
        pltpu.make_async_copy(two_hbm, two, sem_two).start()
        finish(att, sem_att)
        out_grad_rows(tab, 0, att, branch_ref, out_ref, part)
        finish(two, sem_two)

    @pl.when(j > 0)
    def _():
        up_grad_rows(tab, 0, j - 1, two[...], grad_up_ref[j - 1], out_ref, part)


def up_grad(tab, att, branch, two, grad_up):
    return kernel_call(
        up_grad_kernel,
        grid=(3,),
        out_shape=local((CHIPS, 240, LANES)),
        in_specs=[SMEM_SPEC] + [ANY_SPEC] * 2 + [VMEM_SPEC] * 2,
        out_specs=VMEM_SPEC,
        scratch_shapes=[pltpu.VMEM((1024, WIDTH), BF16)] * 2
        + [pltpu.VMEM((WIDTH, WIDTH), BF16)]
        + [pltpu.SemaphoreType.DMA] * 2,
        compiler_params=params(16),
        cost_estimate=cost(3_200_000_000, 11_000_000),
        name="up_grad",
    )(tab, att, two, branch, grad_up)


def mlp_backward_kernel(
    tab, later_tab, u_a, u_b, u_c, u_d, d_a, d_b, d_c, d_d,
    two_hbm, att_hbm, slope_ref, out_grad_ref, mid_ref, vec_ref,
    grad_mid_ref, branch_ref, mine_up_ref, grad_att_ref, gain_ref, theirs_ref,
    w, w_down, two, att, theirs_up, part, sem, sem_down, sem_two, sem_att,
):
    i = pl.program_id(0)
    grad_up = [
        (half_of(tab, side), j, target)
        for side, target in enumerate((mine_up_ref, theirs_up))
        for j in range(2)
    ]

    @pl.when(i == 0)
    def _():
        fetch_pieces(later_tab, (d_a, d_b, d_c, d_d), 192, w_down, sem_down)
        gain_ref[...] = jnp.zeros_like(gain_ref)
        finish(w_down, sem_down)
        fetch_pieces(tab, (u_a, u_b, u_c, u_d), 240, w, sem)

    @pl.when(i < 2)
    def _():
        rows = rows_of(i, 512)
        for half, j, target in grad_up:
            grad_act = dot_last(out_grad_ref[rows, :], down_rows(w_down, 2 * half + j))
            slope = slope_ref[2 * half + j, rows, :].astype(F32)
            target[j, rows, :] = (grad_act * slope).astype(BF16)

    @pl.when(i == 2)
    def _():
        finish(w, sem)
        pltpu.make_async_copy(two_hbm, two, sem_two).start()
        pltpu.make_async_copy(att_hbm, att, sem_att).start()

    @pl.when((i >= 2) & (i < 4))
    def _():
        rows = rows_of(i - 2, 512)
        y = jnp.zeros((512, WIDTH), F32)
        for half, j, target in grad_up:
            y = y + dot_last(target[j, rows, :], up_columns(w, half, j))
        xhat, scale = ln_stats(mid_ref[...])
        grad = out_grad_ref[rows, :].astype(F32) + ln_back(y, vec_ref[1:2, :], xhat, scale)
        grad_mid_ref[...] = grad
        branch = grad.astype(BF16)
        branch_ref[rows, :] = branch
        gain_ref[...] += jnp.sum(y * xhat, axis=0, keepdims=True)
        grad_att_ref[rows, :] = dot_last(branch, both_halves(w, 192)).astype(BF16)

    @pl.when(i == 4)
    def _():
        finish(two, sem_two)
        finish(att, sem_att)
        out_grad_rows(tab, 1, att, branch_ref, theirs_ref, part)

    @pl.when(i >= 4)
    def _():
        up_grad_rows(tab, 1, i - 4, two[...], theirs_up[i - 4], theirs_ref, part)


def mlp_backward(
    tab, later_tab, up_pieces, down_pieces, two, att, slope, out_grad, mid, vectors
):
    row = pl.BlockSpec((512, WIDTH), lambda i: (jnp.clip(i - 2, 0, 1), 0))
    return kernel_call(
        mlp_backward_kernel,
        grid=(6,),
        out_shape=(
            shaped((1024, WIDTH), F32),
            local((1024, WIDTH)),
            local((2, 1024, WIDTH)),
            local((1024, WIDTH)),
            local((1, WIDTH), F32),
            local((CHIPS, 240, LANES)),
        ),
        in_specs=[SMEM_SPEC] * 2
        + [ANY_SPEC] * 10
        + [VMEM_SPEC] * 2
        + [row, fixed(16, WIDTH)],
        out_specs=(row,) + (VMEM_SPEC,) * 5,
        scratch_shapes=[
            pltpu.VMEM((CHIPS, 2, 240, LANES), BF16),
            pltpu.VMEM((CHIPS, 2, 192, LANES), BF16),
            pltpu.VMEM((1024, WIDTH), BF16),
            pltpu.VMEM((1024, WIDTH), BF16),
            pltpu.VMEM((2, 1024, WIDTH), BF16),
            pltpu.VMEM((WIDTH, WIDTH), BF16),
        ]
        + [pltpu.SemaphoreType.DMA] * 4,
        compiler_params=params(38),
        cost_estimate=cost(18_000_000_000, 50_000_000),
        name="mlp_backward",
    )(tab, later_tab, *up_pieces, *down_pieces, two, att, slope, out_grad, mid, vectors)


def attention_backward_tile(first_row, qkv_ref, probs_ref, grad_att_ref, grad_qkv_ref):
    low_half = lax.broadcasted_iota(jnp.int32, (128, 128), 1) < HEAD_DIM
    units = [(k, pair) for k in range(2) for pair in range(6)]

    def rows(k):
        return slice(128 * k, 128 * k + 128)

    def part(k, pair, section):
        base = pair_base(pair) + section * LANES
        return qkv_ref[rows(k), base : base + 128]

    def up(k, pair):
        whole = pl.ds(pl.multiple_of(first_row + 128 * k, 128), 128)
        return two_heads(grad_att_ref[whole, pair * 128 : pair * 128 + 128], low_half)

    def probs_of(k, pair):
        first = 256 * (6 * k + pair)
        return probs_ref[first : first + 256, :]

    def store(k, pair, section, value):
        base = pair_base(pair) + section * LANES
        grad_qkv_ref[rows(k), base : base + 128] = value.astype(BF16)

    grad_probs = [dot_last(up(k, pair), part(k, pair, 2)) for k, pair in units]
    grad_scores = []
    for (k, pair), grad in zip(units, grad_probs):
        probs = probs_of(k, pair).astype(F32)
        inner = jnp.sum(probs * grad, axis=-1, keepdims=True)
        grad_scores.append((probs * (grad - inner)).astype(BF16))
    for (k, pair), grad in zip(units, grad_scores):
        grad_query = dot(side_by_side(grad), two_heads(part(k, pair, 1), low_half))
        store(k, pair, 0, grad_query * HEAD_DIM ** (-0.5))
        grad_key = dot_first(grad, two_heads(part(k, pair, 0), low_half))
        store(k, pair, 1, grad_key * HEAD_DIM ** (-0.5))
        store(k, pair, 2, dot_first(probs_of(k, pair), up(k, pair)))


def qkv_grad_rows(tab, side, normed, grad_qkv, out_ref, part):
    part[...] = dot_first(normed, grad_qkv).astype(BF16)
    for sec in range(3):
        store_blocks(tab, side, out_ref, 48 * sec, part, slice(sec * LANES, (sec + 1) * LANES))


def attention_backward_kernel(
    tab, normed_hbm, qkv_ref, probs_ref, grad_att_ref, grad_qkv_ref, mine_ref, theirs_ref,
    normed, kept, part, sem,
):
    i = pl.program_id(0)

    @pl.when(i == 0)
    def _():
        pltpu.make_async_copy(normed_hbm, normed, sem).start()

    @pl.when(i < 4)
    def _():
        attention_backward_tile(i * 256, qkv_ref, probs_ref, grad_att_ref, grad_qkv_ref)
        for side, target in enumerate((mine_ref, kept)):
            lanes = pl.ds(pl.multiple_of(half_of(tab, side) * 3 * LANES, 128), 3 * LANES)
            target[rows_of(i, 256), :] = grad_qkv_ref[:, lanes]

    @pl.when(i == 4)
    def _():
        finish(normed, sem)
        qkv_grad_rows(tab, 1, normed[...], kept[...], theirs_ref, part)


def attention_backward(tab, normed, qkv, probs, grad_att):
    wide = clamped(256, 3 * WIDTH)
    return kernel_call(
        attention_backward_kernel,
        grid=(5,),
        out_shape=(
            shaped((1024, 3 * WIDTH)), local((1024, 3 * LANES)), local((CHIPS, 144, LANES))
        ),
        in_specs=[SMEM_SPEC, ANY_SPEC, wide, clamped(12 * 256, 128), VMEM_SPEC],
        out_specs=(wide, VMEM_SPEC, VMEM_SPEC),
        scratch_shapes=[
            pltpu.VMEM((1024, WIDTH), BF16),
            pltpu.VMEM((1024, 3 * LANES), BF16),
            pltpu.VMEM((WIDTH, 3 * LANES), BF16),
            pltpu.SemaphoreType.DMA,
        ],
        compiler_params=params(28),
        cost_estimate=cost(11_000_000_000, 22_000_000),
        name="attention_backward",
    )(tab, normed, qkv, probs, grad_att)


def qkv_grad_kernel(
    tab, later_tab, d_a, d_b, d_c, d_d, normed_ref, grad_qkv_ref, act_ref, mid_ref,
    out_ref, result_ref,
    part, w_down, sem,
):
    i = pl.program_id(0)

    @pl.when(i == 0)
    def _():
        fetch_pieces(later_tab, (d_a, d_b, d_c, d_d), 192, w_down, sem)
        qkv_grad_rows(tab, 0, normed_ref[...], grad_qkv_ref[...], out_ref, part)
        finish(w_down, sem)

    @pl.when(i > 0)
    def _():
        total = mid_ref[...]
        for j in range(4):
            total = total + dot(act_ref[j], down_rows(w_down, j))
        result_ref[...] = total.astype(BF16)


def qkv_grad(tab, later_tab, pieces, normed, grad_qkv, act, mid):
    row = pl.BlockSpec((256, WIDTH), lambda i: (jnp.maximum(i - 1, 0), 0))
    wide = pl.BlockSpec((4, 256, WIDTH), lambda i: (0, jnp.maximum(i - 1, 0), 0))
    return kernel_call(
        qkv_grad_kernel,
        grid=(5,),
        out_shape=(local((CHIPS, 144, LANES)), shaped((1024, WIDTH))),
        in_specs=[SMEM_SPEC] * 2 + [ANY_SPEC] * 4 + [fixed(1024, WIDTH), VMEM_SPEC, wide, row],
        out_specs=(VMEM_SPEC, row),
        scratch_shapes=[
            pltpu.VMEM((WIDTH, 3 * LANES), BF16),
            pltpu.VMEM((CHIPS, 2, 192, LANES), BF16),
            pltpu.SemaphoreType.DMA,
        ],
        compiler_params=params(26),
        cost_estimate=cost(7_000_000_000, 22_000_000),
        name="qkv_grad",
    )(tab, later_tab, *pieces, normed, grad_qkv, act, mid)


def input_backward_kernel(
    tab, g_a, g_b, g_c, g_d, grad_qkv_ref, x_ref, te_ref, vec_ref, grad_mid_ref, gain_two_ref,
    input_ref, small_ref,
    w, sem,
):
    i = pl.program_id(0)

    @pl.when(i == 0)
    def _():
        fetch_pieces(tab, (g_a, g_b, g_c, g_d), 144, w, sem)
        small_ref[8:9, :] = jnp.zeros((1, WIDTH), F32)
        small_ref[9:10, :] = gain_two_ref[...]
        small_ref[10:16, :] = jnp.zeros((6, WIDTH), F32)
        finish(w, sem)

    y = jnp.zeros((256, WIDTH), F32)
    for half in (0, 1):
        cols = slice(half * 3 * LANES, (half + 1) * 3 * LANES)
        y = y + dot_last(grad_qkv_ref[:, cols], qkv_columns(w, half))
    xhat, scale = ln_stats(add_embed(x_ref[...], te_ref, i))
    grad = grad_mid_ref[...] + ln_back(y, vec_ref[0:1, :], xhat, scale)
    input_ref[...] = grad.astype(BF16)
    for s in range(2):
        small_ref[pl.ds(i * 2 + s, 1), :] = jnp.sum(
            grad[128 * s : 128 * s + 128], axis=0, keepdims=True
        )
    small_ref[8:9, :] += jnp.sum(y * xhat, axis=0, keepdims=True)


def input_backward(tab, pieces, grad_qkv, rows, embed, vectors, grad_mid, gain_two):
    row = tiles(256, WIDTH)
    return kernel_call(
        input_backward_kernel,
        grid=(4,),
        out_shape=(shaped((1024, WIDTH)), local((16, WIDTH), F32)),
        in_specs=[SMEM_SPEC]
        + [ANY_SPEC] * 4
        + [tiles(256, 3 * WIDTH), row, fixed(8, WIDTH), fixed(16, WIDTH), row, VMEM_SPEC],
        out_specs=(row, VMEM_SPEC),
        scratch_shapes=[pltpu.VMEM((CHIPS, 2, 144, LANES), BF16), pltpu.SemaphoreType.DMA],
        compiler_params=params(20),
        cost_estimate=cost(4_000_000_000, 18_000_000),
        name="input_backward",
    )(tab, *pieces, grad_qkv, rows, embed, vectors, grad_mid, gain_two)


def finish_kernel(
    tab, e_mine, e_theirs, wave_ref, hot_ref, hidden_ref, slope_ref, time_out_ref,
    down_ref, down_other, up_ref, up_other, qkv_ref, qkv_other,
    tin_out, tout_out, one_out, two_out, data_out, down_out, up_out, out_out, qkv_out,
    every, sem,
):
    each_piece(
        tab,
        [e.at[pl.ds(first, 8)] for e in (e_mine, e_theirs) for first in (0, 8)],
        lambda src, chip, half: pltpu.make_async_copy(
            src, every.at[half * CHIPS + chip], sem
        ).start(),
    )
    core = first_core(tab)
    for half, down, up, qkv in (
        (core, down_ref, up_ref, qkv_ref), (1 - core, down_other, up_other, qkv_other)
    ):
        down_out[:, lanes_of(half, LANES)] = down[pl.ds(pl.multiple_of(96 * core, 8), 96), :]
        for b in range(4):
            up_out[:, lanes_of(half, 4 * LANES, b * LANES)] = up[pl.ds(pl.multiple_of(48 * b + 24 * core, 8), 24), :]
        out_out[:, lanes_of(half, LANES)] = up[pl.ds(pl.multiple_of(192 + 24 * core, 8), 24), :]
        for sec in range(3):
            qkv_out[:, lanes_of(half, LANES, sec * WIDTH)] = qkv[pl.ds(pl.multiple_of(48 * sec + 24 * core, 8), 24), :]
    finish(every, sem)
    grads = every[...].reshape(-1, WIDTH)
    tout_out[...] = dot_first(hidden_ref[...], grads)
    grad_pre = dot_last(grads, time_out_ref[...]) * slope_ref[...]
    tin_out[...] = dot_first(grad_pre.astype(BF16), wave_ref[...])
    first = tab[68] * 24
    lane = lax.broadcasted_iota(jnp.int32, (WIDTH, 128), 0)
    place = lax.broadcasted_iota(jnp.int32, (WIDTH, 128), 1)
    own = dot(grads, ((lane == place + first) & (place < 24)).astype(BF16)).astype(BF16)
    sums = dot(hot_ref[...], own)
    data_out[...] = sums[0:2, 0:24]
    one_out[...] = sums[2:3, 0:24]
    two_out[...] = sums[3:4, 0:24]


def finish_grads(tab, parts, wave, hot, hidden, slope, time_out, pieces):
    rows, width = time_out.shape
    return kernel_call(
        finish_kernel,
        out_shape=(
            shaped((rows, wave.shape[1]), F32),
            shaped((rows, width), F32),
            shaped((1, 24), F32),
            shaped((1, 24), F32),
            shaped((2, 24), F32),
            shaped((96, WIDTH), F32),
            shaped((24, FF), F32),
            shaped((24, WIDTH), F32),
            shaped((24, 3 * WIDTH), F32),
        ),
        in_specs=[SMEM_SPEC] + [ANY_SPEC] * 2 + [VMEM_SPEC] * 11,
        out_specs=(VMEM_SPEC,) * 9,
        scratch_shapes=[pltpu.VMEM((2 * CHIPS, 16, width), BF16), pltpu.SemaphoreType.DMA],
        compiler_params=params(16),
        cost_estimate=cost(50_000_000, 4_000_000),
        name="finish_grads",
    )(tab, *parts, wave, hot, hidden, slope, time_out, *pieces)


def pick(stacked, index):
    return lax.dynamic_index_in_dim(stacked, index, 0, keepdims=False)


def in_core_order(core, own, other, axis):
    return jnp.where(
        core == 0,
        jnp.concatenate([own, other], axis=axis),
        jnp.concatenate([other, own], axis=axis),
    )


def position_table(chip, core, order):
    index = jnp.arange(72, dtype=jnp.int32)
    side = jnp.bitwise_xor(core, (index // CHIPS) % 2)
    inner = index % CHIPS
    distance = jnp.bitwise_xor(inner, chip)
    there = jnp.zeros_like(index)
    back = jnp.zeros_like(index)
    for bit in range(4):
        mask = jnp.where(side == 0, order[0][bit], order[1][bit])
        there = there + jnp.where((inner >> bit) & 1 == 1, mask, 0)
        back = back + jnp.where(jnp.bitwise_and(distance, mask) != 0, 1 << bit, 0)
    moved = jnp.where(index < 32, jnp.bitwise_xor(there, chip), back)
    return jnp.where(index < 64, moved, jnp.where(index < 68, core, 2 * chip + core))


def lane_blocks(x, starts, step):
    return [
        jnp.concatenate([x[:, k + h * step : k + h * step + LANES] for k in starts], axis=0)
        for h in (0, 1)
    ]


def swap_halves(halves, core):
    own = jnp.where(core == 0, halves[0], halves[1])
    return own, core_swap(jnp.where(core == 0, halves[1], halves[0]))


def join_rows(own, other, core, blocks):
    shape = (blocks, own.shape[0] // blocks, LANES)
    return in_core_order(core, own.reshape(shape), other.reshape(shape), 1).reshape(-1, LANES)


def pack_extra(time_in, vectors, ints):
    rows = time_in.shape[0]
    filler = jnp.zeros((rows, 128), BF16)
    vec = lax.dynamic_update_slice(filler, vectors, (0, 0))
    num = lax.dynamic_update_slice(filler, ints[None, :], (0, 0))
    return jnp.concatenate([time_in, vec, num], axis=1)


def split_time(timestep, dataset):
    steps = timestep.reshape(-1)
    return jnp.concatenate([steps // 64, steps % 64, dataset.reshape(-1)]).astype(BF16)


def gather_all(x):
    return lax.all_gather(x, AXES, axis=0, tiled=True)


def shards(
    block_input,
    out_grad,
    timestep,
    dataset,
    lengths,
    norm1_gain,
    qkv_weight,
    out_weight,
    norm2_gain,
    up_weight,
    down_weight,
    time_in,
    time_out,
    data_embed,
    devices,
):
    flat = lax.axis_index(AXES)
    exchange = devices == 2 * CHIPS
    vectors = jnp.concatenate([norm1_gain[None], norm2_gain[None], data_embed.T], axis=0)
    numbers = split_time(timestep, dataset)
    count = numbers.shape[0] // 3
    micros, seqs, seq_len, width = block_input.shape
    tokens = micros * seqs * seq_len
    x_rows = block_input.reshape(tokens, width)
    grad_rows = out_grad.reshape(tokens, width)
    features = sinusoid(timestep.reshape(-1), time_in.shape[1] // 2).astype(BF16)
    if exchange:
        core = flat & 1
        chip = flat >> 1

        wide = lane_blocks(qkv_weight, (0, WIDTH, 2 * WIDTH), LANES)
        slim = lane_blocks(time_out, (0,), LANES)
        own, other = swap_halves(
            [jnp.concatenate([x, y], axis=0) for x, y in zip(wide, slim)], core
        )
        attention_piece = jnp.concatenate(
            [
                join_rows(own[:72], other[:72], core, 3),
                join_rows(own[72:], other[72:], core, 1),
                pack_extra(time_in, vectors, numbers),
            ],
            axis=0,
        )[None]
        near = [chip_swap(attention_piece, p) for p in (1, 2, 3)]
        up_weight, out_weight, down_weight, flat = lax.optimization_barrier(
            (up_weight, out_weight, down_weight, flat, attention_piece)
        )[:4]
        tab = position_table(flat >> 1, flat & 1, LINE_FIRST)
        later_tab = position_table(flat >> 1, flat & 1, LINE_LATER)
        wide = lane_blocks(up_weight, range(0, 4 * LANES, LANES), 4 * LANES)
        slim = lane_blocks(out_weight, (0,), LANES)
        own, other = swap_halves(
            [jnp.concatenate([x, y], axis=0) for x, y in zip(wide, slim)], core
        )
        up_piece = jnp.concatenate(
            [join_rows(own[:96], other[:96], core, 4), join_rows(own[96:], other[96:], core, 1)],
            axis=0,
        )[None]
        own, other = swap_halves(lane_blocks(down_weight, (0,), LANES), core)
        down_piece = join_rows(own, other, core, 1)[None]
        down_pair = jnp.concatenate([down_piece, chip_swap(down_piece, 1, LINE_LATER)], axis=0)
        ready = (up_piece, down_pair, tab, later_tab, features)
        line = after(jnp.concatenate([attention_piece] + near, axis=0), *ready)
        plane = chip_swap(line, 4)
        up_near = [chip_swap(after(up_piece, line), p) for p in (1, 2)]
        plane, up_near = together(plane, up_near)
        held = jnp.concatenate([line, plane], axis=0)
        far = chip_swap(held, 8)
        up_near.append(chip_swap(after(up_piece, plane), 3))
        up_line = lax.optimization_barrier(jnp.concatenate([up_piece] + up_near, axis=0))
        up_plane = chip_swap(up_line, 4)
        down_near = [chip_swap(after(down_pair, up_line), p, LINE_LATER) for p in (2, 4)]
        (far, up_plane), down_near = together((far, up_plane), down_near)
        attention_pieces = (held, far, core_swap(held), core_swap(far))
        up_held = jnp.concatenate([up_line, up_plane], axis=0)
        up_far = chip_swap(up_held, 8)
        down_last = chip_swap(after(down_pair, up_held), 6, LINE_LATER)
    else:
        tab = jnp.concatenate(
            [jnp.tile(jnp.arange(CHIPS, dtype=jnp.int32), 4), jnp.zeros((8,), jnp.int32)]
        )
        later_tab = tab
        full_qkv = gather_all(qkv_weight).reshape(CHIPS, 48, 3, 2, LANES)
        full_out = gather_all(out_weight).reshape(CHIPS, 48, 2, LANES)
        full_up = gather_all(up_weight).reshape(CHIPS, 48, 2, 4, LANES)
        full_down = gather_all(down_weight).reshape(CHIPS, 192, 2, LANES)
        full_tin = gather_all(time_in).reshape(CHIPS, 2, 16, 128)
        full_tout = gather_all(time_out).reshape(CHIPS, 32, 2, LANES)
        full_vec = lax.all_gather(vectors, AXES, axis=1, tiled=True).reshape(4, CHIPS, 2, 24)
        numbers_all = gather_all(numbers[None])
        extra = jnp.zeros((CHIPS, 2, 16, LANES), BF16)
        extra = extra.at[:, :, :, :128].set(full_tin)
        extra = extra.at[:, :, 0:4, 128:152].set(full_vec.transpose(1, 2, 0, 3))
        attention_pieces = []
        down_pieces = []
        up_pieces = []
        for half in (0, 1):
            wide = full_qkv[:, :, :, half].transpose(0, 2, 1, 3).reshape(CHIPS, 144, LANES)
            whole = jnp.concatenate([wide, full_tout[:, :, half], extra[:, half]], axis=1)
            attention_pieces += [whole[:8], whole[8:]]
            down_pieces += [full_down[:8, :, half], full_down[8:, :, half]]
            wide = full_up[:, :, half].transpose(0, 2, 1, 3).reshape(CHIPS, 192, LANES)
            whole = jnp.concatenate([wide, full_out[:, :, half]], axis=1)
            up_pieces += [whole[:8], whole[8:]]

    arrivals = []
    if exchange:
        x_rows = after(x_rows, up_held)
        arrivals = [up_far]
    forward = attention_forward(tab, lengths, dataset, attention_pieces, x_rows, features)
    (normed, qkv, embed, vecs, seen, probs, att), arrivals = together(forward, arrivals)
    seen = seen[:, :, 0, : 3 * count].reshape(2 * CHIPS, 3 * count) if exchange else numbers_all
    steps = seen[:, :count] * 64 + seen[:, count : 2 * count].astype(F32)
    wave = sinusoid(steps.reshape(-1), time_in.shape[1] // 2).astype(BF16)
    wave = jnp.pad(wave.reshape(devices, count, -1), ((0, 0), (0, 16 - count), (0, 0)))
    wave = wave.reshape(devices * 16, -1)
    which = jnp.pad(seen[:, 2 * count :], ((0, 0), (0, 16 - count))).reshape(-1)
    place = jnp.tile(jnp.arange(16), devices)
    hot = jnp.stack(
        [(place < count) & (which == 0), (place < count) & (which == 1), place == 8, place == 9]
    )
    hot = jnp.pad(hot.astype(BF16), ((0, 12), (0, 0)))
    pre = dot_last(wave, time_in)
    gate = 1.0 / (1.0 + jnp.exp(-pre))
    hidden = (pre * gate).astype(BF16)
    slope_pre = gate * (1.0 + pre * (1.0 - gate))
    if exchange:
        (up_far,) = arrivals
        down_near = [after(x, embed) for x in [down_pair] + down_near + [down_last]]
        up_pieces = (up_held, up_far, core_swap(up_held), core_swap(up_far))
        down_held = jnp.concatenate(down_near, axis=0)
        att, wave, hot, hidden, slope_pre, down_held = lax.optimization_barrier(
            (att, wave, hot, hidden, slope_pre, down_held)
        )
        arrivals = chip_swap(down_held, 8, LINE_LATER)
    forward = up_forward(tab, up_pieces, att, x_rows, grad_rows, embed, vecs)
    (mid, two, act, slope, down_theirs), arrivals = together(forward, arrivals)
    if exchange:
        down_far = arrivals
        down_sum = Scatter(down_theirs)
        arrivals = [core_swap(down_held), core_swap(down_far)], down_sum.swap()
    (down_mine, act, slope), arrivals = together(down_grad(tab, act, grad_rows, slope), arrivals)
    if exchange:
        down_pieces = (down_held, down_far, *arrivals[0])
        down_sum.land(arrivals[1], down_mine)
        slope = after(slope, *down_sum.send())
        arrivals = down_sum.fly()
    backward = mlp_backward(
        tab, later_tab, up_pieces, down_pieces, two, att, slope, grad_rows, mid, vecs
    )
    backward, arrivals = together(backward, arrivals)
    grad_mid, branch, grad_up, grad_att, gain_two, up_theirs = backward
    if exchange:
        down_sum.land(arrivals)
        up_sum = Scatter(up_theirs)
        grad_up = after(grad_up, *down_sum.send())
        arrivals = down_sum.fly(), up_sum.swap()
    up_mine, arrivals = together(up_grad(tab, att, branch, two, grad_up), arrivals)
    if exchange:
        down_sum.land(arrivals[0])
        up_sum.land(arrivals[1], up_mine)
        grad_att = after(grad_att, *up_sum.send(), *down_sum.send())
        arrivals = up_sum.fly(), down_sum.fly()
    backward = attention_backward(tab, normed, qkv, probs, grad_att)
    (grad_qkv, mine_qkv, att_theirs), arrivals = together(backward, arrivals)
    if exchange:
        up_sum.land(arrivals[0])
        down_sum.land(arrivals[1])
        down_total = down_sum.total()
        att_sum = Scatter(att_theirs)
        mine_qkv = after(mine_qkv, *up_sum.send(), down_total)
        arrivals = up_sum.fly(), att_sum.swap()
    backward = qkv_grad(tab, later_tab, down_pieces, normed, mine_qkv, act, mid)
    (att_mine, result), arrivals = together(backward, arrivals)
    if exchange:
        up_sum.land(arrivals[0])
        att_sum.land(arrivals[1], att_mine)
        grad_qkv = after(grad_qkv, *att_sum.send(), *up_sum.send())
        *up_near, up_last = up_sum.fly()
        arrivals = att_sum.fly(), up_near
    backward = input_backward(
        tab, attention_pieces, grad_qkv, x_rows, embed, vecs, grad_mid, gain_two
    )
    (grad_input, small), arrivals = together(backward, arrivals)

    small = small.astype(BF16)[None]
    if exchange:
        att_sum.land(arrivals[0])
        up_sum.land(arrivals[1])
        att_sum.send()
        near = [chip_swap(small, p) for p in (1, 2, 3)]
        brought, near = together(att_sum.fly(), near)
        att_sum.land(brought)
        small_line = jnp.concatenate([small] + near, axis=0)
        att_sum.send()
        brought = att_sum.fly()
        small_line, brought[1] = lax.optimization_barrier((small_line, brought[1]))
        plane = [small_line] + [chip_swap(small_line, p) for p in (4, 8, 12)]
        every = jnp.concatenate(plane, axis=0)
        every = every, core_swap(every)
        brought, up_last = together(brought, up_last)
        att_sum.land(brought)
        up_sum.land([up_last])
        sums = after(down_total, small_line), after(up_sum.total(), small_line), att_sum.total()
        pieces = [x for total in sums for x in (total, core_swap(total))]
        finished = finish_grads(
            tab, every, wave, hot, hidden, slope_pre, time_out, pieces
        )
        grad_tin, grad_tout, gain_one, gain_two, grad_data, *weights = finished
        grad_down, grad_up_weight, grad_out, grad_qkv_weight = weights
    else:
        every = gather_all(small).reshape(devices * 16, width)
        grad_tout = dot_first(hidden, every)
        grad_pre = dot_last(every, time_out) * slope_pre
        grad_tin = dot_first(grad_pre.astype(BF16), wave)
        own_cols = norm1_gain.shape[0]
        sums = lax.dynamic_slice_in_dim(dot(hot, every), flat * own_cols, own_cols, 1)
        grad_data, gain_one, gain_two = sums[0:2], sums[2], sums[3]
        scatter = partial(lax.psum_scatter, axis_name=AXES, scatter_dimension=0, tiled=True)
        both = jnp.stack([down_mine, down_theirs]).astype(F32)
        grad_down = scatter(both.transpose(1, 2, 0, 3).reshape(FF, WIDTH))
        both = jnp.stack([up_mine, up_theirs]).astype(F32)
        grad_out = scatter(both[:, :, 192:].transpose(1, 2, 0, 3).reshape(WIDTH, WIDTH))
        both = both[:, :, :192].reshape(2, CHIPS, 4, 48, LANES)
        grad_up_weight = scatter(both.transpose(1, 3, 0, 2, 4).reshape(WIDTH, FF))
        both = jnp.stack([att_mine, att_theirs]).astype(F32).reshape(2, CHIPS, 3, 48, LANES)
        grad_qkv_weight = scatter(both.transpose(1, 3, 2, 0, 4).reshape(WIDTH, 3 * WIDTH))

    return (
        result.reshape(block_input.shape),
        grad_input.reshape(block_input.shape),
        gain_one.reshape(-1),
        grad_qkv_weight,
        grad_out,
        gain_two.reshape(-1),
        grad_up_weight,
        grad_down,
        grad_tin,
        grad_tout,
        grad_data.T,
    )


def solution(mesh):
    devices = mesh.shape["dp"] * mesh.shape["fsdp"]
    seq_spec = P(None, AXES, None, None)
    int_spec = P(None, AXES)
    row_spec = P(AXES, None)
    in_specs = (seq_spec, seq_spec, int_spec, int_spec, int_spec, P(AXES), row_spec, row_spec, P(AXES))
    in_specs = in_specs + (row_spec,) * 5
    out_specs = (seq_spec, seq_spec, P(AXES), row_spec, row_spec, P(AXES)) + (row_spec,) * 5
    return jax.shard_map(
        partial(shards, devices=devices),
        mesh=mesh,
        in_specs=in_specs,
        out_specs=out_specs,
        check_vma=False,
    )
```

```python
from functools import partial
import math

import jax
import jax.numpy as jnp
from jax import lax
from jax.experimental import pallas as pl
from jax.experimental.pallas import tpu as pltpu
from jax.sharding import PartitionSpec as P

HEAD_DIM = 64
AXES = ("dp", "fsdp")
LANES = 384
CHIPS = 16
WIDTH = 768
FF = 3072
F32 = jnp.float32
BF16 = jnp.bfloat16
NEG = -1000000000.0


def sinusoid(timestep, half_width):
    frequency = jnp.exp(-math.log(10000.0) * jnp.arange(half_width, dtype=F32) / half_width)
    angles = timestep.astype(F32)[:, None] * frequency[None, :]
    return jnp.concatenate([jnp.cos(angles), jnp.sin(angles)], axis=-1)


def dot(left, right):
    return jnp.dot(left, right, preferred_element_type=F32)


def dot_last(left, right):
    return lax.dot_general(left, right, (((1,), (1,)), ((), ())), preferred_element_type=F32)


def dot_first(left, right):
    return lax.dot_general(left, right, (((0,), (0,)), ((), ())), preferred_element_type=F32)


def positions(masks):
    return [sum(masks[b] for b in range(4) if (p >> b) & 1) for p in range(CHIPS)]


LINE_FIRST = ((2, 1, 8, 4), (2, 1, 4, 8))
LINE_LATER = ((8, 2, 1, 4), (4, 2, 1, 8))


def core_swap(x):
    return lax.ppermute(x, AXES, [(i, i ^ 1) for i in range(2 * CHIPS)])


def chip_swap(x, position, order=LINE_FIRST):
    far = [positions(masks)[position] * 2 for masks in order]
    return lax.ppermute(x, AXES, [(i, i ^ far[i & 1]) for i in range(2 * CHIPS)])


def after(x, *others):
    return lax.optimization_barrier((x,) + others)[0]


def gather_line(piece):
    return jnp.concatenate([piece] + [chip_swap(piece, p) for p in (1, 2, 3)], axis=0)


def gather_plane(held):
    return jnp.concatenate([held, chip_swap(held, 4)], axis=0)


def together(outs, arrivals):
    return lax.optimization_barrier((outs, arrivals))


class Scatter:
    def __init__(self, theirs):
        self.parts = []
        self.steps = [(8,), (4,), (1, 2, 3)]
        self.theirs = theirs

    def swap(self):
        return [core_swap(self.theirs)]

    def land(self, brought, *own):
        self.parts += [*brought, *own]

    def sum(self, start, stop):
        total = self.parts[0][start:stop].astype(F32)
        for part in self.parts[1:]:
            total = total + part[start:stop].astype(F32)
        return total

    def send(self):
        self.at = self.steps.pop(0)
        size = 1 if len(self.at) == 3 else self.at[0]
        self.sent = [self.sum(p, p + size).astype(BF16) for p in self.at]
        self.parts = [self.sum(0, size)]
        return [*self.sent, self.parts[0]]

    def fly(self):
        return [chip_swap(x, p) for x, p in zip(self.sent, self.at)]

    def total(self):
        return self.sum(0, 1)[0]


VMEM_SPEC = pl.BlockSpec(memory_space=pltpu.VMEM)
SMEM_SPEC = pl.BlockSpec(memory_space=pltpu.SMEM)
ANY_SPEC = pl.BlockSpec(memory_space=pl.ANY)


def tiles(rows, cols):
    return pl.BlockSpec((rows, cols), lambda i: (i, 0))


def columns(rows, cols):
    return pl.BlockSpec((rows, cols), lambda i: (0, i))


def fixed(*shape):
    return pl.BlockSpec(shape, lambda i: (0,) * len(shape))


def shaped(shape, dtype=BF16):
    return pltpu.HBM(shape, dtype)


def local(shape, dtype=BF16):
    return pltpu.VMEM(shape, dtype)


def params(mib):
    return pltpu.CompilerParams(vmem_limit_bytes=mib * 1024 * 1024)


def kernel_call(kernel, **kwargs):
    call = pl.pallas_call(kernel, **kwargs)
    if "grid_spec" in kwargs:
        grid_spec = kwargs["grid_spec"]
        specs = [SMEM_SPEC] * grid_spec.num_scalar_prefetch + list(grid_spec.in_specs)
    else:
        specs = kwargs["in_specs"]

    def place(x, spec):
        if spec is SMEM_SPEC:
            return x
        space = pltpu.VMEM if spec is VMEM_SPEC else pltpu.HBM
        return pltpu.with_memory_space_constraint(x, space)

    def run(*operands):
        return call(*[place(x, spec) for x, spec in zip(operands, specs, strict=True)])

    return run


def cost(flops, nbytes, transcendentals=0):
    return pl.CostEstimate(flops=flops, bytes_accessed=nbytes, transcendentals=transcendentals)


def ln_stats(v):
    center = v - jnp.mean(v, axis=-1, keepdims=True)
    scale = lax.rsqrt(jnp.mean(center * center, axis=-1, keepdims=True) + 1e-05)
    return center * scale, scale


def ln_back(y, gain, xhat, scale):
    yg = y * gain
    return scale * (
        yg - jnp.mean(yg, axis=-1, keepdims=True) - xhat * jnp.mean(yg * xhat, axis=-1, keepdims=True)
    )


def first_core(tab):
    return tab[64]


def each_piece(tab, parts, fn):
    core = first_core(tab)
    for side in (0, 1):
        half = core if side == 0 else 1 - core
        for group in (0, 1):
            part = parts[side * 2 + group]

            def body(q, _, part=part, side=side, group=group, half=half):
                chip = tab[side * CHIPS + group * 8 + q]
                fn(part.at[q], chip, half)
                return 0

            lax.fori_loop(0, 8, body, 0)


def rows_of(chip, size):
    return pl.ds(pl.multiple_of(chip * size, size), size)


def lanes_of(half, size, base=0):
    return pl.ds(pl.multiple_of(half * size + base, 128), LANES)


def fetch_pieces(tab, parts, rows, dst, sem, first=0):
    each_piece(
        tab,
        parts,
        lambda src, chip, half: pltpu.make_async_copy(
            src.at[pl.ds(first, rows), :], dst.at[chip, half], sem
        ).start(),
    )


def block(pieces, half, first, rows=48):
    return pieces[:, half, first : first + rows, :].reshape(CHIPS * rows, LANES)


def both_halves(pieces, first, rows=48):
    return jnp.concatenate([block(pieces, h, first, rows) for h in (0, 1)], axis=1)


def down_rows(pieces, j):
    chips = pl.ds(4 * j, 4)
    return jnp.concatenate([pieces[chips, h].reshape(WIDTH, LANES) for h in (0, 1)], axis=1)


def qkv_columns(pieces, half):
    return jnp.concatenate([block(pieces, half, 48 * sec) for sec in range(3)], axis=1)


def finish(ref, sem):
    pltpu.make_async_copy(ref, ref, sem).wait()


def add_embed(x, embed, i):
    seqs = x.shape[0] // 128
    parts = [
        x[128 * k : 128 * k + 128].astype(F32) + embed[pl.ds(i * seqs + k, 1), :]
        for k in range(seqs)
    ]
    return jnp.concatenate(parts, axis=0)


def two_heads(x, low_half):
    none = jnp.zeros_like(x)
    return jnp.concatenate([jnp.where(low_half, x, none), jnp.where(low_half, none, x)], axis=0)


def side_by_side(x):
    return jnp.concatenate([x[:128], x[128:]], axis=1)


def pair_base(pair):
    return (pair // 3) * 3 * LANES + (pair % 3) * 128


def attention_tile(lengths, qkv_ref, probs_ref, att_ref):
    low_half = lax.broadcasted_iota(jnp.int32, (128, 128), 1) < HEAD_DIM
    lane = lax.broadcasted_iota(jnp.int32, (256, 128), 1)
    keep = [lane < length for length in lengths]
    units = [(k, pair) for k in range(2) for pair in range(6)]

    def part(k, pair, section):
        base = pair_base(pair) + section * LANES
        return qkv_ref[128 * k : 128 * k + 128, base : base + 128]

    scores = []
    for k, pair in units:
        query = two_heads(part(k, pair, 0), low_half)
        score = dot_last(query, part(k, pair, 1)) * HEAD_DIM ** (-0.5)
        scores.append(jnp.where(keep[k], score, NEG))
    probs = []
    for (k, pair), score in zip(units, scores):
        shifted = jnp.exp(score - jnp.max(score, axis=-1, keepdims=True))
        total = jnp.sum(shifted, axis=-1, keepdims=True)
        probs.append((shifted * (1.0 / total)).astype(BF16))
        first = 256 * (6 * k + pair)
        probs_ref[first : first + 256, :] = probs[-1]
    for (k, pair), prob in zip(units, probs):
        value = two_heads(part(k, pair, 2), low_half)
        att_ref[128 * k : 128 * k + 128, pair * 128 : pair * 128 + 128] = dot(
            side_by_side(prob), value
        ).astype(BF16)


def attention_kernel(
    tab, lens, sets, g_a, g_b, g_c, g_d, x_ref, feat_ref,
    normed_ref, qkv_ref, te_ref, vec_ref, seen_ref, probs_ref, att_ref,
    w, w_time, sem, sem_time,
):
    i = pl.program_id(0)

    @pl.when(i == 0)
    def _():
        fetch_pieces(tab, (g_a, g_b, g_c, g_d), 48, w_time, sem_time, 144)
        fetch_pieces(tab, (g_a, g_b, g_c, g_d), 144, w, sem)
        finish(w_time, sem_time)
        lane = lax.broadcasted_iota(jnp.int32, (128, WIDTH), 1)
        spread = (lax.broadcasted_iota(jnp.int32, (128, WIDTH), 0) == lane % 24).astype(BF16)
        vectors = jnp.zeros((16, WIDTH), F32)
        embed = jnp.zeros((8, WIDTH), F32)
        for owner in (0, 1):
            extra = block(w_time, owner, 32, 16)
            wide = dot(extra[:, 128:256], spread)
            chip = lax.broadcasted_iota(jnp.int32, (256, WIDTH), 0) // 16
            place = lax.broadcasted_iota(jnp.int32, (256, WIDTH), 1) // 24
            wide = jnp.where(place == chip * 2 + owner, wide, 0.0)
            vectors = vectors + jnp.sum(wide.reshape(CHIPS, 16, WIDTH), axis=0)
            pre = dot_last(feat_ref[...], extra[:, 0:128])
            hidden = (pre / (1.0 + jnp.exp(-pre))).astype(BF16)
            embed = embed + dot(hidden, both_halves(w_time, 16 * owner, 16))
            seen_ref[owner] = w_time[:, owner, 32:48, 256:]
        vec_ref[...] = vectors
        for s in range(8):
            chosen = jnp.where(sets[s // 4, s % 4] == 1, vectors[3:4, :], vectors[2:3, :])
            te_ref[s : s + 1, :] = embed[s : s + 1, :] + chosen

    xhat, _unused = ln_stats(add_embed(x_ref[...], te_ref, i))
    normed_ref[...] = (xhat * vec_ref[0:1, :]).astype(BF16)

    @pl.when(i == 0)
    def _():
        finish(w, sem)

    for half in (0, 1):
        cols = slice(half * 3 * LANES, (half + 1) * 3 * LANES)
        qkv_ref[:, cols] = dot(normed_ref[...], qkv_columns(w, half)).astype(BF16)
    lengths = [lens[i // 2, i % 2 * 2 + k] for k in range(2)]
    attention_tile(lengths, qkv_ref, probs_ref, att_ref)


def attention_forward(tab, lens, sets, pieces, rows, features):
    row = tiles(256, WIDTH)
    return kernel_call(
        attention_kernel,
        grid=(4,),
        out_shape=(
            shaped((1024, WIDTH)),
            shaped((1024, 3 * WIDTH)),
            shaped((8, WIDTH), F32),
            shaped((16, WIDTH), F32),
            shaped((2, CHIPS, 16, 128)),
            shaped((48 * 256, 128)),
            shaped((1024, WIDTH)),
        ),
        in_specs=[SMEM_SPEC] * 3 + [ANY_SPEC] * 4 + [row, fixed(8, 128)],
        out_specs=(
            row, tiles(256, 3 * WIDTH), fixed(8, WIDTH), fixed(16, WIDTH),
            fixed(2, CHIPS, 16, 128), tiles(12 * 256, 128), row,
        ),
        scratch_shapes=[
            pltpu.VMEM((CHIPS, 2, 144, LANES), BF16),
            pltpu.VMEM((CHIPS, 2, 48, LANES), BF16),
            pltpu.SemaphoreType.DMA,
            pltpu.SemaphoreType.DMA,
        ],
        compiler_params=params(26),
        cost_estimate=cost(8_000_000_000, 20_000_000, 1_600_000),
        name="attention_forward",
    )(tab, lens, sets, *pieces, rows, features)


def gelu_parts(u):
    cdf = 0.5 + 0.5 * lax.erf(u * math.sqrt(0.5))
    return cdf, jnp.exp(u * u * -0.5) * (1.0 / math.sqrt(2.0 * math.pi))


def up_columns(pieces, half, j):
    return jnp.concatenate(
        [block(pieces, half, 96 * j), block(pieces, half, 96 * j + 48)], axis=1
    )


def half_of(tab, side):
    return first_core(tab) if side == 0 else 1 - first_core(tab)


def clamped(rows, cols):
    return pl.BlockSpec((rows, cols), lambda i: (jnp.minimum(i, 3), 0))


def down_grad_rows(tab, side, j, act, out_grad, out_ref):
    lanes = lanes_of(half_of(tab, side), LANES)
    grad = dot_first(act, out_grad[:, lanes]).astype(BF16)
    for k in range(4):
        place = tab[32 + side * CHIPS + j * 4 + k]
        out_ref[place, :, :] = grad[192 * k : 192 * k + 192, :]


def up_kernel(
    tab, u_a, u_b, u_c, u_d, out_grad_ref, att_ref, x_ref, te_ref, vec_ref,
    mid_ref, two_ref, act_ref, slope_ref, theirs_ref,
    w, w_out, sem, sem_out,
):
    i = pl.program_id(0)
    parts = (u_a, u_b, u_c, u_d)

    def token_rows(arrived):
        rows = rows_of(i, 256)
        mid = add_embed(x_ref[...], te_ref, i) + dot(att_ref[...], both_halves(w_out, 0))
        mid_ref[...] = mid
        xhat, _unused = ln_stats(mid)
        two = (xhat * vec_ref[1:2, :]).astype(BF16)
        two_ref[...] = two
        arrived()
        for j in range(4):
            up = dot(two, up_columns(w, j // 2, j % 2))
            cdf, density = gelu_parts(up)
            act_ref[j, rows, :] = (up * cdf).astype(BF16)
            slope_ref[j, rows, :] = (cdf + up * density).astype(BF16)

    @pl.when(i == 0)
    def _():
        fetch_pieces(tab, parts, 48, w_out, sem_out, 192)
        fetch_pieces(tab, parts, 192, w, sem)
        finish(w_out, sem_out)
        token_rows(lambda: finish(w, sem))

    @pl.when((i > 0) & (i < 4))
    def _():
        token_rows(lambda: None)

    @pl.when(i >= 4)
    def _():
        down_grad_rows(tab, 1, i - 4, act_ref[i - 4], out_grad_ref, theirs_ref)


def up_forward(tab, pieces, att, rows, out_grad, embed, vectors):
    row = clamped(256, WIDTH)
    return kernel_call(
        up_kernel,
        grid=(8,),
        out_shape=(
            shaped((1024, WIDTH), F32),
            shaped((1024, WIDTH)),
            local((4, 1024, WIDTH)),
            local((4, 1024, WIDTH)),
            local((CHIPS, 192, LANES)),
        ),
        in_specs=[SMEM_SPEC]
        + [ANY_SPEC] * 4
        + [VMEM_SPEC, row, row, fixed(8, WIDTH), fixed(16, WIDTH)],
        out_specs=(row, row) + (VMEM_SPEC,) * 3,
        scratch_shapes=[
            pltpu.VMEM((CHIPS, 2, 192, LANES), BF16),
            pltpu.VMEM((CHIPS, 2, 48, LANES), BF16),
            pltpu.SemaphoreType.DMA,
            pltpu.SemaphoreType.DMA,
        ],
        compiler_params=params(26),
        cost_estimate=cost(10_000_000_000, 30_000_000, 6_000_000),
        name="up_forward",
    )(tab, *pieces, out_grad, att, rows, embed, vectors)


def down_grad_kernel(tab, act_ref, out_grad_ref, _slope, out_ref, act_hbm, _slope_out, sem):
    j = pl.program_id(0)

    @pl.when(j == 0)
    def _():
        pltpu.make_async_copy(act_ref, act_hbm, sem).start()

    down_grad_rows(tab, 0, j, act_ref[j], out_grad_ref, out_ref)

    @pl.when(j == 3)
    def _():
        pltpu.make_async_copy(act_ref, act_hbm, sem).wait()


def down_grad(tab, act, out_grad, slope):
    return kernel_call(
        down_grad_kernel,
        grid=(4,),
        out_shape=(
            local((CHIPS, 192, LANES)), shaped((4, 1024, WIDTH)), local((4, 1024, WIDTH))
        ),
        in_specs=[SMEM_SPEC] + [VMEM_SPEC] * 3,
        out_specs=(VMEM_SPEC, ANY_SPEC, VMEM_SPEC),
        input_output_aliases={3: 2},
        scratch_shapes=[pltpu.SemaphoreType.DMA],
        compiler_params=params(12),
        cost_estimate=cost(3_000_000_000, 10_000_000),
        name="down_grad",
    )(tab, act, out_grad, slope)


def store_blocks(tab, side, target, first, part, lanes):
    for chip in range(CHIPS):
        place = tab[32 + side * CHIPS + chip]
        target[place, pl.ds(first, 48), :] = part[48 * chip : 48 * chip + 48, lanes]


def out_grad_rows(tab, side, att, branch, out_ref, part):
    lanes = lanes_of(half_of(tab, side), LANES)
    part[:, 0:LANES] = dot_first(att[...], branch[:, lanes]).astype(BF16)
    store_blocks(tab, side, out_ref, 192, part, slice(0, LANES))


def up_grad_rows(tab, side, j, two, grad_up, out_ref, part):
    part[...] = dot_first(two, grad_up).astype(BF16)
    for b in range(2):
        first = pl.multiple_of((2 * j + b) * 48, 48)
        store_blocks(tab, side, out_ref, first, part, slice(b * LANES, (b + 1) * LANES))


def up_grad_kernel(
    tab, att_hbm, two_hbm, branch_ref, grad_up_ref, out_ref, att, two, part, sem_att, sem_two
):
    j = pl.program_id(0)

    @pl.when(j == 0)
    def _():
        pltpu.make_async_copy(att_hbm, att, sem_att).start()
        pltpu.make_async_copy(two_hbm, two, sem_two).start()
        finish(att, sem_att)
        out_grad_rows(tab, 0, att, branch_ref, out_ref, part)
        finish(two, sem_two)

    @pl.when(j > 0)
    def _():
        up_grad_rows(tab, 0, j - 1, two[...], grad_up_ref[j - 1], out_ref, part)


def up_grad(tab, att, branch, two, grad_up):
    return kernel_call(
        up_grad_kernel,
        grid=(3,),
        out_shape=local((CHIPS, 240, LANES)),
        in_specs=[SMEM_SPEC] + [ANY_SPEC] * 2 + [VMEM_SPEC] * 2,
        out_specs=VMEM_SPEC,
        scratch_shapes=[pltpu.VMEM((1024, WIDTH), BF16)] * 2
        + [pltpu.VMEM((WIDTH, WIDTH), BF16)]
        + [pltpu.SemaphoreType.DMA] * 2,
        compiler_params=params(16),
        cost_estimate=cost(3_200_000_000, 11_000_000),
        name="up_grad",
    )(tab, att, two, branch, grad_up)


def mlp_backward_kernel(
    tab, later_tab, u_a, u_b, u_c, u_d, d_a, d_b, d_c, d_d,
    two_hbm, att_hbm, slope_ref, out_grad_ref, mid_ref, vec_ref,
    grad_mid_ref, branch_ref, mine_up_ref, grad_att_ref, gain_ref, theirs_ref,
    w, w_down, two, att, theirs_up, part, sem, sem_down, sem_two, sem_att,
):
    i = pl.program_id(0)
    grad_up = [
        (half_of(tab, side), j, target)
        for side, target in enumerate((mine_up_ref, theirs_up))
        for j in range(2)
    ]

    @pl.when(i == 0)
    def _():
        fetch_pieces(later_tab, (d_a, d_b, d_c, d_d), 192, w_down, sem_down)
        gain_ref[...] = jnp.zeros_like(gain_ref)
        finish(w_down, sem_down)
        fetch_pieces(tab, (u_a, u_b, u_c, u_d), 240, w, sem)

    @pl.when(i < 4)
    def _():
        rows = rows_of(i, 256)
        for half, j, target in grad_up:
            grad_act = dot_last(out_grad_ref[rows, :], down_rows(w_down, 2 * half + j))
            slope = slope_ref[2 * half + j, rows, :].astype(F32)
            target[j, rows, :] = (grad_act * slope).astype(BF16)

    @pl.when(i == 4)
    def _():
        finish(w, sem)
        pltpu.make_async_copy(two_hbm, two, sem_two).start()
        pltpu.make_async_copy(att_hbm, att, sem_att).start()

    @pl.when((i >= 4) & (i < 8))
    def _():
        rows = rows_of(i - 4, 256)
        y = jnp.zeros((256, WIDTH), F32)
        for half, j, target in grad_up:
            y = y + dot_last(target[j, rows, :], up_columns(w, half, j))
        xhat, scale = ln_stats(mid_ref[...])
        grad = out_grad_ref[rows, :].astype(F32) + ln_back(y, vec_ref[1:2, :], xhat, scale)
        grad_mid_ref[...] = grad
        branch = grad.astype(BF16)
        branch_ref[rows, :] = branch
        gain_ref[...] += jnp.sum(y * xhat, axis=0, keepdims=True)
        grad_att_ref[rows, :] = dot_last(branch, both_halves(w, 192)).astype(BF16)

    @pl.when(i == 8)
    def _():
        finish(two, sem_two)
        finish(att, sem_att)
        out_grad_rows(tab, 1, att, branch_ref, theirs_ref, part)

    @pl.when(i >= 8)
    def _():
        up_grad_rows(tab, 1, i - 8, two[...], theirs_up[i - 8], theirs_ref, part)


def mlp_backward(
    tab, later_tab, up_pieces, down_pieces, two, att, slope, out_grad, mid, vectors
):
    row = pl.BlockSpec((256, WIDTH), lambda i: (jnp.clip(i - 4, 0, 3), 0))
    return kernel_call(
        mlp_backward_kernel,
        grid=(10,),
        out_shape=(
            shaped((1024, WIDTH), F32),
            local((1024, WIDTH)),
            local((2, 1024, WIDTH)),
            local((1024, WIDTH)),
            local((1, WIDTH), F32),
            local((CHIPS, 240, LANES)),
        ),
        in_specs=[SMEM_SPEC] * 2
        + [ANY_SPEC] * 10
        + [VMEM_SPEC] * 2
        + [row, fixed(16, WIDTH)],
        out_specs=(row,) + (VMEM_SPEC,) * 5,
        scratch_shapes=[
            pltpu.VMEM((CHIPS, 2, 240, LANES), BF16),
            pltpu.VMEM((CHIPS, 2, 192, LANES), BF16),
            pltpu.VMEM((1024, WIDTH), BF16),
            pltpu.VMEM((1024, WIDTH), BF16),
            pltpu.VMEM((2, 1024, WIDTH), BF16),
            pltpu.VMEM((WIDTH, WIDTH), BF16),
        ]
        + [pltpu.SemaphoreType.DMA] * 4,
        compiler_params=params(38),
        cost_estimate=cost(18_000_000_000, 50_000_000),
        name="mlp_backward",
    )(tab, later_tab, *up_pieces, *down_pieces, two, att, slope, out_grad, mid, vectors)


def attention_backward_tile(first_row, qkv_ref, probs_ref, grad_att_ref, grad_qkv_ref):
    low_half = lax.broadcasted_iota(jnp.int32, (128, 128), 1) < HEAD_DIM
    units = [(k, pair) for k in range(2) for pair in range(6)]

    def rows(k):
        return slice(128 * k, 128 * k + 128)

    def part(k, pair, section):
        base = pair_base(pair) + section * LANES
        return qkv_ref[rows(k), base : base + 128]

    def up(k, pair):
        whole = pl.ds(pl.multiple_of(first_row + 128 * k, 128), 128)
        return two_heads(grad_att_ref[whole, pair * 128 : pair * 128 + 128], low_half)

    def probs_of(k, pair):
        first = 256 * (6 * k + pair)
        return probs_ref[first : first + 256, :]

    def store(k, pair, section, value):
        base = pair_base(pair) + section * LANES
        grad_qkv_ref[rows(k), base : base + 128] = value.astype(BF16)

    grad_probs = [dot_last(up(k, pair), part(k, pair, 2)) for k, pair in units]
    grad_scores = []
    for (k, pair), grad in zip(units, grad_probs):
        probs = probs_of(k, pair).astype(F32)
        inner = jnp.sum(probs * grad, axis=-1, keepdims=True)
        grad_scores.append((probs * (grad - inner)).astype(BF16))
    for (k, pair), grad in zip(units, grad_scores):
        grad_query = dot(side_by_side(grad), two_heads(part(k, pair, 1), low_half))
        store(k, pair, 0, grad_query * HEAD_DIM ** (-0.5))
        grad_key = dot_first(grad, two_heads(part(k, pair, 0), low_half))
        store(k, pair, 1, grad_key * HEAD_DIM ** (-0.5))
        store(k, pair, 2, dot_first(probs_of(k, pair), up(k, pair)))


def qkv_grad_rows(tab, side, normed, grad_qkv, out_ref, part):
    part[...] = dot_first(normed, grad_qkv).astype(BF16)
    for sec in range(3):
        store_blocks(tab, side, out_ref, 48 * sec, part, slice(sec * LANES, (sec + 1) * LANES))


def attention_backward_kernel(
    tab, normed_hbm, qkv_ref, probs_ref, grad_att_ref, grad_qkv_ref, mine_ref, theirs_ref,
    normed, kept, part, sem,
):
    i = pl.program_id(0)

    @pl.when(i == 0)
    def _():
        pltpu.make_async_copy(normed_hbm, normed, sem).start()

    @pl.when(i < 4)
    def _():
        attention_backward_tile(i * 256, qkv_ref, probs_ref, grad_att_ref, grad_qkv_ref)
        for side, target in enumerate((mine_ref, kept)):
            lanes = pl.ds(pl.multiple_of(half_of(tab, side) * 3 * LANES, 128), 3 * LANES)
            target[rows_of(i, 256), :] = grad_qkv_ref[:, lanes]

    @pl.when(i == 4)
    def _():
        finish(normed, sem)
        qkv_grad_rows(tab, 1, normed[...], kept[...], theirs_ref, part)


def attention_backward(tab, normed, qkv, probs, grad_att):
    wide = clamped(256, 3 * WIDTH)
    return kernel_call(
        attention_backward_kernel,
        grid=(5,),
        out_shape=(
            shaped((1024, 3 * WIDTH)), local((1024, 3 * LANES)), local((CHIPS, 144, LANES))
        ),
        in_specs=[SMEM_SPEC, ANY_SPEC, wide, clamped(12 * 256, 128), VMEM_SPEC],
        out_specs=(wide, VMEM_SPEC, VMEM_SPEC),
        scratch_shapes=[
            pltpu.VMEM((1024, WIDTH), BF16),
            pltpu.VMEM((1024, 3 * LANES), BF16),
            pltpu.VMEM((WIDTH, 3 * LANES), BF16),
            pltpu.SemaphoreType.DMA,
        ],
        compiler_params=params(28),
        cost_estimate=cost(11_000_000_000, 22_000_000),
        name="attention_backward",
    )(tab, normed, qkv, probs, grad_att)


def qkv_grad_kernel(
    tab, later_tab, d_a, d_b, d_c, d_d, normed_ref, grad_qkv_ref, act_ref, mid_ref,
    out_ref, result_ref,
    part, w_down, sem,
):
    i = pl.program_id(0)

    @pl.when(i == 0)
    def _():
        fetch_pieces(later_tab, (d_a, d_b, d_c, d_d), 192, w_down, sem)
        qkv_grad_rows(tab, 0, normed_ref[...], grad_qkv_ref[...], out_ref, part)
        finish(w_down, sem)

    @pl.when(i > 0)
    def _():
        total = mid_ref[...]
        for j in range(4):
            total = total + dot(act_ref[j], down_rows(w_down, j))
        result_ref[...] = total.astype(BF16)


def qkv_grad(tab, later_tab, pieces, normed, grad_qkv, act, mid):
    row = pl.BlockSpec((256, WIDTH), lambda i: (jnp.maximum(i - 1, 0), 0))
    wide = pl.BlockSpec((4, 256, WIDTH), lambda i: (0, jnp.maximum(i - 1, 0), 0))
    return kernel_call(
        qkv_grad_kernel,
        grid=(5,),
        out_shape=(local((CHIPS, 144, LANES)), shaped((1024, WIDTH))),
        in_specs=[SMEM_SPEC] * 2 + [ANY_SPEC] * 4 + [fixed(1024, WIDTH), VMEM_SPEC, wide, row],
        out_specs=(VMEM_SPEC, row),
        scratch_shapes=[
            pltpu.VMEM((WIDTH, 3 * LANES), BF16),
            pltpu.VMEM((CHIPS, 2, 192, LANES), BF16),
            pltpu.SemaphoreType.DMA,
        ],
        compiler_params=params(26),
        cost_estimate=cost(7_000_000_000, 22_000_000),
        name="qkv_grad",
    )(tab, later_tab, *pieces, normed, grad_qkv, act, mid)


def input_backward_kernel(
    tab, g_a, g_b, g_c, g_d, grad_qkv_ref, x_ref, te_ref, vec_ref, grad_mid_ref, gain_two_ref,
    input_ref, small_ref,
    w, sem,
):
    i = pl.program_id(0)

    @pl.when(i == 0)
    def _():
        fetch_pieces(tab, (g_a, g_b, g_c, g_d), 144, w, sem)
        small_ref[8:9, :] = jnp.zeros((1, WIDTH), F32)
        small_ref[9:10, :] = gain_two_ref[...]
        small_ref[10:16, :] = jnp.zeros((6, WIDTH), F32)
        finish(w, sem)

    y = jnp.zeros((256, WIDTH), F32)
    for half in (0, 1):
        cols = slice(half * 3 * LANES, (half + 1) * 3 * LANES)
        y = y + dot_last(grad_qkv_ref[:, cols], qkv_columns(w, half))
    xhat, scale = ln_stats(add_embed(x_ref[...], te_ref, i))
    grad = grad_mid_ref[...] + ln_back(y, vec_ref[0:1, :], xhat, scale)
    input_ref[...] = grad.astype(BF16)
    for s in range(2):
        small_ref[pl.ds(i * 2 + s, 1), :] = jnp.sum(
            grad[128 * s : 128 * s + 128], axis=0, keepdims=True
        )
    small_ref[8:9, :] += jnp.sum(y * xhat, axis=0, keepdims=True)


def input_backward(tab, pieces, grad_qkv, rows, embed, vectors, grad_mid, gain_two):
    row = tiles(256, WIDTH)
    return kernel_call(
        input_backward_kernel,
        grid=(4,),
        out_shape=(shaped((1024, WIDTH)), local((16, WIDTH), F32)),
        in_specs=[SMEM_SPEC]
        + [ANY_SPEC] * 4
        + [tiles(256, 3 * WIDTH), row, fixed(8, WIDTH), fixed(16, WIDTH), row, VMEM_SPEC],
        out_specs=(row, VMEM_SPEC),
        scratch_shapes=[pltpu.VMEM((CHIPS, 2, 144, LANES), BF16), pltpu.SemaphoreType.DMA],
        compiler_params=params(20),
        cost_estimate=cost(4_000_000_000, 18_000_000),
        name="input_backward",
    )(tab, *pieces, grad_qkv, rows, embed, vectors, grad_mid, gain_two)


def finish_kernel(
    tab, e_mine, e_theirs, wave_ref, hot_ref, hidden_ref, slope_ref, time_out_ref,
    down_ref, down_other, up_ref, up_other, qkv_ref, qkv_other,
    tin_out, tout_out, one_out, two_out, data_out, down_out, up_out, out_out, qkv_out,
    every, sem,
):
    each_piece(
        tab,
        [e.at[pl.ds(first, 8)] for e in (e_mine, e_theirs) for first in (0, 8)],
        lambda src, chip, half: pltpu.make_async_copy(
            src, every.at[half * CHIPS + chip], sem
        ).start(),
    )
    core = first_core(tab)
    for half, down, up, qkv in (
        (core, down_ref, up_ref, qkv_ref), (1 - core, down_other, up_other, qkv_other)
    ):
        down_out[:, lanes_of(half, LANES)] = down[pl.ds(pl.multiple_of(96 * core, 8), 96), :]
        for b in range(4):
            up_out[:, lanes_of(half, 4 * LANES, b * LANES)] = up[pl.ds(pl.multiple_of(48 * b + 24 * core, 8), 24), :]
        out_out[:, lanes_of(half, LANES)] = up[pl.ds(pl.multiple_of(192 + 24 * core, 8), 24), :]
        for sec in range(3):
            qkv_out[:, lanes_of(half, LANES, sec * WIDTH)] = qkv[pl.ds(pl.multiple_of(48 * sec + 24 * core, 8), 24), :]
    finish(every, sem)
    grads = every[...].reshape(-1, WIDTH)
    tout_out[...] = dot_first(hidden_ref[...], grads)
    grad_pre = dot_last(grads, time_out_ref[...]) * slope_ref[...]
    tin_out[...] = dot_first(grad_pre.astype(BF16), wave_ref[...])
    first = tab[68] * 24
    lane = lax.broadcasted_iota(jnp.int32, (WIDTH, 128), 0)
    place = lax.broadcasted_iota(jnp.int32, (WIDTH, 128), 1)
    own = dot(grads, ((lane == place + first) & (place < 24)).astype(BF16)).astype(BF16)
    sums = dot(hot_ref[...], own)
    data_out[...] = sums[0:2, 0:24]
    one_out[...] = sums[2:3, 0:24]
    two_out[...] = sums[3:4, 0:24]


def finish_grads(tab, parts, wave, hot, hidden, slope, time_out, pieces):
    rows, width = time_out.shape
    return kernel_call(
        finish_kernel,
        out_shape=(
            shaped((rows, wave.shape[1]), F32),
            shaped((rows, width), F32),
            shaped((1, 24), F32),
            shaped((1, 24), F32),
            shaped((2, 24), F32),
            shaped((96, WIDTH), F32),
            shaped((24, FF), F32),
            shaped((24, WIDTH), F32),
            shaped((24, 3 * WIDTH), F32),
        ),
        in_specs=[SMEM_SPEC] + [ANY_SPEC] * 2 + [VMEM_SPEC] * 11,
        out_specs=(VMEM_SPEC,) * 9,
        scratch_shapes=[pltpu.VMEM((2 * CHIPS, 16, width), BF16), pltpu.SemaphoreType.DMA],
        compiler_params=params(16),
        cost_estimate=cost(50_000_000, 4_000_000),
        name="finish_grads",
    )(tab, *parts, wave, hot, hidden, slope, time_out, *pieces)


def pick(stacked, index):
    return lax.dynamic_index_in_dim(stacked, index, 0, keepdims=False)


def in_core_order(core, own, other, axis):
    return jnp.where(
        core == 0,
        jnp.concatenate([own, other], axis=axis),
        jnp.concatenate([other, own], axis=axis),
    )


def position_table(chip, core, order):
    index = jnp.arange(72, dtype=jnp.int32)
    side = jnp.bitwise_xor(core, (index // CHIPS) % 2)
    inner = index % CHIPS
    distance = jnp.bitwise_xor(inner, chip)
    there = jnp.zeros_like(index)
    back = jnp.zeros_like(index)
    for bit in range(4):
        mask = jnp.where(side == 0, order[0][bit], order[1][bit])
        there = there + jnp.where((inner >> bit) & 1 == 1, mask, 0)
        back = back + jnp.where(jnp.bitwise_and(distance, mask) != 0, 1 << bit, 0)
    moved = jnp.where(index < 32, jnp.bitwise_xor(there, chip), back)
    return jnp.where(index < 64, moved, jnp.where(index < 68, core, 2 * chip + core))


def lane_blocks(x, starts, step):
    return [
        jnp.concatenate([x[:, k + h * step : k + h * step + LANES] for k in starts], axis=0)
        for h in (0, 1)
    ]


def swap_halves(halves, core):
    own = jnp.where(core == 0, halves[0], halves[1])
    return own, core_swap(jnp.where(core == 0, halves[1], halves[0]))


def join_rows(own, other, core, blocks):
    shape = (blocks, own.shape[0] // blocks, LANES)
    return in_core_order(core, own.reshape(shape), other.reshape(shape), 1).reshape(-1, LANES)


def pack_extra(time_in, vectors, ints):
    rows = time_in.shape[0]
    filler = jnp.zeros((rows, 128), BF16)
    vec = lax.dynamic_update_slice(filler, vectors, (0, 0))
    num = lax.dynamic_update_slice(filler, ints[None, :], (0, 0))
    return jnp.concatenate([time_in, vec, num], axis=1)


def split_time(timestep, dataset):
    steps = timestep.reshape(-1)
    return jnp.concatenate([steps // 64, steps % 64, dataset.reshape(-1)]).astype(BF16)


def gather_all(x):
    return lax.all_gather(x, AXES, axis=0, tiled=True)


def shards(
    block_input,
    out_grad,
    timestep,
    dataset,
    lengths,
    norm1_gain,
    qkv_weight,
    out_weight,
    norm2_gain,
    up_weight,
    down_weight,
    time_in,
    time_out,
    data_embed,
    devices,
):
    flat = lax.axis_index(AXES)
    exchange = devices == 2 * CHIPS
    vectors = jnp.concatenate([norm1_gain[None], norm2_gain[None], data_embed.T], axis=0)
    numbers = split_time(timestep, dataset)
    count = numbers.shape[0] // 3
    micros, seqs, seq_len, width = block_input.shape
    tokens = micros * seqs * seq_len
    x_rows = block_input.reshape(tokens, width)
    grad_rows = out_grad.reshape(tokens, width)
    features = sinusoid(timestep.reshape(-1), time_in.shape[1] // 2).astype(BF16)
    if exchange:
        core = flat & 1
        chip = flat >> 1

        wide = lane_blocks(qkv_weight, (0, WIDTH, 2 * WIDTH), LANES)
        slim = lane_blocks(time_out, (0,), LANES)
        own, other = swap_halves(
            [jnp.concatenate([x, y], axis=0) for x, y in zip(wide, slim)], core
        )
        attention_piece = jnp.concatenate(
            [
                join_rows(own[:72], other[:72], core, 3),
                join_rows(own[72:], other[72:], core, 1),
                pack_extra(time_in, vectors, numbers),
            ],
            axis=0,
        )[None]
        near = [chip_swap(attention_piece, p) for p in (1, 2, 3)]
        up_weight, out_weight, down_weight, flat = lax.optimization_barrier(
            (up_weight, out_weight, down_weight, flat, attention_piece)
        )[:4]
        tab = position_table(flat >> 1, flat & 1, LINE_FIRST)
        later_tab = position_table(flat >> 1, flat & 1, LINE_LATER)
        wide = lane_blocks(up_weight, range(0, 4 * LANES, LANES), 4 * LANES)
        slim = lane_blocks(out_weight, (0,), LANES)
        own, other = swap_halves(
            [jnp.concatenate([x, y], axis=0) for x, y in zip(wide, slim)], core
        )
        up_piece = jnp.concatenate(
            [join_rows(own[:96], other[:96], core, 4), join_rows(own[96:], other[96:], core, 1)],
            axis=0,
        )[None]
        own, other = swap_halves(lane_blocks(down_weight, (0,), LANES), core)
        down_piece = join_rows(own, other, core, 1)[None]
        down_pair = jnp.concatenate([down_piece, chip_swap(down_piece, 1, LINE_LATER)], axis=0)
        ready = (up_piece, down_pair, tab, later_tab, features)
        line = after(jnp.concatenate([attention_piece] + near, axis=0), *ready)
        plane = chip_swap(line, 4)
        up_near = [chip_swap(after(up_piece, line), p) for p in (1, 2)]
        plane, up_near = together(plane, up_near)
        held = jnp.concatenate([line, plane], axis=0)
        far = chip_swap(held, 8)
        up_near.append(chip_swap(after(up_piece, plane), 3))
        up_line = lax.optimization_barrier(jnp.concatenate([up_piece] + up_near, axis=0))
        up_plane = chip_swap(up_line, 4)
        down_near = [chip_swap(after(down_pair, up_line), p, LINE_LATER) for p in (2, 4)]
        (far, up_plane), down_near = together((far, up_plane), down_near)
        attention_pieces = (held, far, core_swap(held), core_swap(far))
        up_held = jnp.concatenate([up_line, up_plane], axis=0)
        up_far = chip_swap(up_held, 8)
        down_last = chip_swap(after(down_pair, up_held), 6, LINE_LATER)
    else:
        tab = jnp.concatenate(
            [jnp.tile(jnp.arange(CHIPS, dtype=jnp.int32), 4), jnp.zeros((8,), jnp.int32)]
        )
        later_tab = tab
        full_qkv = gather_all(qkv_weight).reshape(CHIPS, 48, 3, 2, LANES)
        full_out = gather_all(out_weight).reshape(CHIPS, 48, 2, LANES)
        full_up = gather_all(up_weight).reshape(CHIPS, 48, 2, 4, LANES)
        full_down = gather_all(down_weight).reshape(CHIPS, 192, 2, LANES)
        full_tin = gather_all(time_in).reshape(CHIPS, 2, 16, 128)
        full_tout = gather_all(time_out).reshape(CHIPS, 32, 2, LANES)
        full_vec = lax.all_gather(vectors, AXES, axis=1, tiled=True).reshape(4, CHIPS, 2, 24)
        numbers_all = gather_all(numbers[None])
        extra = jnp.zeros((CHIPS, 2, 16, LANES), BF16)
        extra = extra.at[:, :, :, :128].set(full_tin)
        extra = extra.at[:, :, 0:4, 128:152].set(full_vec.transpose(1, 2, 0, 3))
        attention_pieces = []
        down_pieces = []
        up_pieces = []
        for half in (0, 1):
            wide = full_qkv[:, :, :, half].transpose(0, 2, 1, 3).reshape(CHIPS, 144, LANES)
            whole = jnp.concatenate([wide, full_tout[:, :, half], extra[:, half]], axis=1)
            attention_pieces += [whole[:8], whole[8:]]
            down_pieces += [full_down[:8, :, half], full_down[8:, :, half]]
            wide = full_up[:, :, half].transpose(0, 2, 1, 3).reshape(CHIPS, 192, LANES)
            whole = jnp.concatenate([wide, full_out[:, :, half]], axis=1)
            up_pieces += [whole[:8], whole[8:]]

    arrivals = []
    if exchange:
        x_rows = after(x_rows, up_held)
        arrivals = [up_far]
    forward = attention_forward(tab, lengths, dataset, attention_pieces, x_rows, features)
    (normed, qkv, embed, vecs, seen, probs, att), arrivals = together(forward, arrivals)
    seen = seen[:, :, 0, : 3 * count].reshape(2 * CHIPS, 3 * count) if exchange else numbers_all
    steps = seen[:, :count] * 64 + seen[:, count : 2 * count].astype(F32)
    wave = sinusoid(steps.reshape(-1), time_in.shape[1] // 2).astype(BF16)
    wave = jnp.pad(wave.reshape(devices, count, -1), ((0, 0), (0, 16 - count), (0, 0)))
    wave = wave.reshape(devices * 16, -1)
    which = jnp.pad(seen[:, 2 * count :], ((0, 0), (0, 16 - count))).reshape(-1)
    place = jnp.tile(jnp.arange(16), devices)
    hot = jnp.stack(
        [(place < count) & (which == 0), (place < count) & (which == 1), place == 8, place == 9]
    )
    hot = jnp.pad(hot.astype(BF16), ((0, 12), (0, 0)))
    pre = dot_last(wave, time_in)
    gate = 1.0 / (1.0 + jnp.exp(-pre))
    hidden = (pre * gate).astype(BF16)
    slope_pre = gate * (1.0 + pre * (1.0 - gate))
    if exchange:
        (up_far,) = arrivals
        down_near = [after(x, embed) for x in [down_pair] + down_near + [down_last]]
        up_pieces = (up_held, up_far, core_swap(up_held), core_swap(up_far))
        down_held = jnp.concatenate(down_near, axis=0)
        att, wave, hot, hidden, slope_pre, down_held = lax.optimization_barrier(
            (att, wave, hot, hidden, slope_pre, down_held)
        )
        arrivals = chip_swap(down_held, 8, LINE_LATER)
    forward = up_forward(tab, up_pieces, att, x_rows, grad_rows, embed, vecs)
    (mid, two, act, slope, down_theirs), arrivals = together(forward, arrivals)
    if exchange:
        down_far = arrivals
        down_sum = Scatter(down_theirs)
        arrivals = [core_swap(down_held), core_swap(down_far)], down_sum.swap()
    (down_mine, act, slope), arrivals = together(down_grad(tab, act, grad_rows, slope), arrivals)
    if exchange:
        down_pieces = (down_held, down_far, *arrivals[0])
        down_sum.land(arrivals[1], down_mine)
        slope = after(slope, *down_sum.send())
        arrivals = down_sum.fly()
    backward = mlp_backward(
        tab, later_tab, up_pieces, down_pieces, two, att, slope, grad_rows, mid, vecs
    )
    backward, arrivals = together(backward, arrivals)
    grad_mid, branch, grad_up, grad_att, gain_two, up_theirs = backward
    if exchange:
        down_sum.land(arrivals)
        up_sum = Scatter(up_theirs)
        grad_up = after(grad_up, *down_sum.send())
        arrivals = down_sum.fly(), up_sum.swap()
    up_mine, arrivals = together(up_grad(tab, att, branch, two, grad_up), arrivals)
    if exchange:
        down_sum.land(arrivals[0])
        up_sum.land(arrivals[1], up_mine)
        grad_att = after(grad_att, *up_sum.send(), *down_sum.send())
        arrivals = up_sum.fly(), down_sum.fly()
    backward = attention_backward(tab, normed, qkv, probs, grad_att)
    (grad_qkv, mine_qkv, att_theirs), arrivals = together(backward, arrivals)
    if exchange:
        up_sum.land(arrivals[0])
        down_sum.land(arrivals[1])
        down_total = down_sum.total()
        att_sum = Scatter(att_theirs)
        mine_qkv = after(mine_qkv, *up_sum.send(), down_total)
        arrivals = up_sum.fly(), att_sum.swap()
    backward = qkv_grad(tab, later_tab, down_pieces, normed, mine_qkv, act, mid)
    (att_mine, result), arrivals = together(backward, arrivals)
    if exchange:
        up_sum.land(arrivals[0])
        att_sum.land(arrivals[1], att_mine)
        grad_qkv = after(grad_qkv, *att_sum.send(), *up_sum.send())
        *up_near, up_last = up_sum.fly()
        arrivals = att_sum.fly(), up_near
    backward = input_backward(
        tab, attention_pieces, grad_qkv, x_rows, embed, vecs, grad_mid, gain_two
    )
    (grad_input, small), arrivals = together(backward, arrivals)

    small = small.astype(BF16)[None]
    if exchange:
        att_sum.land(arrivals[0])
        up_sum.land(arrivals[1])
        att_sum.send()
        near = [chip_swap(small, p) for p in (1, 2, 3)]
        brought, near = together(att_sum.fly(), near)
        att_sum.land(brought)
        small_line = jnp.concatenate([small] + near, axis=0)
        att_sum.send()
        brought = att_sum.fly()
        small_line, brought[1] = lax.optimization_barrier((small_line, brought[1]))
        plane = [small_line] + [chip_swap(small_line, p) for p in (4, 8, 12)]
        every = jnp.concatenate(plane, axis=0)
        every = every, core_swap(every)
        brought, up_last = together(brought, up_last)
        att_sum.land(brought)
        up_sum.land([up_last])
        sums = after(down_total, small_line), after(up_sum.total(), small_line), att_sum.total()
        pieces = [x for total in sums for x in (total, core_swap(total))]
        finished = finish_grads(
            tab, every, wave, hot, hidden, slope_pre, time_out, pieces
        )
        grad_tin, grad_tout, gain_one, gain_two, grad_data, *weights = finished
        grad_down, grad_up_weight, grad_out, grad_qkv_weight = weights
    else:
        every = gather_all(small).reshape(devices * 16, width)
        grad_tout = dot_first(hidden, every)
        grad_pre = dot_last(every, time_out) * slope_pre
        grad_tin = dot_first(grad_pre.astype(BF16), wave)
        own_cols = norm1_gain.shape[0]
        sums = lax.dynamic_slice_in_dim(dot(hot, every), flat * own_cols, own_cols, 1)
        grad_data, gain_one, gain_two = sums[0:2], sums[2], sums[3]
        scatter = partial(lax.psum_scatter, axis_name=AXES, scatter_dimension=0, tiled=True)
        both = jnp.stack([down_mine, down_theirs]).astype(F32)
        grad_down = scatter(both.transpose(1, 2, 0, 3).reshape(FF, WIDTH))
        both = jnp.stack([up_mine, up_theirs]).astype(F32)
        grad_out = scatter(both[:, :, 192:].transpose(1, 2, 0, 3).reshape(WIDTH, WIDTH))
        both = both[:, :, :192].reshape(2, CHIPS, 4, 48, LANES)
        grad_up_weight = scatter(both.transpose(1, 3, 0, 2, 4).reshape(WIDTH, FF))
        both = jnp.stack([att_mine, att_theirs]).astype(F32).reshape(2, CHIPS, 3, 48, LANES)
        grad_qkv_weight = scatter(both.transpose(1, 3, 2, 0, 4).reshape(WIDTH, 3 * WIDTH))

    return (
        result.reshape(block_input.shape),
        grad_input.reshape(block_input.shape),
        gain_one.reshape(-1),
        grad_qkv_weight,
        grad_out,
        gain_two.reshape(-1),
        grad_up_weight,
        grad_down,
        grad_tin,
        grad_tout,
        grad_data.T,
    )


def solution(mesh):
    devices = mesh.shape["dp"] * mesh.shape["fsdp"]
    seq_spec = P(None, AXES, None, None)
    int_spec = P(None, AXES)
    row_spec = P(AXES, None)
    in_specs = (seq_spec, seq_spec, int_spec, int_spec, int_spec, P(AXES), row_spec, row_spec, P(AXES))
    in_specs = in_specs + (row_spec,) * 5
    out_specs = (seq_spec, seq_spec, P(AXES), row_spec, row_spec, P(AXES)) + (row_spec,) * 5
    return jax.shard_map(
        partial(shards, devices=devices),
        mesh=mesh,
        in_specs=in_specs,
        out_specs=out_specs,
        check_vma=False,
    )
```

```python
from functools import partial
import math

import jax
import jax.numpy as jnp
from jax import lax
from jax.experimental import pallas as pl
from jax.experimental.pallas import tpu as pltpu
from jax.sharding import PartitionSpec as P

HEAD_DIM = 64
AXES = ("dp", "fsdp")
LANES = 384
CHIPS = 16
WIDTH = 768
FF = 3072
F32 = jnp.float32
BF16 = jnp.bfloat16
NEG = -1000000000.0


def sinusoid(timestep, half_width):
    frequency = jnp.exp(-math.log(10000.0) * jnp.arange(half_width, dtype=F32) / half_width)
    angles = timestep.astype(F32)[:, None] * frequency[None, :]
    return jnp.concatenate([jnp.cos(angles), jnp.sin(angles)], axis=-1)


def dot(left, right):
    return jnp.dot(left, right, preferred_element_type=F32)


def dot_last(left, right):
    return lax.dot_general(left, right, (((1,), (1,)), ((), ())), preferred_element_type=F32)


def dot_first(left, right):
    return lax.dot_general(left, right, (((0,), (0,)), ((), ())), preferred_element_type=F32)


def positions(masks):
    return [sum(masks[b] for b in range(4) if (p >> b) & 1) for p in range(CHIPS)]


LINE_FIRST = ((2, 1, 8, 4), (2, 1, 4, 8))
LINE_LATER = ((8, 2, 1, 4), (4, 2, 1, 8))


def core_swap(x):
    return lax.ppermute(x, AXES, [(i, i ^ 1) for i in range(2 * CHIPS)])


def chip_swap(x, position, order=LINE_FIRST):
    far = [positions(masks)[position] * 2 for masks in order]
    return lax.ppermute(x, AXES, [(i, i ^ far[i & 1]) for i in range(2 * CHIPS)])


def after(x, *others):
    return lax.optimization_barrier((x,) + others)[0]


def gather_line(piece):
    return jnp.concatenate([piece] + [chip_swap(piece, p) for p in (1, 2, 3)], axis=0)


def gather_plane(held):
    return jnp.concatenate([held, chip_swap(held, 4)], axis=0)


def together(outs, arrivals):
    return lax.optimization_barrier((outs, arrivals))


class Scatter:
    def __init__(self, theirs):
        self.parts = []
        self.steps = [(8,), (4,), (1, 2, 3)]
        self.theirs = theirs

    def swap(self):
        return [core_swap(self.theirs)]

    def land(self, brought, *own):
        self.parts += [*brought, *own]

    def sum(self, start, stop):
        total = self.parts[0][start:stop].astype(F32)
        for part in self.parts[1:]:
            total = total + part[start:stop].astype(F32)
        return total

    def send(self):
        self.at = self.steps.pop(0)
        size = 1 if len(self.at) == 3 else self.at[0]
        self.sent = [self.sum(p, p + size).astype(BF16) for p in self.at]
        self.parts = [self.sum(0, size)]
        return [*self.sent, self.parts[0]]

    def fly(self):
        return [chip_swap(x, p) for x, p in zip(self.sent, self.at)]

    def total(self):
        return self.sum(0, 1)[0]


VMEM_SPEC = pl.BlockSpec(memory_space=pltpu.VMEM)
SMEM_SPEC = pl.BlockSpec(memory_space=pltpu.SMEM)
ANY_SPEC = pl.BlockSpec(memory_space=pl.ANY)


def tiles(rows, cols):
    return pl.BlockSpec((rows, cols), lambda i: (i, 0))


def columns(rows, cols):
    return pl.BlockSpec((rows, cols), lambda i: (0, i))


def fixed(*shape):
    return pl.BlockSpec(shape, lambda i: (0,) * len(shape))


def shaped(shape, dtype=BF16):
    return pltpu.HBM(shape, dtype)


def local(shape, dtype=BF16):
    return pltpu.VMEM(shape, dtype)


def params(mib):
    return pltpu.CompilerParams(vmem_limit_bytes=mib * 1024 * 1024)


def kernel_call(kernel, **kwargs):
    call = pl.pallas_call(kernel, **kwargs)
    if "grid_spec" in kwargs:
        grid_spec = kwargs["grid_spec"]
        specs = [SMEM_SPEC] * grid_spec.num_scalar_prefetch + list(grid_spec.in_specs)
    else:
        specs = kwargs["in_specs"]

    def place(x, spec):
        if spec is SMEM_SPEC:
            return x
        space = pltpu.VMEM if spec is VMEM_SPEC else pltpu.HBM
        return pltpu.with_memory_space_constraint(x, space)

    def run(*operands):
        return call(*[place(x, spec) for x, spec in zip(operands, specs, strict=True)])

    return run


def cost(flops, nbytes, transcendentals=0):
    return pl.CostEstimate(flops=flops, bytes_accessed=nbytes, transcendentals=transcendentals)


def ln_stats(v):
    center = v - jnp.mean(v, axis=-1, keepdims=True)
    scale = lax.rsqrt(jnp.mean(center * center, axis=-1, keepdims=True) + 1e-05)
    return center * scale, scale


def ln_back(y, gain, xhat, scale):
    yg = y * gain
    return scale * (
        yg - jnp.mean(yg, axis=-1, keepdims=True) - xhat * jnp.mean(yg * xhat, axis=-1, keepdims=True)
    )


def first_core(tab):
    return tab[64]


def each_piece(tab, parts, fn):
    core = first_core(tab)
    for side in (0, 1):
        half = core if side == 0 else 1 - core
        for group in (0, 1):
            part = parts[side * 2 + group]

            def body(q, _, part=part, side=side, group=group, half=half):
                chip = tab[side * CHIPS + group * 8 + q]
                fn(part.at[q], chip, half)
                return 0

            lax.fori_loop(0, 8, body, 0)


def rows_of(chip, size):
    return pl.ds(pl.multiple_of(chip * size, size), size)


def lanes_of(half, size, base=0):
    return pl.ds(pl.multiple_of(half * size + base, 128), LANES)


def fetch_pieces(tab, parts, rows, dst, sem, first=0):
    each_piece(
        tab,
        parts,
        lambda src, chip, half: pltpu.make_async_copy(
            src.at[pl.ds(first, rows), :], dst.at[chip, half], sem
        ).start(),
    )


def block(pieces, half, first, rows=48):
    return pieces[:, half, first : first + rows, :].reshape(CHIPS * rows, LANES)


def both_halves(pieces, first, rows=48):
    return jnp.concatenate([block(pieces, h, first, rows) for h in (0, 1)], axis=1)


def down_rows(pieces, j):
    chips = pl.ds(4 * j, 4)
    return jnp.concatenate([pieces[chips, h].reshape(WIDTH, LANES) for h in (0, 1)], axis=1)


def qkv_columns(pieces, half):
    return jnp.concatenate([block(pieces, half, 48 * sec) for sec in range(3)], axis=1)


def finish(ref, sem):
    pltpu.make_async_copy(ref, ref, sem).wait()


def add_embed(x, embed, i):
    seqs = x.shape[0] // 128
    parts = [
        x[128 * k : 128 * k + 128].astype(F32) + embed[pl.ds(i * seqs + k, 1), :]
        for k in range(seqs)
    ]
    return jnp.concatenate(parts, axis=0)


def two_heads(x, low_half):
    none = jnp.zeros_like(x)
    return jnp.concatenate([jnp.where(low_half, x, none), jnp.where(low_half, none, x)], axis=0)


def side_by_side(x):
    return jnp.concatenate([x[:128], x[128:]], axis=1)


def pair_base(pair):
    return (pair // 3) * 3 * LANES + (pair % 3) * 128


def attention_tile(lengths, qkv_ref, probs_ref, att_ref):
    low_half = lax.broadcasted_iota(jnp.int32, (128, 128), 1) < HEAD_DIM
    lane = lax.broadcasted_iota(jnp.int32, (256, 128), 1)
    keep = [lane < length for length in lengths]
    units = [(k, pair) for k in range(2) for pair in range(6)]

    def part(k, pair, section):
        base = pair_base(pair) + section * LANES
        return qkv_ref[128 * k : 128 * k + 128, base : base + 128]

    scores = []
    for k, pair in units:
        query = two_heads(part(k, pair, 0), low_half)
        score = dot_last(query, part(k, pair, 1)) * HEAD_DIM ** (-0.5)
        scores.append(jnp.where(keep[k], score, NEG))
    probs = []
    for (k, pair), score in zip(units, scores):
        shifted = jnp.exp(score - jnp.max(score, axis=-1, keepdims=True))
        total = jnp.sum(shifted, axis=-1, keepdims=True)
        probs.append((shifted * (1.0 / total)).astype(BF16))
        first = 256 * (6 * k + pair)
        probs_ref[first : first + 256, :] = probs[-1]
    for (k, pair), prob in zip(units, probs):
        value = two_heads(part(k, pair, 2), low_half)
        att_ref[128 * k : 128 * k + 128, pair * 128 : pair * 128 + 128] = dot(
            side_by_side(prob), value
        ).astype(BF16)


def attention_kernel(
    tab, lens, sets, g_a, g_b, g_c, g_d, x_ref, feat_ref,
    normed_ref, qkv_ref, te_ref, vec_ref, seen_ref, probs_ref, att_ref,
    w, w_time, sem, sem_time,
):
    i = pl.program_id(0)

    @pl.when(i == 0)
    def _():
        fetch_pieces(tab, (g_a, g_b, g_c, g_d), 48, w_time, sem_time, 144)
        fetch_pieces(tab, (g_a, g_b, g_c, g_d), 144, w, sem)
        finish(w_time, sem_time)
        lane = lax.broadcasted_iota(jnp.int32, (128, WIDTH), 1)
        spread = (lax.broadcasted_iota(jnp.int32, (128, WIDTH), 0) == lane % 24).astype(BF16)
        vectors = jnp.zeros((16, WIDTH), F32)
        embed = jnp.zeros((8, WIDTH), F32)
        for owner in (0, 1):
            extra = block(w_time, owner, 32, 16)
            wide = dot(extra[:, 128:256], spread)
            chip = lax.broadcasted_iota(jnp.int32, (256, WIDTH), 0) // 16
            place = lax.broadcasted_iota(jnp.int32, (256, WIDTH), 1) // 24
            wide = jnp.where(place == chip * 2 + owner, wide, 0.0)
            vectors = vectors + jnp.sum(wide.reshape(CHIPS, 16, WIDTH), axis=0)
            pre = dot_last(feat_ref[...], extra[:, 0:128])
            hidden = (pre / (1.0 + jnp.exp(-pre))).astype(BF16)
            embed = embed + dot(hidden, both_halves(w_time, 16 * owner, 16))
            seen_ref[owner] = w_time[:, owner, 32:48, 256:]
        vec_ref[...] = vectors
        for s in range(8):
            chosen = jnp.where(sets[s // 4, s % 4] == 1, vectors[3:4, :], vectors[2:3, :])
            te_ref[s : s + 1, :] = embed[s : s + 1, :] + chosen

    xhat, _unused = ln_stats(add_embed(x_ref[...], te_ref, i))
    normed_ref[...] = (xhat * vec_ref[0:1, :]).astype(BF16)

    @pl.when(i == 0)
    def _():
        finish(w, sem)

    for half in (0, 1):
        cols = slice(half * 3 * LANES, (half + 1) * 3 * LANES)
        qkv_ref[:, cols] = dot(normed_ref[...], qkv_columns(w, half)).astype(BF16)
    lengths = [lens[i // 2, i % 2 * 2 + k] for k in range(2)]
    attention_tile(lengths, qkv_ref, probs_ref, att_ref)


def attention_forward(tab, lens, sets, pieces, rows, features):
    row = tiles(256, WIDTH)
    return kernel_call(
        attention_kernel,
        grid=(4,),
        out_shape=(
            shaped((1024, WIDTH)),
            shaped((1024, 3 * WIDTH)),
            shaped((8, WIDTH), F32),
            shaped((16, WIDTH), F32),
            shaped((2, CHIPS, 16, 128)),
            shaped((48 * 256, 128)),
            shaped((1024, WIDTH)),
        ),
        in_specs=[SMEM_SPEC] * 3 + [ANY_SPEC] * 4 + [row, fixed(8, 128)],
        out_specs=(
            row, tiles(256, 3 * WIDTH), fixed(8, WIDTH), fixed(16, WIDTH),
            fixed(2, CHIPS, 16, 128), tiles(12 * 256, 128), row,
        ),
        scratch_shapes=[
            pltpu.VMEM((CHIPS, 2, 144, LANES), BF16),
            pltpu.VMEM((CHIPS, 2, 48, LANES), BF16),
            pltpu.SemaphoreType.DMA,
            pltpu.SemaphoreType.DMA,
        ],
        compiler_params=params(26),
        cost_estimate=cost(8_000_000_000, 20_000_000, 1_600_000),
        name="attention_forward",
    )(tab, lens, sets, *pieces, rows, features)


def gelu_parts(u):
    cdf = 0.5 + 0.5 * lax.erf(u * math.sqrt(0.5))
    return cdf, jnp.exp(u * u * -0.5) * (1.0 / math.sqrt(2.0 * math.pi))


def up_columns(pieces, half, j):
    return jnp.concatenate(
        [block(pieces, half, 96 * j), block(pieces, half, 96 * j + 48)], axis=1
    )


def half_of(tab, side):
    return first_core(tab) if side == 0 else 1 - first_core(tab)


def clamped(rows, cols):
    return pl.BlockSpec((rows, cols), lambda i: (jnp.minimum(i, 3), 0))


def down_grad_rows(tab, side, j, act, out_grad, out_ref):
    lanes = lanes_of(half_of(tab, side), LANES)
    grad = dot_first(act, out_grad[:, lanes]).astype(BF16)
    for k in range(4):
        place = tab[32 + side * CHIPS + j * 4 + k]
        out_ref[place, :, :] = grad[192 * k : 192 * k + 192, :]


def up_kernel(
    tab, u_a, u_b, u_c, u_d, out_grad_ref, att_ref, x_ref, te_ref, vec_ref,
    mid_ref, two_ref, act_ref, slope_ref, theirs_ref,
    w, w_out, sem, sem_out,
):
    i = pl.program_id(0)
    parts = (u_a, u_b, u_c, u_d)

    def token_rows(arrived):
        rows = rows_of(i, 256)
        mid = add_embed(x_ref[...], te_ref, i) + dot(att_ref[...], both_halves(w_out, 0))
        mid_ref[...] = mid
        xhat, _unused = ln_stats(mid)
        two = (xhat * vec_ref[1:2, :]).astype(BF16)
        two_ref[...] = two
        arrived()
        for j in range(4):
            up = dot(two, up_columns(w, j // 2, j % 2))
            cdf, density = gelu_parts(up)
            act_ref[j, rows, :] = (up * cdf).astype(BF16)
            slope_ref[j, rows, :] = (cdf + up * density).astype(BF16)

    @pl.when(i == 0)
    def _():
        fetch_pieces(tab, parts, 48, w_out, sem_out, 192)
        fetch_pieces(tab, parts, 192, w, sem)
        finish(w_out, sem_out)
        token_rows(lambda: finish(w, sem))

    @pl.when((i > 0) & (i < 4))
    def _():
        token_rows(lambda: None)

    @pl.when(i >= 4)
    def _():
        down_grad_rows(tab, 1, i - 4, act_ref[i - 4], out_grad_ref, theirs_ref)


def up_forward(tab, pieces, att, rows, out_grad, embed, vectors):
    row = clamped(256, WIDTH)
    return kernel_call(
        up_kernel,
        grid=(8,),
        out_shape=(
            shaped((1024, WIDTH), F32),
            shaped((1024, WIDTH)),
            local((4, 1024, WIDTH)),
            local((4, 1024, WIDTH)),
            local((CHIPS, 192, LANES)),
        ),
        in_specs=[SMEM_SPEC]
        + [ANY_SPEC] * 4
        + [VMEM_SPEC, row, row, fixed(8, WIDTH), fixed(16, WIDTH)],
        out_specs=(row, row) + (VMEM_SPEC,) * 3,
        scratch_shapes=[
            pltpu.VMEM((CHIPS, 2, 192, LANES), BF16),
            pltpu.VMEM((CHIPS, 2, 48, LANES), BF16),
            pltpu.SemaphoreType.DMA,
            pltpu.SemaphoreType.DMA,
        ],
        compiler_params=params(26),
        cost_estimate=cost(10_000_000_000, 30_000_000, 6_000_000),
        name="up_forward",
    )(tab, *pieces, out_grad, att, rows, embed, vectors)


def down_grad_kernel(tab, act_ref, out_grad_ref, _slope, out_ref, act_hbm, _slope_out, sem):
    j = pl.program_id(0)

    @pl.when(j == 0)
    def _():
        pltpu.make_async_copy(act_ref, act_hbm, sem).start()

    down_grad_rows(tab, 0, j, act_ref[j], out_grad_ref, out_ref)

    @pl.when(j == 3)
    def _():
        pltpu.make_async_copy(act_ref, act_hbm, sem).wait()


def down_grad(tab, act, out_grad, slope):
    return kernel_call(
        down_grad_kernel,
        grid=(4,),
        out_shape=(
            local((CHIPS, 192, LANES)), shaped((4, 1024, WIDTH)), local((4, 1024, WIDTH))
        ),
        in_specs=[SMEM_SPEC] + [VMEM_SPEC] * 3,
        out_specs=(VMEM_SPEC, ANY_SPEC, VMEM_SPEC),
        input_output_aliases={3: 2},
        scratch_shapes=[pltpu.SemaphoreType.DMA],
        compiler_params=params(12),
        cost_estimate=cost(3_000_000_000, 10_000_000),
        name="down_grad",
    )(tab, act, out_grad, slope)


def store_blocks(tab, side, target, first, part, lanes):
    for chip in range(CHIPS):
        place = tab[32 + side * CHIPS + chip]
        target[place, pl.ds(first, 48), :] = part[48 * chip : 48 * chip + 48, lanes]


def out_grad_rows(tab, side, att, branch, out_ref, part):
    lanes = lanes_of(half_of(tab, side), LANES)
    part[:, 0:LANES] = dot_first(att[...], branch[:, lanes]).astype(BF16)
    store_blocks(tab, side, out_ref, 192, part, slice(0, LANES))


def up_grad_rows(tab, side, j, two, grad_up, out_ref, part):
    part[...] = dot_first(two, grad_up).astype(BF16)
    for b in range(2):
        first = pl.multiple_of((2 * j + b) * 48, 48)
        store_blocks(tab, side, out_ref, first, part, slice(b * LANES, (b + 1) * LANES))


def up_grad_kernel(
    tab, att_hbm, two_hbm, branch_ref, grad_up_ref, out_ref, att, two, part, sem_att, sem_two
):
    j = pl.program_id(0)

    @pl.when(j == 0)
    def _():
        pltpu.make_async_copy(att_hbm, att, sem_att).start()
        pltpu.make_async_copy(two_hbm, two, sem_two).start()
        finish(att, sem_att)
        out_grad_rows(tab, 0, att, branch_ref, out_ref, part)
        finish(two, sem_two)

    @pl.when(j > 0)
    def _():
        up_grad_rows(tab, 0, j - 1, two[...], grad_up_ref[j - 1], out_ref, part)


def up_grad(tab, att, branch, two, grad_up):
    return kernel_call(
        up_grad_kernel,
        grid=(3,),
        out_shape=local((CHIPS, 240, LANES)),
        in_specs=[SMEM_SPEC] + [ANY_SPEC] * 2 + [VMEM_SPEC] * 2,
        out_specs=VMEM_SPEC,
        scratch_shapes=[pltpu.VMEM((1024, WIDTH), BF16)] * 2
        + [pltpu.VMEM((WIDTH, WIDTH), BF16)]
        + [pltpu.SemaphoreType.DMA] * 2,
        compiler_params=params(16),
        cost_estimate=cost(3_200_000_000, 11_000_000),
        name="up_grad",
    )(tab, att, two, branch, grad_up)


def mlp_backward_kernel(
    tab, later_tab, u_a, u_b, u_c, u_d, d_a, d_b, d_c, d_d,
    two_hbm, att_hbm, slope_ref, out_grad_ref, mid_ref, vec_ref,
    grad_mid_ref, branch_ref, mine_up_ref, grad_att_ref, gain_ref, theirs_ref,
    w, w_down, two, att, theirs_up, part, sem, sem_down, sem_two, sem_att,
):
    i = pl.program_id(0)
    grad_up = [
        (half_of(tab, side), j, target)
        for side, target in enumerate((mine_up_ref, theirs_up))
        for j in range(2)
    ]

    @pl.when(i == 0)
    def _():
        fetch_pieces(later_tab, (d_a, d_b, d_c, d_d), 192, w_down, sem_down)
        gain_ref[...] = jnp.zeros_like(gain_ref)
        finish(w_down, sem_down)
        fetch_pieces(tab, (u_a, u_b, u_c, u_d), 240, w, sem)

    @pl.when(i < 4)
    def _():
        rows = rows_of(i, 256)
        for half, j, target in grad_up:
            grad_act = dot_last(out_grad_ref[rows, :], down_rows(w_down, 2 * half + j))
            slope = slope_ref[2 * half + j, rows, :].astype(F32)
            target[j, rows, :] = (grad_act * slope).astype(BF16)

    @pl.when(i == 4)
    def _():
        finish(w, sem)
        pltpu.make_async_copy(two_hbm, two, sem_two).start()
        pltpu.make_async_copy(att_hbm, att, sem_att).start()

    @pl.when((i >= 4) & (i < 8))
    def _():
        rows = rows_of(i - 4, 256)
        y = jnp.zeros((256, WIDTH), F32)
        for half, j, target in grad_up:
            y = y + dot_last(target[j, rows, :], up_columns(w, half, j))
        xhat, scale = ln_stats(mid_ref[...])
        grad = out_grad_ref[rows, :].astype(F32) + ln_back(y, vec_ref[1:2, :], xhat, scale)
        grad_mid_ref[...] = grad
        branch = grad.astype(BF16)
        branch_ref[rows, :] = branch
        gain_ref[...] += jnp.sum(y * xhat, axis=0, keepdims=True)
        grad_att_ref[rows, :] = dot_last(branch, both_halves(w, 192)).astype(BF16)

    @pl.when(i == 8)
    def _():
        finish(two, sem_two)
        finish(att, sem_att)
        out_grad_rows(tab, 1, att, branch_ref, theirs_ref, part)

    @pl.when(i >= 8)
    def _():
        up_grad_rows(tab, 1, i - 8, two[...], theirs_up[i - 8], theirs_ref, part)


def mlp_backward(
    tab, later_tab, up_pieces, down_pieces, two, att, slope, out_grad, mid, vectors
):
    row = pl.BlockSpec((256, WIDTH), lambda i: (jnp.clip(i - 4, 0, 3), 0))
    return kernel_call(
        mlp_backward_kernel,
        grid=(10,),
        out_shape=(
            shaped((1024, WIDTH), F32),
            local((1024, WIDTH)),
            local((2, 1024, WIDTH)),
            local((1024, WIDTH)),
            local((1, WIDTH), F32),
            local((CHIPS, 240, LANES)),
        ),
        in_specs=[SMEM_SPEC] * 2
        + [ANY_SPEC] * 10
        + [VMEM_SPEC] * 2
        + [row, fixed(16, WIDTH)],
        out_specs=(row,) + (VMEM_SPEC,) * 5,
        scratch_shapes=[
            pltpu.VMEM((CHIPS, 2, 240, LANES), BF16),
            pltpu.VMEM((CHIPS, 2, 192, LANES), BF16),
            pltpu.VMEM((1024, WIDTH), BF16),
            pltpu.VMEM((1024, WIDTH), BF16),
            pltpu.VMEM((2, 1024, WIDTH), BF16),
            pltpu.VMEM((WIDTH, WIDTH), BF16),
        ]
        + [pltpu.SemaphoreType.DMA] * 4,
        compiler_params=params(38),
        cost_estimate=cost(18_000_000_000, 50_000_000),
        name="mlp_backward",
    )(tab, later_tab, *up_pieces, *down_pieces, two, att, slope, out_grad, mid, vectors)


def attention_backward_tile(first_row, qkv_ref, probs_ref, grad_att_ref, grad_qkv_ref):
    low_half = lax.broadcasted_iota(jnp.int32, (128, 128), 1) < HEAD_DIM
    units = [(k, pair) for k in range(2) for pair in range(6)]

    def rows(k):
        return slice(128 * k, 128 * k + 128)

    def part(k, pair, section):
        base = pair_base(pair) + section * LANES
        return qkv_ref[rows(k), base : base + 128]

    def up(k, pair):
        whole = pl.ds(pl.multiple_of(first_row + 128 * k, 128), 128)
        return two_heads(grad_att_ref[whole, pair * 128 : pair * 128 + 128], low_half)

    def probs_of(k, pair):
        first = 256 * (6 * k + pair)
        return probs_ref[first : first + 256, :]

    def store(k, pair, section, value):
        base = pair_base(pair) + section * LANES
        grad_qkv_ref[rows(k), base : base + 128] = value.astype(BF16)

    grad_probs = [dot_last(up(k, pair), part(k, pair, 2)) for k, pair in units]
    grad_scores = []
    for (k, pair), grad in zip(units, grad_probs):
        probs = probs_of(k, pair).astype(F32)
        inner = jnp.sum(probs * grad, axis=-1, keepdims=True)
        grad_scores.append((probs * (grad - inner)).astype(BF16))
    for (k, pair), grad in zip(units, grad_scores):
        grad_query = dot(side_by_side(grad), two_heads(part(k, pair, 1), low_half))
        store(k, pair, 0, grad_query * HEAD_DIM ** (-0.5))
        grad_key = dot_first(grad, two_heads(part(k, pair, 0), low_half))
        store(k, pair, 1, grad_key * HEAD_DIM ** (-0.5))
        store(k, pair, 2, dot_first(probs_of(k, pair), up(k, pair)))


def qkv_grad_rows(tab, side, normed, grad_qkv, out_ref, part):
    part[...] = dot_first(normed, grad_qkv).astype(BF16)
    for sec in range(3):
        store_blocks(tab, side, out_ref, 48 * sec, part, slice(sec * LANES, (sec + 1) * LANES))


def attention_backward_kernel(
    tab, normed_hbm, qkv_ref, probs_ref, grad_att_ref, grad_qkv_ref, mine_ref, theirs_ref,
    normed, kept, part, sem,
):
    i = pl.program_id(0)

    @pl.when(i == 0)
    def _():
        pltpu.make_async_copy(normed_hbm, normed, sem).start()

    @pl.when(i < 4)
    def _():
        attention_backward_tile(i * 256, qkv_ref, probs_ref, grad_att_ref, grad_qkv_ref)
        for side, target in enumerate((mine_ref, kept)):
            lanes = pl.ds(pl.multiple_of(half_of(tab, side) * 3 * LANES, 128), 3 * LANES)
            target[rows_of(i, 256), :] = grad_qkv_ref[:, lanes]

    @pl.when(i == 4)
    def _():
        finish(normed, sem)
        qkv_grad_rows(tab, 1, normed[...], kept[...], theirs_ref, part)


def attention_backward(tab, normed, qkv, probs, grad_att):
    wide = clamped(256, 3 * WIDTH)
    return kernel_call(
        attention_backward_kernel,
        grid=(5,),
        out_shape=(
            shaped((1024, 3 * WIDTH)), local((1024, 3 * LANES)), local((CHIPS, 144, LANES))
        ),
        in_specs=[SMEM_SPEC, ANY_SPEC, wide, clamped(12 * 256, 128), VMEM_SPEC],
        out_specs=(wide, VMEM_SPEC, VMEM_SPEC),
        scratch_shapes=[
            pltpu.VMEM((1024, WIDTH), BF16),
            pltpu.VMEM((1024, 3 * LANES), BF16),
            pltpu.VMEM((WIDTH, 3 * LANES), BF16),
            pltpu.SemaphoreType.DMA,
        ],
        compiler_params=params(28),
        cost_estimate=cost(11_000_000_000, 22_000_000),
        name="attention_backward",
    )(tab, normed, qkv, probs, grad_att)


def qkv_grad_kernel(
    tab, later_tab, d_a, d_b, d_c, d_d, normed_ref, grad_qkv_ref, act_ref, mid_ref,
    out_ref, result_ref,
    part, w_down, sem,
):
    i = pl.program_id(0)

    @pl.when(i == 0)
    def _():
        fetch_pieces(later_tab, (d_a, d_b, d_c, d_d), 192, w_down, sem)
        qkv_grad_rows(tab, 0, normed_ref[...], grad_qkv_ref[...], out_ref, part)
        finish(w_down, sem)

    @pl.when(i > 0)
    def _():
        total = mid_ref[...]
        for j in range(4):
            total = total + dot(act_ref[j], down_rows(w_down, j))
        result_ref[...] = total.astype(BF16)


def qkv_grad(tab, later_tab, pieces, normed, grad_qkv, act, mid):
    row = pl.BlockSpec((256, WIDTH), lambda i: (jnp.maximum(i - 1, 0), 0))
    wide = pl.BlockSpec((4, 256, WIDTH), lambda i: (0, jnp.maximum(i - 1, 0), 0))
    return kernel_call(
        qkv_grad_kernel,
        grid=(5,),
        out_shape=(local((CHIPS, 144, LANES)), shaped((1024, WIDTH))),
        in_specs=[SMEM_SPEC] * 2 + [ANY_SPEC] * 4 + [fixed(1024, WIDTH), VMEM_SPEC, wide, row],
        out_specs=(VMEM_SPEC, row),
        scratch_shapes=[
            pltpu.VMEM((WIDTH, 3 * LANES), BF16),
            pltpu.VMEM((CHIPS, 2, 192, LANES), BF16),
            pltpu.SemaphoreType.DMA,
        ],
        compiler_params=params(26),
        cost_estimate=cost(7_000_000_000, 22_000_000),
        name="qkv_grad",
    )(tab, later_tab, *pieces, normed, grad_qkv, act, mid)


def input_backward_kernel(
    tab, g_a, g_b, g_c, g_d, grad_qkv_ref, x_ref, te_ref, vec_ref, grad_mid_ref, gain_two_ref,
    input_ref, small_ref,
    w, sem,
):
    i = pl.program_id(0)

    @pl.when(i == 0)
    def _():
        fetch_pieces(tab, (g_a, g_b, g_c, g_d), 144, w, sem)
        small_ref[8:9, :] = jnp.zeros((1, WIDTH), F32)
        small_ref[9:10, :] = gain_two_ref[...]
        small_ref[10:16, :] = jnp.zeros((6, WIDTH), F32)
        finish(w, sem)

    y = jnp.zeros((256, WIDTH), F32)
    for half in (0, 1):
        cols = slice(half * 3 * LANES, (half + 1) * 3 * LANES)
        y = y + dot_last(grad_qkv_ref[:, cols], qkv_columns(w, half))
    xhat, scale = ln_stats(add_embed(x_ref[...], te_ref, i))
    grad = grad_mid_ref[...] + ln_back(y, vec_ref[0:1, :], xhat, scale)
    input_ref[...] = grad.astype(BF16)
    for s in range(2):
        small_ref[pl.ds(i * 2 + s, 1), :] = jnp.sum(
            grad[128 * s : 128 * s + 128], axis=0, keepdims=True
        )
    small_ref[8:9, :] += jnp.sum(y * xhat, axis=0, keepdims=True)


def input_backward(tab, pieces, grad_qkv, rows, embed, vectors, grad_mid, gain_two):
    row = tiles(256, WIDTH)
    return kernel_call(
        input_backward_kernel,
        grid=(4,),
        out_shape=(shaped((1024, WIDTH)), local((16, WIDTH), F32)),
        in_specs=[SMEM_SPEC]
        + [ANY_SPEC] * 4
        + [tiles(256, 3 * WIDTH), row, fixed(8, WIDTH), fixed(16, WIDTH), row, VMEM_SPEC],
        out_specs=(row, VMEM_SPEC),
        scratch_shapes=[pltpu.VMEM((CHIPS, 2, 144, LANES), BF16), pltpu.SemaphoreType.DMA],
        compiler_params=params(20),
        cost_estimate=cost(4_000_000_000, 18_000_000),
        name="input_backward",
    )(tab, *pieces, grad_qkv, rows, embed, vectors, grad_mid, gain_two)


def finish_kernel(
    tab, e_mine, e_theirs, wave_ref, hot_ref, hidden_ref, slope_ref, time_out_ref,
    down_ref, down_other, up_ref, up_other, qkv_ref, qkv_other,
    tin_out, tout_out, one_out, two_out, data_out, down_out, up_out, out_out, qkv_out,
    every, sem,
):
    each_piece(
        tab,
        [e.at[pl.ds(first, 8)] for e in (e_mine, e_theirs) for first in (0, 8)],
        lambda src, chip, half: pltpu.make_async_copy(
            src, every.at[half * CHIPS + chip], sem
        ).start(),
    )
    core = first_core(tab)
    for half, down, up, qkv in (
        (core, down_ref, up_ref, qkv_ref), (1 - core, down_other, up_other, qkv_other)
    ):
        down_out[:, lanes_of(half, LANES)] = down[pl.ds(pl.multiple_of(96 * core, 8), 96), :]
        for b in range(4):
            up_out[:, lanes_of(half, 4 * LANES, b * LANES)] = up[pl.ds(pl.multiple_of(48 * b + 24 * core, 8), 24), :]
        out_out[:, lanes_of(half, LANES)] = up[pl.ds(pl.multiple_of(192 + 24 * core, 8), 24), :]
        for sec in range(3):
            qkv_out[:, lanes_of(half, LANES, sec * WIDTH)] = qkv[pl.ds(pl.multiple_of(48 * sec + 24 * core, 8), 24), :]
    finish(every, sem)
    grads = every[...].reshape(-1, WIDTH)
    tout_out[...] = dot_first(hidden_ref[...], grads)
    grad_pre = dot_last(grads, time_out_ref[...]) * slope_ref[...]
    tin_out[...] = dot_first(grad_pre.astype(BF16), wave_ref[...])
    first = tab[68] * 24
    lane = lax.broadcasted_iota(jnp.int32, (WIDTH, 128), 0)
    place = lax.broadcasted_iota(jnp.int32, (WIDTH, 128), 1)
    own = dot(grads, ((lane == place + first) & (place < 24)).astype(BF16)).astype(BF16)
    sums = dot(hot_ref[...], own)
    data_out[...] = sums[0:2, 0:24]
    one_out[...] = sums[2:3, 0:24]
    two_out[...] = sums[3:4, 0:24]


def finish_grads(tab, parts, wave, hot, hidden, slope, time_out, pieces):
    rows, width = time_out.shape
    return kernel_call(
        finish_kernel,
        out_shape=(
            shaped((rows, wave.shape[1]), F32),
            shaped((rows, width), F32),
            shaped((1, 24), F32),
            shaped((1, 24), F32),
            shaped((2, 24), F32),
            shaped((96, WIDTH), F32),
            shaped((24, FF), F32),
            shaped((24, WIDTH), F32),
            shaped((24, 3 * WIDTH), F32),
        ),
        in_specs=[SMEM_SPEC] + [ANY_SPEC] * 2 + [VMEM_SPEC] * 11,
        out_specs=(VMEM_SPEC,) * 9,
        scratch_shapes=[pltpu.VMEM((2 * CHIPS, 16, width), BF16), pltpu.SemaphoreType.DMA],
        compiler_params=params(16),
        cost_estimate=cost(50_000_000, 4_000_000),
        name="finish_grads",
    )(tab, *parts, wave, hot, hidden, slope, time_out, *pieces)


def pick(stacked, index):
    return lax.dynamic_index_in_dim(stacked, index, 0, keepdims=False)


def in_core_order(core, own, other, axis):
    return jnp.where(
        core == 0,
        jnp.concatenate([own, other], axis=axis),
        jnp.concatenate([other, own], axis=axis),
    )


def position_table(chip, core, order):
    index = jnp.arange(72, dtype=jnp.int32)
    side = jnp.bitwise_xor(core, (index // CHIPS) % 2)
    inner = index % CHIPS
    distance = jnp.bitwise_xor(inner, chip)
    there = jnp.zeros_like(index)
    back = jnp.zeros_like(index)
    for bit in range(4):
        mask = jnp.where(side == 0, order[0][bit], order[1][bit])
        there = there + jnp.where((inner >> bit) & 1 == 1, mask, 0)
        back = back + jnp.where(jnp.bitwise_and(distance, mask) != 0, 1 << bit, 0)
    moved = jnp.where(index < 32, jnp.bitwise_xor(there, chip), back)
    return jnp.where(index < 64, moved, jnp.where(index < 68, core, 2 * chip + core))


def lane_blocks(x, starts, step):
    return [
        jnp.concatenate([x[:, k + h * step : k + h * step + LANES] for k in starts], axis=0)
        for h in (0, 1)
    ]


def swap_halves(halves, core):
    own = jnp.where(core == 0, halves[0], halves[1])
    return own, core_swap(jnp.where(core == 0, halves[1], halves[0]))


def join_rows(own, other, core, blocks):
    shape = (blocks, own.shape[0] // blocks, LANES)
    return in_core_order(core, own.reshape(shape), other.reshape(shape), 1).reshape(-1, LANES)


def pack_extra(time_in, vectors, ints):
    rows = time_in.shape[0]
    filler = jnp.zeros((rows, 128), BF16)
    vec = lax.dynamic_update_slice(filler, vectors, (0, 0))
    num = lax.dynamic_update_slice(filler, ints[None, :], (0, 0))
    return jnp.concatenate([time_in, vec, num], axis=1)


def split_time(timestep, dataset):
    steps = timestep.reshape(-1)
    return jnp.concatenate([steps // 64, steps % 64, dataset.reshape(-1)]).astype(BF16)


def gather_all(x):
    return lax.all_gather(x, AXES, axis=0, tiled=True)


def shards(
    block_input,
    out_grad,
    timestep,
    dataset,
    lengths,
    norm1_gain,
    qkv_weight,
    out_weight,
    norm2_gain,
    up_weight,
    down_weight,
    time_in,
    time_out,
    data_embed,
    devices,
):
    flat = lax.axis_index(AXES)
    exchange = devices == 2 * CHIPS
    vectors = jnp.concatenate([norm1_gain[None], norm2_gain[None], data_embed.T], axis=0)
    numbers = split_time(timestep, dataset)
    count = numbers.shape[0] // 3
    micros, seqs, seq_len, width = block_input.shape
    tokens = micros * seqs * seq_len
    x_rows = block_input.reshape(tokens, width)
    grad_rows = out_grad.reshape(tokens, width)
    features = sinusoid(timestep.reshape(-1), time_in.shape[1] // 2).astype(BF16)
    if exchange:
        core = flat & 1
        chip = flat >> 1

        wide = lane_blocks(qkv_weight, (0, WIDTH, 2 * WIDTH), LANES)
        slim = lane_blocks(time_out, (0,), LANES)
        own, other = swap_halves(
            [jnp.concatenate([x, y], axis=0) for x, y in zip(wide, slim)], core
        )
        attention_piece = jnp.concatenate(
            [
                join_rows(own[:72], other[:72], core, 3),
                join_rows(own[72:], other[72:], core, 1),
                pack_extra(time_in, vectors, numbers),
            ],
            axis=0,
        )[None]
        near = [chip_swap(attention_piece, p) for p in (1, 2, 3)]
        up_weight, out_weight, down_weight, flat = lax.optimization_barrier(
            (up_weight, out_weight, down_weight, flat, attention_piece)
        )[:4]
        tab = position_table(flat >> 1, flat & 1, LINE_FIRST)
        later_tab = position_table(flat >> 1, flat & 1, LINE_LATER)
        wide = lane_blocks(up_weight, range(0, 4 * LANES, LANES), 4 * LANES)
        slim = lane_blocks(out_weight, (0,), LANES)
        own, other = swap_halves(
            [jnp.concatenate([x, y], axis=0) for x, y in zip(wide, slim)], core
        )
        up_piece = jnp.concatenate(
            [join_rows(own[:96], other[:96], core, 4), join_rows(own[96:], other[96:], core, 1)],
            axis=0,
        )[None]
        own, other = swap_halves(lane_blocks(down_weight, (0,), LANES), core)
        down_piece = join_rows(own, other, core, 1)[None]
        down_pair = jnp.concatenate([down_piece, chip_swap(down_piece, 1, LINE_LATER)], axis=0)
        ready = (up_piece, down_pair, tab, later_tab, features)
        line = after(jnp.concatenate([attention_piece] + near, axis=0), *ready)
        plane = chip_swap(line, 4)
        up_near = [chip_swap(after(up_piece, line), p) for p in (1, 2)]
        plane, up_near = together(plane, up_near)
        held = jnp.concatenate([line, plane], axis=0)
        far = chip_swap(held, 8)
        up_near.append(chip_swap(after(up_piece, plane), 3))
        up_line = lax.optimization_barrier(jnp.concatenate([up_piece] + up_near, axis=0))
        up_plane = chip_swap(up_line, 4)
        down_near = [chip_swap(after(down_pair, up_line), p, LINE_LATER) for p in (2, 4)]
        (far, up_plane), down_near = together((far, up_plane), down_near)
        attention_pieces = (held, far, core_swap(held), core_swap(far))
        up_held = jnp.concatenate([up_line, up_plane], axis=0)
        up_far = chip_swap(up_held, 8)
        down_last = chip_swap(after(down_pair, up_held), 6, LINE_LATER)
    else:
        tab = jnp.concatenate(
            [jnp.tile(jnp.arange(CHIPS, dtype=jnp.int32), 4), jnp.zeros((8,), jnp.int32)]
        )
        later_tab = tab
        full_qkv = gather_all(qkv_weight).reshape(CHIPS, 48, 3, 2, LANES)
        full_out = gather_all(out_weight).reshape(CHIPS, 48, 2, LANES)
        full_up = gather_all(up_weight).reshape(CHIPS, 48, 2, 4, LANES)
        full_down = gather_all(down_weight).reshape(CHIPS, 192, 2, LANES)
        full_tin = gather_all(time_in).reshape(CHIPS, 2, 16, 128)
        full_tout = gather_all(time_out).reshape(CHIPS, 32, 2, LANES)
        full_vec = lax.all_gather(vectors, AXES, axis=1, tiled=True).reshape(4, CHIPS, 2, 24)
        numbers_all = gather_all(numbers[None])
        extra = jnp.zeros((CHIPS, 2, 16, LANES), BF16)
        extra = extra.at[:, :, :, :128].set(full_tin)
        extra = extra.at[:, :, 0:4, 128:152].set(full_vec.transpose(1, 2, 0, 3))
        attention_pieces = []
        down_pieces = []
        up_pieces = []
        for half in (0, 1):
            wide = full_qkv[:, :, :, half].transpose(0, 2, 1, 3).reshape(CHIPS, 144, LANES)
            whole = jnp.concatenate([wide, full_tout[:, :, half], extra[:, half]], axis=1)
            attention_pieces += [whole[:8], whole[8:]]
            down_pieces += [full_down[:8, :, half], full_down[8:, :, half]]
            wide = full_up[:, :, half].transpose(0, 2, 1, 3).reshape(CHIPS, 192, LANES)
            whole = jnp.concatenate([wide, full_out[:, :, half]], axis=1)
            up_pieces += [whole[:8], whole[8:]]

    arrivals = []
    if exchange:
        x_rows = after(x_rows, up_held)
        arrivals = [up_far]
    forward = attention_forward(tab, lengths, dataset, attention_pieces, x_rows, features)
    (normed, qkv, embed, vecs, seen, probs, att), arrivals = together(forward, arrivals)
    seen = seen[:, :, 0, : 3 * count].reshape(2 * CHIPS, 3 * count) if exchange else numbers_all
    steps = seen[:, :count] * 64 + seen[:, count : 2 * count].astype(F32)
    wave = sinusoid(steps.reshape(-1), time_in.shape[1] // 2).astype(BF16)
    wave = jnp.pad(wave.reshape(devices, count, -1), ((0, 0), (0, 16 - count), (0, 0)))
    wave = wave.reshape(devices * 16, -1)
    which = jnp.pad(seen[:, 2 * count :], ((0, 0), (0, 16 - count))).reshape(-1)
    place = jnp.tile(jnp.arange(16), devices)
    hot = jnp.stack(
        [(place < count) & (which == 0), (place < count) & (which == 1), place == 8, place == 9]
    )
    hot = jnp.pad(hot.astype(BF16), ((0, 12), (0, 0)))
    pre = dot_last(wave, time_in)
    gate = 1.0 / (1.0 + jnp.exp(-pre))
    hidden = (pre * gate).astype(BF16)
    slope_pre = gate * (1.0 + pre * (1.0 - gate))
    if exchange:
        (up_far,) = arrivals
        down_near = [after(x, embed) for x in [down_pair] + down_near + [down_last]]
        up_pieces = (up_held, up_far, core_swap(up_held), core_swap(up_far))
        down_held = jnp.concatenate(down_near, axis=0)
        att, wave, hot, hidden, slope_pre, down_held = lax.optimization_barrier(
            (att, wave, hot, hidden, slope_pre, down_held)
        )
        arrivals = chip_swap(down_held, 8, LINE_LATER)
    forward = up_forward(tab, up_pieces, att, x_rows, grad_rows, embed, vecs)
    (mid, two, act, slope, down_theirs), arrivals = together(forward, arrivals)
    if exchange:
        down_far = arrivals
        down_sum = Scatter(down_theirs)
        arrivals = [core_swap(down_held), core_swap(down_far)], down_sum.swap()
    (down_mine, act, slope), arrivals = together(down_grad(tab, act, grad_rows, slope), arrivals)
    if exchange:
        down_pieces = (down_held, down_far, *arrivals[0])
        down_sum.land(arrivals[1], down_mine)
        slope = after(slope, *down_sum.send())
        arrivals = down_sum.fly()
    backward = mlp_backward(
        tab, later_tab, up_pieces, down_pieces, two, att, slope, grad_rows, mid, vecs
    )
    backward, arrivals = together(backward, arrivals)
    grad_mid, branch, grad_up, grad_att, gain_two, up_theirs = backward
    if exchange:
        down_sum.land(arrivals)
        up_sum = Scatter(up_theirs)
        grad_up = after(grad_up, *down_sum.send())
        arrivals = down_sum.fly(), up_sum.swap()
    up_mine, arrivals = together(up_grad(tab, att, branch, two, grad_up), arrivals)
    if exchange:
        down_sum.land(arrivals[0])
        up_sum.land(arrivals[1], up_mine)
        grad_att = after(grad_att, *up_sum.send(), *down_sum.send())
        arrivals = up_sum.fly(), down_sum.fly()
    backward = attention_backward(tab, normed, qkv, probs, grad_att)
    (grad_qkv, mine_qkv, att_theirs), arrivals = together(backward, arrivals)
    if exchange:
        up_sum.land(arrivals[0])
        down_sum.land(arrivals[1])
        down_total = down_sum.total()
        att_sum = Scatter(att_theirs)
        mine_qkv = after(mine_qkv, *up_sum.send(), down_total)
        arrivals = up_sum.fly(), att_sum.swap()
    backward = qkv_grad(tab, later_tab, down_pieces, normed, mine_qkv, act, mid)
    (att_mine, result), arrivals = together(backward, arrivals)
    if exchange:
        up_sum.land(arrivals[0])
        att_sum.land(arrivals[1], att_mine)
        grad_qkv = after(grad_qkv, *att_sum.send(), *up_sum.send())
        *up_near, up_last = up_sum.fly()
        arrivals = att_sum.fly(), up_near
    backward = input_backward(
        tab, attention_pieces, grad_qkv, x_rows, embed, vecs, grad_mid, gain_two
    )
    (grad_input, small), arrivals = together(backward, arrivals)

    small = small.astype(BF16)[None]
    if exchange:
        att_sum.land(arrivals[0])
        up_sum.land(arrivals[1])
        att_sum.send()
        near = [chip_swap(small, p) for p in (1, 2, 3)]
        att_sum.land(att_sum.fly())
        small_line = jnp.concatenate([small] + near, axis=0)
        att_sum.send()
        brought = att_sum.fly()
        small_line, brought[1] = lax.optimization_barrier((small_line, brought[1]))
        plane = [small_line] + [chip_swap(small_line, p) for p in (4, 8, 12)]
        every = jnp.concatenate(plane, axis=0)
        every = every, core_swap(every)
        att_sum.land(brought)
        up_sum.land([after(up_last, small_line)])
        sums = after(down_total, small_line), after(up_sum.total(), small_line), att_sum.total()
        pieces = [x for total in sums for x in (total, core_swap(total))]
        finished = finish_grads(
            tab, every, wave, hot, hidden, slope_pre, time_out, pieces
        )
        grad_tin, grad_tout, gain_one, gain_two, grad_data, *weights = finished
        grad_down, grad_up_weight, grad_out, grad_qkv_weight = weights
    else:
        every = gather_all(small).reshape(devices * 16, width)
        grad_tout = dot_first(hidden, every)
        grad_pre = dot_last(every, time_out) * slope_pre
        grad_tin = dot_first(grad_pre.astype(BF16), wave)
        own_cols = norm1_gain.shape[0]
        sums = lax.dynamic_slice_in_dim(dot(hot, every), flat * own_cols, own_cols, 1)
        grad_data, gain_one, gain_two = sums[0:2], sums[2], sums[3]
        scatter = partial(lax.psum_scatter, axis_name=AXES, scatter_dimension=0, tiled=True)
        both = jnp.stack([down_mine, down_theirs]).astype(F32)
        grad_down = scatter(both.transpose(1, 2, 0, 3).reshape(FF, WIDTH))
        both = jnp.stack([up_mine, up_theirs]).astype(F32)
        grad_out = scatter(both[:, :, 192:].transpose(1, 2, 0, 3).reshape(WIDTH, WIDTH))
        both = both[:, :, :192].reshape(2, CHIPS, 4, 48, LANES)
        grad_up_weight = scatter(both.transpose(1, 3, 0, 2, 4).reshape(WIDTH, FF))
        both = jnp.stack([att_mine, att_theirs]).astype(F32).reshape(2, CHIPS, 3, 48, LANES)
        grad_qkv_weight = scatter(both.transpose(1, 3, 2, 0, 4).reshape(WIDTH, 3 * WIDTH))

    return (
        result.reshape(block_input.shape),
        grad_input.reshape(block_input.shape),
        gain_one.reshape(-1),
        grad_qkv_weight,
        grad_out,
        gain_two.reshape(-1),
        grad_up_weight,
        grad_down,
        grad_tin,
        grad_tout,
        grad_data.T,
    )


def solution(mesh):
    devices = mesh.shape["dp"] * mesh.shape["fsdp"]
    seq_spec = P(None, AXES, None, None)
    int_spec = P(None, AXES)
    row_spec = P(AXES, None)
    in_specs = (seq_spec, seq_spec, int_spec, int_spec, int_spec, P(AXES), row_spec, row_spec, P(AXES))
    in_specs = in_specs + (row_spec,) * 5
    out_specs = (seq_spec, seq_spec, P(AXES), row_spec, row_spec, P(AXES)) + (row_spec,) * 5
    return jax.shard_map(
        partial(shards, devices=devices),
        mesh=mesh,
        in_specs=in_specs,
        out_specs=out_specs,
        check_vma=False,
    )
```
